512 devices in a mesh: gx: 4 (over y), gy: 16 (over z), gz: 8 (over x, core).
Axes of the slice: x: 4, y: 4, z: 16, core: 2. Of those that a mesh axis runs over, the one named last changes fastest.
Arguments:
- state: float32 [3, 128, 640, 512], P(None, 'gz', 'gy', 'gx'), may hold values from -6 to 6
- right_side: float32 [3, 128, 640, 512], P(None, 'gz', 'gy', 'gx'), may hold values from -6 to 6
- permeability: bfloat16 [128, 640, 512], P('gz', 'gy', 'gx'), may hold values from 0.099609375 to 10
- pore_volume: bfloat16 [128, 640, 512], P('gz', 'gy', 'gx'), may hold values from 0.019897461 to 0.19921875
- facies: int32 [128], P('gz'), may hold values from 0 to 3
- storage_table: float32 [4, 3, 3], replicated, may hold values from -0.3 to 2, as said below
- coupling_table: float32 [4, 3, 3], replicated, may hold values from -0.3 to 2, as said below
Outputs:
- new_state: float32 [3, 128, 640, 512], P(None, 'gz', 'gy', 'gx')
- correction: float32 [640, 512], P('gy', 'gx')
The draws below stay inside these ranges and needn't reach their ends.
Inputs may be any that keep to these rules, and one draw needn't show every extreme that they name: `storage_table`: each facies block has a diagonal of 1 to 2 and off-diagonal entries of magnitude at most 0.3. `coupling_table`: each facies block has a diagonal of 1 to 2 and off-diagonal entries of magnitude at most 0.3.
All inputs are finite; a program needn't handle non-finite values.
Results may differ from the reference program's by a relative error of at most 0.0003.
Values sent between devices are 32-bit elements; how exact they have to be, the bound alone decides.
No kernel may reach another device: no remote copies, remote signals or barrier semaphores. Data moves between devices by JAX's collectives and lax.ppermute only.
A program may use at most 64 MiB of HBM per device.

```python
import math
import jax
import jax.numpy as jnp
from jax import lax

FACIES = 4
SWEEPS = 8
NX = 512
NY = 640
NZ = 128


def draw_table(key):
    first_key, second_key = jax.random.split(key)
    diagonal = jax.random.uniform(first_key, (FACIES, 3), jnp.float32, 1.0, 2.0)
    spread = jax.random.uniform(second_key, (FACIES, 3, 3), jnp.float32, -0.3, 0.3)
    identity = jnp.eye(3, dtype=jnp.float32)
    return spread * (1.0 - identity) + diagonal[:, :, None] * identity


def draw_storage_table(key, part):
    return draw_table(jax.random.fold_in(key, 11))


def draw_coupling_table(key, part):
    return draw_table(jax.random.fold_in(key, 12))


def plant(result, rng, least, top_value):
    longest = result.shape.index(max(result.shape))
    spots = []
    for shift in (0, 1):
        where = [jax.random.randint(jax.random.fold_in(rng, axis), (), 0, length) for axis, length in enumerate(result.shape)]
        where[longest] = (where[longest] + shift) % result.shape[longest]
        spots.append(tuple(where))
    return result.at[spots[0]].set(least).at[spots[1]].set(top_value)


def steps_of(rng, dims, cuts, low, largest):
    factor_of, own = 1.0, jax.random.fold_in(rng, 6)
    for dim, parts in cuts:
        heights = jnp.exp(jax.random.uniform(jax.random.fold_in(own, dim), (parts,), jnp.float32, low / len(cuts), largest / len(cuts)))
        factor_of = factor_of * jnp.repeat(heights, dims[dim] // parts).reshape([-1 if axis == dim else 1 for axis in range(len(dims))])
    return factor_of


def gaussian(rng, extent, width, limit, shards=(), held_as=jnp.bfloat16):
    gain = steps_of(rng, extent, shards, -0.22, 0.18) if shards else 1.0
    result = jax.random.normal(rng, extent, jnp.float32) * width * gain
    return jnp.minimum(jnp.maximum(result, -limit), limit).astype(held_as)


def setup_inputs(seed: int = 0) -> dict:
    arg_keys = jax.random.split(jax.random.key(seed), 8)
    state = gaussian(arg_keys[0], (3, NZ, NY, NX), 1.0, 6.0, ((1, 8), (2, 16), (3, 4)), jnp.float32)
    right_side = gaussian(arg_keys[1], (3, NZ, NY, NX), 1.0, 6.0, ((1, 8), (2, 16), (3, 4)), jnp.float32)
    permeability = jnp.clip(jnp.exp(math.log(10.0) - 4.609084 * jax.random.uniform(arg_keys[2], (NZ, NY, NX), jnp.float32) ** steps_of(arg_keys[2], (NZ, NY, NX), ((0, 8), (1, 16), (2, 4)), -0.2, 0.2)), 0.099609375, 10.0).astype(jnp.bfloat16)
    pore_volume = jnp.clip(jnp.exp(math.log(0.19921875) - 2.3038113 * jax.random.uniform(arg_keys[3], (NZ, NY, NX), jnp.float32) ** steps_of(arg_keys[3], (NZ, NY, NX), ((0, 8), (1, 16), (2, 4)), -0.2, 0.2)), 0.019897461, 0.19921875).astype(jnp.bfloat16)
    facies = plant(jax.random.randint(arg_keys[4], (NZ,), 0, FACIES), jax.random.fold_in(arg_keys[4], 1), 0, FACIES - 1).astype(jnp.int32)
    storage_table = draw_storage_table(jax.random.fold_in(arg_keys[7], 71), 0)
    coupling_table = draw_coupling_table(jax.random.fold_in(arg_keys[7], 71), 0)
    return dict(state=state, right_side=right_side, permeability=permeability, pore_volume=pore_volume, facies=facies, storage_table=storage_table, coupling_table=coupling_table)


relax = 0.8


def layer_tables(facies, table):
    onehot = (facies[:, None] == jnp.arange(table.shape[0])[None, :]).astype(jnp.float32)
    return jnp.dot(onehot, table.reshape(table.shape[0], 9), precision=lax.Precision.HIGHEST)


def layer_coefficient(rows, row_index, column_index):
    return rows[:, 3 * row_index + column_index][:, None, None]


def neighbours(padded):
    return [padded[..., 2:, 1:-1, 1:-1], padded[..., :-2, 1:-1, 1:-1],
            padded[..., 1:-1, 2:, 1:-1], padded[..., 1:-1, :-2, 1:-1],
            padded[..., 1:-1, 1:-1, 2:], padded[..., 1:-1, 1:-1, :-2]]


def face_weights(padded_perm):
    center = padded_perm[1:-1, 1:-1, 1:-1]
    return [2.0 * center * nearby / (center + nearby) for nearby in neighbours(padded_perm)]


def apply_operator(padded_state, weights, storage, storage_rows, coupling_rows):
    center = padded_state[:, 1:-1, 1:-1, 1:-1]
    fluxes = jnp.zeros_like(center)
    for weight, nearby in zip(weights, neighbours(padded_state)):
        fluxes = fluxes + weight[None] * (center - nearby)
    outputs = []
    for row_index in range(3):
        local = sum(layer_coefficient(storage_rows, row_index, k) * center[k] for k in range(3))
        moved = sum(layer_coefficient(coupling_rows, row_index, k) * fluxes[k] for k in range(3))
        outputs.append(storage * local + moved)
    return jnp.stack(outputs)


def coarse_planes(residual, weights, storage, storage_rows, coupling_rows):
    first_coupling = layer_coefficient(coupling_rows, 0, 0)
    first_storage = layer_coefficient(storage_rows, 0, 0)
    items = [residual[0], storage * first_storage] + [weights[k] * first_coupling for k in range(2, 6)]
    return jnp.stack([jnp.sum(item, axis=0) for item in items])


def jacobi(field, bordered, planes):
    diagonal = planes[1] + planes[2] + planes[3] + planes[4] + planes[5]
    nearby = (planes[2] * bordered[2:, 1:-1] + planes[3] * bordered[:-2, 1:-1]
              + planes[4] * bordered[1:-1, 2:] + planes[5] * bordered[1:-1, :-2])
    return field + relax * (planes[0] - diagonal * field + nearby) / diagonal


def block_solve(weights, storage, storage_rows, coupling_rows, residual):
    face_total = weights[0] + weights[1] + weights[2] + weights[3] + weights[4] + weights[5]
    entries = [[storage * layer_coefficient(storage_rows, r, c) + face_total * layer_coefficient(coupling_rows, r, c)
                for c in range(3)] for r in range(3)]

    def cofactor(r, c):
        return (entries[(r + 1) % 3][(c + 1) % 3] * entries[(r + 2) % 3][(c + 2) % 3]
                - entries[(r + 1) % 3][(c + 2) % 3] * entries[(r + 2) % 3][(c + 1) % 3])

    factors = [[cofactor(r, c) for c in range(3)] for r in range(3)]
    determinant = entries[0][0] * factors[0][0] + entries[0][1] * factors[0][1] + entries[0][2] * factors[0][2]
    return jnp.stack([(factors[0][r] * residual[0] + factors[1][r] * residual[1] + factors[2][r] * residual[2]) / determinant
                      for r in range(3)])


def reference(state, right_side, permeability, pore_volume, facies, storage_table, coupling_table):
    perm_wide = permeability.astype(jnp.float32)
    storage = pore_volume.astype(jnp.float32)
    storage_rows = layer_tables(facies, storage_table)
    coupling_rows = layer_tables(facies, coupling_table)
    weights = face_weights(jnp.pad(perm_wide, 1))
    widths = ((0, 0), (1, 1), (1, 1), (1, 1))
    residual = right_side - apply_operator(jnp.pad(state, widths), weights, storage, storage_rows, coupling_rows)
    planes = coarse_planes(residual, weights, storage, storage_rows, coupling_rows)
    correction = jnp.zeros(planes.shape[1:], jnp.float32)
    for repeat_index in range(SWEEPS):
        correction = jacobi(correction, jnp.pad(correction, 1), planes)
    state_one = state.at[0].add(correction[None])
    later_residual = right_side - apply_operator(jnp.pad(state_one, widths), weights, storage, storage_rows, coupling_rows)
    new_state = state_one + block_solve(weights, storage, storage_rows, coupling_rows, later_residual)
    return new_state, correction
```

```python
import jax
import jax.numpy as jnp
from jax import lax
from jax.experimental import pallas as pl
from jax.experimental.pallas import tpu as pltpu
from jax.sharding import PartitionSpec as P

SWEEPS = 8
RELAX = 0.8
DIRECTIONS = ((-1, 0), (1, 0), (0, -1), (0, 1), (-1, -1), (1, 1), (-1, 1), (1, -1))
F32 = jnp.float32
PARAMS = pltpu.CompilerParams(vmem_limit_bytes=24 * 2**20)


def vmem(count):
    return [pl.BlockSpec(memory_space=pltpu.VMEM)] * count


def smem(count):
    return [pl.BlockSpec(memory_space=pltpu.SMEM)] * count


def lane_index(shape):
    return lax.broadcasted_iota(jnp.int32, shape, len(shape) - 1)


def row_index(shape):
    return lax.broadcasted_iota(jnp.int32, shape, len(shape) - 2)


def faces_kernel(state, perm, zlo, zhi, ylo, yhi, xlo, xhi):
    depth, height, width = perm.shape
    tiles = height // 8
    lanes = lane_index((8, 128))

    def layer(z, columns):
        columns = list(columns)
        for c in range(4):
            cells = state[c, z] if c < 3 else perm[z].astype(F32)
            ylo[c, pl.ds(z, 1), :] = cells[0:1]
            yhi[c, pl.ds(z, 1), :] = cells[height - 1 : height]
            for t in range(tiles):
                here = lanes == z * tiles + t
                block = cells[8 * t : 8 * t + 8]
                first = jnp.broadcast_to(block[:, 0:1], (8, 128))
                last = jnp.broadcast_to(block[:, width - 1 : width], (8, 128))
                columns[c] = jnp.where(here, first, columns[c])
                columns[4 + c] = jnp.where(here, last, columns[4 + c])
        return tuple(columns)

    columns = lax.fori_loop(0, depth, layer, (jnp.zeros((8, 128), F32),) * 8)
    for c in range(4):
        xlo[c] = columns[c]
        xhi[c] = columns[4 + c]
        zlo[c] = state[c, 0] if c < 3 else perm[0].astype(F32)
        zhi[c] = state[c, depth - 1] if c < 3 else perm[depth - 1].astype(F32)


def inverse(value):
    return 1.0 / value


def mean_weight(a, b):
    return 2.0 * a * b * inverse(a + b)


def cells_kernel(
    facies, storage_table, coupling_table,
    state, right, perm, pore, zlo, zhi, ylo, yhi, xlo, xhi,
    base, gain, face, message,
    sums,
):
    depth, height, width = perm.shape
    tiles = height // 8
    rows = row_index((height, width))
    lanes = lane_index((height, width))
    sums[...] = jnp.zeros_like(sums)

    def layer(z, carry):
        fid = facies[z]
        m = [[storage_table[fid, 3 * i + j] for j in range(3)] for i in range(3)]
        k = [[coupling_table[fid, 3 * i + j] for j in range(3)] for i in range(3)]
        below = jnp.minimum(z + 1, depth - 1)
        above = jnp.maximum(z - 1, 0)
        shift = lax.rem(128 - tiles * z, 128)

        def values(c):
            if c < 3:
                here, down, up = state[c, z], state[c, below], state[c, above]
            else:
                here, down, up = (perm[i].astype(F32) for i in (z, below, above))
            down = jnp.where(z == depth - 1, zhi[c], down)
            up = jnp.where(z == 0, zlo[c], up)
            south = pltpu.roll(here, height - 1, 0)
            south = jnp.where(rows == height - 1, yhi[c, pl.ds(z, 1), :], south)
            north = pltpu.roll(here, 1, 0)
            north = jnp.where(rows == 0, ylo[c, pl.ds(z, 1), :], north)

            def column(ref):
                turned = pltpu.roll(ref[c], shift, 1)
                return jnp.concatenate(
                    [jnp.broadcast_to(turned[:, t : t + 1], (8, width)) for t in range(tiles)], axis=0
                )

            east = jnp.where(lanes == width - 1, column(xhi), pltpu.roll(here, width - 1, 1))
            west = jnp.where(lanes == 0, column(xlo), pltpu.roll(here, 1, 1))
            return here, (down, up, south, north, east, west)

        q, near = values(3)
        weights = [mean_weight(q, n) for n in near]
        total = weights[0] + weights[1] + weights[2] + weights[3] + weights[4] + weights[5]
        cells, flux = [], []
        for c in range(3):
            u, near = values(c)
            moved = weights[0] * (u - near[0])
            for w, n in zip(weights[1:], near[1:]):
                moved = moved + w * (u - n)
            cells.append(u)
            flux.append(moved)
        v = pore[z].astype(F32)
        residual = [
            right[i, z]
            - v * (m[i][0] * cells[0] + m[i][1] * cells[1] + m[i][2] * cells[2])
            - (k[i][0] * flux[0] + k[i][1] * flux[1] + k[i][2] * flux[2])
            for i in range(3)
        ]
        entries = [[v * m[i][j] + total * k[i][j] for j in range(3)] for i in range(3)]

        def cofactor(r, c):
            r1, r2, c1, c2 = (r + 1) % 3, (r + 2) % 3, (c + 1) % 3, (c + 2) % 3
            return entries[r1][c1] * entries[r2][c2] - entries[r1][c2] * entries[r2][c1]

        factors = [[cofactor(r, c) for c in range(3)] for r in range(3)]
        determinant = (
            entries[0][0] * factors[0][0] + entries[0][1] * factors[0][1] + entries[0][2] * factors[0][2]
        )
        scale = inverse(determinant)
        for i in range(3):
            base[i, z] = cells[i] + scale * (
                factors[0][i] * residual[0] + factors[1][i] * residual[1] + factors[2][i] * residual[2]
            )
            gain[i, z] = scale * (factors[0][i] * k[0][0] + factors[1][i] * k[1][0] + factors[2][i] * k[2][0])
        face[0, z] = weights[0] + weights[1]
        for d in range(2, 6):
            face[d - 1, z] = weights[d]
        areal = weights[2] + weights[3] + weights[4] + weights[5]
        sums[0] += residual[0]
        sums[1] += v * m[0][0] + areal * k[0][0]
        sums[2] += weights[2] * k[0][0]
        sums[3] += weights[4] * k[0][0]
        return carry

    lax.fori_loop(0, depth, layer, 0)

    lane = lane_index((8, 128))
    last = tiles - 1

    def tile(p, t):
        return sums[p, 8 * t : 8 * t + 8, :]

    for p in range(4):
        message[0, 8 * p : 8 * p + 8, :] = tile(p, 0)
        message[1, 8 * p : 8 * p + 8, :] = tile(p, last)
        left = jnp.zeros((8, 128), F32)
        right_side = jnp.zeros((8, 128), F32)
        for t in range(tiles):
            here = (lane >= 8 * t) & (lane < 8 * t + 8)
            left = jnp.where(here, pltpu.roll(tile(p, t), 8 * t, 1) if t else tile(p, t), left)
            right_side = jnp.where(here, pltpu.roll(tile(p, t), 8 * t + 8, 1), right_side)
        message[2, 8 * p : 8 * p + 8, :] = left
        message[3, 8 * p : 8 * p + 8, :] = right_side
    for k, (t, at_end) in enumerate(((0, 0), (last, 1), (0, 1), (last, 0))):
        corner = jnp.zeros((8, 128), F32)
        for p in range(4):
            here = (lane >= 8 * p) & (lane < 8 * p + 8)
            turn = (8 * p + 8 * at_end) % 128
            corner = jnp.where(here, pltpu.roll(tile(p, t), turn, 1) if turn else tile(p, t), corner)
        message[4 + k, 0:8, :] = corner
        for t in range(4):
            message[4 + k, 8 + 8 * t : 16 + 8 * t, :] = tile(k, t)
        message[k, 32:40, :] = tile(k, last)


def sum_kernel(parts, total):
    result = parts[0]
    for i in range(1, parts.shape[0]):
        result = result + parts[i]
    total[...] = result


def sweep_kernel(shares, base, gain, face, new_state, correction):
    depth, height, width = base.shape[1:]
    tiles = height // 8
    lane = lane_index((8, 128))

    def tile(k, t):
        return shares[k, 8 * t : 8 * t + 8, :]

    def side(right, right_at, left, left_at):
        turn_right, turn_left = (128 - right_at) % 128, (width - 8 - left_at) % 128
        right = pltpu.roll(right, turn_right, 1) if turn_right else right
        left = pltpu.roll(left, turn_left, 1) if turn_left else left
        return jnp.where(lane < 8, right, jnp.where(lane >= width - 8, left, 0.0))

    planes = []
    for p in range(4):
        main = [tile(1, p)] + [tile(4 + p, 1 + t) for t in range(tiles - 1)] + [tile(p, 4), tile(0, p)]
        edge = [side(tile(7, 0), 8 * p, tile(5, 0), 8 * p)]
        for t in range(tiles):
            edge.append(side(tile(2, p), 8 * t, tile(3, p), 8 * t))
        edge.append(side(tile(4, 0), 8 * p, tile(6, 0), 8 * p))
        planes.append(
            jnp.concatenate([jnp.concatenate(main, axis=0), jnp.concatenate(edge, axis=0)], axis=1)
        )
    wide_rows, wide_columns = planes[0].shape
    filled = planes[1] > 0.0
    scale = jnp.where(filled, RELAX / jnp.where(filled, planes[1], 1.0), 0.0)
    source = scale * planes[0]
    south = scale * planes[2]
    north = scale * pltpu.roll(planes[2], 1, 0)
    east = scale * planes[3]
    west = scale * pltpu.roll(planes[3], 1, 1)

    def around(field):
        return (
            pltpu.roll(field, wide_rows - 1, 0),
            pltpu.roll(field, 1, 0),
            pltpu.roll(field, wide_columns - 1, 1),
            pltpu.roll(field, 1, 1),
        )

    field = source
    for _ in range(SWEEPS - 1):
        s, n, e, w = around(field)
        field = (1.0 - RELAX) * field + source + south * s + north * n + east * e + west * w
    near = around(field)
    own = field[8 : 8 + height, 0:width]
    near = [n[8 : 8 + height, 0:width] for n in near]
    correction[...] = own

    def layer(z, carry):
        push = face[0, z] * own
        for d in range(4):
            push = push + face[1 + d, z] * near[d]
        for i in range(3):
            new_state[i, z] = base[i, z] + gain[i, z] * push
        return carry

    lax.fori_loop(0, depth, layer, 0)


def shape_of(*dims):
    return jax.ShapeDtypeStruct(dims, F32)


def per_device(state, right_side, permeability, pore_volume, facies, storage_table, coupling_table):
    _, depth, height, width = state.shape
    layers = lax.axis_size("gz")
    row_of, rows, columns = lax.axis_size("gx"), lax.axis_size("gy"), lax.axis_size("gz")

    faces = pl.pallas_call(
        faces_kernel,
        out_shape=[shape_of(4, height, width)] * 2 + [shape_of(4, depth, width)] * 2 + [shape_of(4, 8, 128)] * 2,
        in_specs=vmem(2),
        out_specs=vmem(6),
        compiler_params=PARAMS,
    )(state, permeability)

    def from_next(first, axis):
        n = lax.axis_size(axis)
        return lax.ppermute(first, axis, [(i + 1, i) for i in range(n - 1)])

    def from_previous(last, axis):
        n = lax.axis_size(axis)
        return lax.ppermute(last, axis, [(i, i + 1) for i in range(n - 1)])

    around = []
    for axis, first, last in (("gz", 0, 1), ("gy", 2, 3), ("gx", 4, 5)):
        around += [from_previous(faces[last], axis), from_next(faces[first], axis)]

    base, gain, face, message = pl.pallas_call(
        cells_kernel,
        out_shape=[
            shape_of(3, depth, height, width),
            shape_of(3, depth, height, width),
            shape_of(5, depth, height, width),
            shape_of(layers, 40, 128),
        ],
        in_specs=smem(3) + vmem(10),
        out_specs=vmem(4),
        scratch_shapes=[pltpu.VMEM((4, height, width), F32)],
        compiler_params=PARAMS,
    )(
        facies,
        storage_table.reshape(-1, 9),
        coupling_table.reshape(-1, 9),
        state,
        right_side,
        permeability,
        pore_volume,
        *around,
    )

    parts = lax.all_to_all(message, "gz", 0, 0)
    share = pl.pallas_call(
        sum_kernel,
        out_shape=shape_of(40, 128),
        in_specs=vmem(1),
        out_specs=pl.BlockSpec(memory_space=pltpu.VMEM),
        compiler_params=PARAMS,
    )(parts)
    pairs = []
    for x in range(row_of):
        for y in range(rows):
            for k, (dy, dx) in enumerate(DIRECTIONS):
                if 0 <= x + dx < row_of and 0 <= y + dy < rows:
                    pairs.append(
                        ((x * rows + y) * columns + k, ((x + dx) * rows + y + dy) * columns + k)
                    )
    strip = lax.ppermute(share[:32], ("gx", "gy", "gz"), pairs)
    corner = lax.axis_index("gz") >= 4
    tile_row = lax.broadcasted_iota(jnp.int32, (40, 128), 0)
    take_strip = (tile_row < 8) | ((tile_row < 32) & jnp.logical_not(corner))
    padded = jnp.concatenate([strip, share[32:]], axis=0)
    merged = jnp.where(take_strip, padded, share)
    shares = lax.all_to_all(jnp.broadcast_to(merged[None], (layers, 40, 128)), "gz", 0, 0)

    new_state, correction = pl.pallas_call(
        sweep_kernel,
        out_shape=[shape_of(3, depth, height, width), shape_of(height, width)],
        in_specs=vmem(4),
        out_specs=vmem(2),
        compiler_params=PARAMS,
    )(shares, base, gain, face)
    return (new_state, correction)


def solution(mesh):
    return jax.shard_map(
        per_device,
        mesh=mesh,
        in_specs=(
            P(None, "gz", "gy", "gx"),
            P(None, "gz", "gy", "gx"),
            P("gz", "gy", "gx"),
            P("gz", "gy", "gx"),
            P("gz"),
            P(),
            P(),
        ),
        out_specs=(P(None, "gz", "gy", "gx"), P("gy", "gx")),
        check_vma=False,
    )
```

```python
import jax
import jax.numpy as jnp
from jax import lax
from jax.experimental import pallas as pl
from jax.experimental.pallas import tpu as pltpu
from jax.sharding import PartitionSpec as P

SWEEPS = 8
RELAX = 0.8
DIRECTIONS = ((-1, 0), (1, 0), (0, -1), (0, 1), (-1, -1), (1, 1), (-1, 1), (1, -1))
F32 = jnp.float32
PARAMS = pltpu.CompilerParams(vmem_limit_bytes=16 * 2**20)
CHUNK = 4


def vmem(count):
    return [pl.BlockSpec(memory_space=pltpu.VMEM)] * count


def hbm(count):
    return [pl.BlockSpec(memory_space=pltpu.HBM)] * count


def shape_of(*dims):
    return jax.ShapeDtypeStruct(dims, F32)


def in_hbm(*arrays):
    return [pltpu.with_memory_space_constraint(a, pltpu.HBM) for a in arrays]


def lane_index(shape):
    return lax.broadcasted_iota(jnp.int32, shape, len(shape) - 1)


def row_index(shape):
    return lax.broadcasted_iota(jnp.int32, shape, len(shape) - 2)


def turn(block, shift, axis):
    shift = shift % block.shape[axis]
    return pltpu.roll(block, shift, axis) if shift else block


def inverse(value):
    guess = pl.reciprocal(value, approx=True)
    return guess * (2.0 - value * guess)


def mean_weight(a, b):
    return (a + a) * b * inverse(a + b)


def faces_kernel(
    state, right, perm, pore, facies, storage_table, coupling_table,
    state_v, right_v, perm_v, pore_v, coef, coef_lane, zlo, zhi, ylo, yhi, xpack,
    perm_half, pore_half, facies_s, storage_s, coupling_s, sems,
):
    depth, height, width = perm.shape
    tiles, half = height // 8, depth // 2
    copies = [
        pltpu.make_async_copy(perm, perm_half, sems.at[0]),
        pltpu.make_async_copy(pore, pore_half, sems.at[1]),
        pltpu.make_async_copy(facies, facies_s, sems.at[2]),
        pltpu.make_async_copy(storage_table, storage_s, sems.at[3]),
        pltpu.make_async_copy(coupling_table, coupling_s, sems.at[4]),
        pltpu.make_async_copy(right.at[0], right_v, sems.at[5]),
    ]
    pieces = [
        pltpu.make_async_copy(state.at[:, pl.ds(z, CHUNK)], state_v.at[:, pl.ds(z, CHUNK)], sems.at[6 + z // CHUNK])
        for z in range(0, depth, CHUNK)
    ]
    copies[0].start()
    for piece in pieces:
        piece.start()
    for copy in copies[1:]:
        copy.start()
    lanes = lane_index((8, 128))
    pairs = lanes // 2
    packed = [[jnp.full((8, 128), 1.0 if c == 3 else 0.0, F32) for _ in range(2)] for c in range(4)]
    copies[0].wait()
    for z in range(depth):
        if z % CHUNK == 0:
            pieces[z // CHUNK].wait()
        for c in range(4):
            if c < 3:
                cells = state_v[c, z]
            else:
                cells = perm_half[z].astype(F32)
                perm_v[z] = cells
            ylo[c, z : z + 1, :] = cells[0:1]
            yhi[c, z : z + 1, :] = cells[height - 1 : height]
            if z == 0:
                zlo[c] = cells
            if z == depth - 1:
                zhi[c] = cells
            for t in range(tiles):
                i = (z % half) * tiles + t
                turned = turn(cells[8 * t : 8 * t + 8], 2 * i + 1, 1)
                packed[c][z // half] = jnp.where(pairs == i, turned, packed[c][z // half])
    for c in range(4):
        for h in range(2):
            xpack[c, h] = packed[c][h]
    for copy in copies[1:5]:
        copy.wait()
    for z in range(depth):
        pore_v[z] = pore_half[z].astype(F32)
    rows = row_index((depth, 128))
    fids = jnp.zeros((depth, 128), jnp.int32)
    fids_lane = [jnp.zeros((8, 128), jnp.int32) for _ in range(2)]
    for z in range(depth):
        fid = facies_s[z]
        fids = jnp.where(rows == z, fid, fids)
        fids_lane[z // half] = jnp.where(lanes >= 2 * tiles * (z % half), fid, fids_lane[z // half])
    kinds = storage_table.shape[1]
    for which, table in enumerate((storage_s, coupling_s)):
        for k in range(9):
            rows_of = jnp.zeros((depth, 128), F32)
            for f in range(kinds):
                rows_of = jnp.where(fids == f, table[k // 3, f, k % 3], rows_of)
            coef[9 * which + k] = rows_of
    for k in range(3):
        for h in range(2):
            lane_of = jnp.zeros((8, 128), F32)
            for f in range(kinds):
                lane_of = jnp.where(fids_lane[h] == f, coupling_s[0, f, k], lane_of)
            coef_lane[k, h] = lane_of
    copies[5].wait()


def sums_kernel(
    coef, coef_lane, state, right, perm, pore, ylo_own, yhi_own, xpack, zlo, zhi, ylo, yhi, xlo, xhi,
    layer_out, areal_out, xnear, message,
    acc, layer_face, areal_face, sems,
):
    depth, height, width = perm.shape
    tiles, half = height // 8, depth // 2
    rows = row_index((height, width))
    lanes = lane_index((height, width))
    lane = lane_index((8, 128))

    def flat(own, near, k0):
        weight = mean_weight(own[3], near[3])
        jump = k0[0] * (own[0] - near[0]) + k0[1] * (own[1] - near[1]) + k0[2] * (own[2] - near[2])
        return weight, weight * jump

    def down_rows(block):
        return jnp.sum(block, axis=0, keepdims=True)

    k_rows = [coef[9 + k] for k in range(3)]
    south, south_flux = flat([yhi_own[c] for c in range(4)], [yhi[c] for c in range(4)], k_rows)
    north, north_flux = flat([ylo_own[c] for c in range(4)], [ylo[c] for c in range(4)], k_rows)
    south_sum, north_sum = down_rows(k_rows[0] * south), down_rows(k_rows[0] * north)
    south_flux, north_flux = down_rows(south_flux), down_rows(north_flux)
    side, side_sum, side_flux = [], 0.0, 0.0
    for h in range(2):
        near = [jnp.where(lane % 2 == 0, turn(xhi[c, h], -1, 1), turn(xlo[c, h], 1, 1)) for c in range(4)]
        for c in range(3):
            xnear[c, h] = near[c]
        weight, flux = flat([xpack[c, h] for c in range(4)], near, [coef_lane[k, h] for k in range(3)])
        used = lane < 2 * tiles * half
        side.append(weight)
        side_sum += jnp.where(used, coef_lane[0, h] * weight, 0.0)
        side_flux += jnp.where(used, flux, 0.0)
    gap = tiles * half
    while gap >= 2 * tiles:
        side_sum = side_sum + turn(side_sum, -gap, 1)
        side_flux = side_flux + turn(side_flux, -gap, 1)
        gap //= 2

    def row_of(k, z):
        return coef[k, pl.ds(z, 1), :]

    weight = mean_weight(zlo[3], perm[0])
    layer_face[0] = weight
    for a in range(1, 6):
        acc[a] = jnp.zeros((height, width), F32)
    acc[0] = -weight * (
        row_of(9, 0) * (state[0, 0] - zlo[0])
        + row_of(10, 0) * (state[1, 0] - zlo[1])
        + row_of(11, 0) * (state[2, 0] - zlo[2])
    )

    def layer(z, below, step, side_here, shift):
        q = perm[z]
        u = [state[c, z] for c in range(3)]
        k0 = [row_of(9 + c, z) for c in range(3)]
        down = mean_weight(q, below[3])
        layer_face[z + 1] = down
        jump = step[0] * (u[0] - below[0]) + step[1] * (u[1] - below[1]) + step[2] * (u[2] - below[2])
        v = pore[z]
        acc[0] += (
            right[z]
            - v * (row_of(0, z) * u[0] + row_of(1, z) * u[1] + row_of(2, z) * u[2])
            - down * jump
        )
        acc[1] += row_of(0, z) * v
        w = k0[0] * u[0] + k0[1] * u[1] + k0[2] * u[2]
        ty = jnp.where(rows == height - 1, 0.0, mean_weight(q, turn(q, -1, 0)))
        tx = jnp.where(lanes == width - 1, 0.0, mean_weight(q, turn(q, -1, 1)))
        acc[2] += k0[0] * ty
        acc[3] += k0[0] * tx
        acc[4] += ty * (w - turn(w, -1, 0))
        acc[5] += tx * (w - turn(w, -1, 1))
        edges = jnp.concatenate(
            [pltpu.roll(side_here, shift - 2 * t, 1) for t in range(tiles)], axis=0
        )
        areal_face[0, z] = jnp.where(rows == height - 1, areal_face[0, z, 0:1, :], ty)
        areal_face[1, z] = jnp.where(rows == 0, areal_face[1, z, 0:1, :], turn(ty, 1, 0))
        areal_face[2, z] = jnp.where(lanes == width - 1, edges, tx)
        areal_face[3, z] = jnp.where(lanes == 0, edges, turn(tx, 1, 1))

    for z in range(depth):
        areal_face[0, z, 0:1, :] = south[z : z + 1]
        areal_face[1, z, 0:1, :] = north[z : z + 1]

    def keep(h):
        tops, all_areal = pl.ds(h * (half + 1), half + 1 - h), pl.ds(h * half, half)
        copies = [
            pltpu.make_async_copy(layer_face.at[tops], layer_out.at[tops], sems.at[2 * h]),
            pltpu.make_async_copy(areal_face.at[:, all_areal], areal_out.at[:, all_areal], sems.at[2 * h + 1]),
        ]
        for copy in copies:
            copy.start()
        return copies

    for h in range(2):

        def body(z, carry, h=h):
            below = [state[c, z + 1] for c in range(3)] + [perm[z + 1]]
            step = [row_of(9 + c, z) - row_of(9 + c, z + 1) for c in range(3)]
            layer(z, below, step, side[h], 127 - 2 * tiles * (z - h * half))
            return carry

        lax.fori_loop(h * half, half if h == 0 else depth - 1, body, 0)
        if h == 0:
            copies = keep(0)
    z = depth - 1
    layer(z, [zhi[c] for c in range(4)], [row_of(9 + c, z) for c in range(3)], side[1], 127 - 2 * tiles * (half - 1))

    copies += keep(1)
    rhs, diag, ty, tx = acc[0], acc[1], acc[2], acc[3]
    fy, fx = acc[4], acc[5]
    edge_sum = jnp.concatenate([turn(side_sum, 127 - 2 * t, 1) for t in range(tiles)], axis=0)
    edge_flux = jnp.concatenate([turn(side_flux, 127 - 2 * t, 1) for t in range(tiles)], axis=0)
    last_row, first_row, last_lane, first_lane = rows == height - 1, rows == 0, lanes == width - 1, lanes == 0
    ty_plus, ty_minus = jnp.where(last_row, south_sum, ty), jnp.where(first_row, north_sum, turn(ty, 1, 0))
    tx_plus, tx_minus = jnp.where(last_lane, edge_sum, tx), jnp.where(first_lane, edge_sum, turn(tx, 1, 1))
    fy_plus, fy_minus = jnp.where(last_row, south_flux, fy), jnp.where(first_row, north_flux, -turn(fy, 1, 0))
    fx_plus, fx_minus = jnp.where(last_lane, edge_flux, fx), jnp.where(first_lane, edge_flux, -turn(fx, 1, 1))
    planes = [
        rhs - (fy_plus + fy_minus) - (fx_plus + fx_minus),
        diag + (ty_plus + ty_minus) + (tx_plus + tx_minus),
        ty_plus,
        tx_plus,
    ]

    last = tiles - 1

    def tile(p, t):
        return planes[p][8 * t : 8 * t + 8]

    for p in range(4):
        message[0, 8 * p : 8 * p + 8, :] = tile(p, 0)
        message[1, 8 * p : 8 * p + 8, :] = tile(p, last)
        left = jnp.zeros((8, 128), F32)
        right_side = jnp.zeros((8, 128), F32)
        for t in range(tiles):
            here = lane // 8 == t
            left = jnp.where(here, turn(tile(p, t), 8 * t, 1), left)
            right_side = jnp.where(here, turn(tile(p, t), 8 * t + 8, 1), right_side)
        message[2, 8 * p : 8 * p + 8, :] = left
        message[3, 8 * p : 8 * p + 8, :] = right_side
    for k, (t, at_end) in enumerate(((0, 0), (last, 1), (0, 1), (last, 0))):
        corner = jnp.zeros((8, 128), F32)
        for p in range(4):
            corner = jnp.where(lane // 8 == p, turn(tile(p, t), 8 * p + 8 * at_end, 1), corner)
        message[4 + k, 0:8, :] = corner
        for t in range(4):
            message[4 + k, 8 + 8 * t : 16 + 8 * t, :] = tile(k, t)
        message[k, 32:40, :] = tile(k, last)
    for copy in copies:
        copy.wait()


def cells_kernel(
    h, coef, z_face, ylo, yhi, xnear, order, state_in, right_in, pore_in, layer_in, areal_in,
    base_out, gain_out,
    state, right, pore, layer_face, areal_face, base, gain, sems,
):
    del order
    half, height, width = pore.shape
    tiles, first, pieces = height // 8, h * half, half // CHUNK
    rows = row_index((height, width))
    lanes = lane_index((height, width))
    arrivals = []
    for p in range(pieces):
        here, there = pl.ds(p * CHUNK, CHUNK), pl.ds(first + p * CHUNK, CHUNK)
        low, high = (0 if p == 0 else p * CHUNK + 1), (p + 1) * CHUNK + 1
        state_low = 1 if p == 0 and h == 0 else (0 if p == 0 else p * CHUNK + 2)
        state_high = (p + 1) * CHUNK + (1 if p == pieces - 1 and h == 1 else 2)
        z_low = first - 1 + state_low
        arrivals.append([
            pltpu.make_async_copy(
                state_in.at[:, pl.ds(z_low, state_high - state_low)],
                state.at[:, pl.ds(state_low, state_high - state_low)],
                sems.at[0, p],
            ),
            pltpu.make_async_copy(
                layer_in.at[pl.ds(first + low, high - low)], layer_face.at[pl.ds(low, high - low)], sems.at[1, p]
            ),
            pltpu.make_async_copy(areal_in.at[:, there], areal_face.at[:, here], sems.at[2, p]),
            pltpu.make_async_copy(right_in.at[:, there], right.at[:, here], sems.at[3, p]),
            pltpu.make_async_copy(pore_in.at[there], pore.at[here], sems.at[4, p]),
        ])
    for group in arrivals:
        for copy in group:
            copy.start()
    for c in range(3):
        state[c, 0 if h == 0 else half + 1] = z_face[c]

    def layer(i, carry):
        z = first + i
        m = [[coef[3 * r + c, pl.ds(z, 1), :] for c in range(3)] for r in range(3)]
        k = [[coef[9 + 3 * r + c, pl.ds(z, 1), :] for c in range(3)] for r in range(3)]
        weights = [layer_face[i + 1], layer_face[i]] + [areal_face[d, i] for d in range(4)]
        total = weights[0] + weights[1] + weights[2] + weights[3] + weights[4] + weights[5]
        cells, flux = [], []
        for c in range(3):
            u = state[c, i + 1]
            edges = jnp.concatenate(
                [pltpu.roll(xnear[c, h], 127 - 2 * tiles * i - 2 * t, 1) for t in range(tiles)], axis=0
            )
            near = (
                state[c, i + 2],
                state[c, i],
                jnp.where(rows == height - 1, yhi[c, pl.ds(z, 1), :], turn(u, -1, 0)),
                jnp.where(rows == 0, ylo[c, pl.ds(z, 1), :], turn(u, 1, 0)),
                jnp.where(lanes == width - 1, edges, turn(u, -1, 1)),
                jnp.where(lanes == 0, edges, turn(u, 1, 1)),
            )
            moved = weights[0] * (u - near[0])
            for w, n in zip(weights[1:], near[1:]):
                moved = moved + w * (u - n)
            cells.append(u)
            flux.append(moved)
        v = pore[i].astype(F32)
        residual = [
            right[r, i]
            - v * (m[r][0] * cells[0] + m[r][1] * cells[1] + m[r][2] * cells[2])
            - (k[r][0] * flux[0] + k[r][1] * flux[1] + k[r][2] * flux[2])
            for r in range(3)
        ]
        entries = [[v * m[r][c] + total * k[r][c] for c in range(3)] for r in range(3)]

        def cofactor(r, c):
            r1, r2, c1, c2 = (r + 1) % 3, (r + 2) % 3, (c + 1) % 3, (c + 2) % 3
            return entries[r1][c1] * entries[r2][c2] - entries[r1][c2] * entries[r2][c1]

        factors = [[cofactor(r, c) for c in range(3)] for r in range(3)]
        determinant = (
            entries[0][0] * factors[0][0] + entries[0][1] * factors[0][1] + entries[0][2] * factors[0][2]
        )
        scale = inverse(determinant)
        for r in range(3):
            base[r, i] = cells[r] + scale * (
                factors[0][r] * residual[0] + factors[1][r] * residual[1] + factors[2][r] * residual[2]
            )
            gain[r, i] = scale * (factors[0][r] * k[0][0] + factors[1][r] * k[1][0] + factors[2][r] * k[2][0])
        return carry

    departures = []
    for p in range(pieces):
        for copy in arrivals[p]:
            copy.wait()
        lax.fori_loop(p * CHUNK, (p + 1) * CHUNK, layer, 0)
        here = pl.ds(p * CHUNK, CHUNK)
        for n, (source, target) in enumerate(((base, base_out), (gain, gain_out))):
            copy = pltpu.make_async_copy(source.at[:, here], target.at[:, here], sems.at[5 + n, p])
            copy.start()
            departures.append(copy)
    for copy in departures:
        copy.wait()


def total_kernel(parts, total, strip):
    result = parts[0]
    for i in range(1, parts.shape[0]):
        result = result + parts[i]
    total[...] = result
    strip[...] = result[: strip.shape[0]]


def sweep_kernel(
    shares, base0, gain0, base1, gain1, layer_in, areal_in, new_state, correction,
    base, gain, layer_face, areal_face, result, plane, sems,
):
    _, depth, height, width = areal_face.shape
    tiles, half = height // 8, depth // 2
    lane = lane_index((8, 128))
    arrivals = []
    for p in range(depth // CHUNK):
        first = p * CHUNK
        here, there = pl.ds(first, CHUNK), pl.ds(first % half, CHUNK)
        low = 0 if p == 0 else first + 1
        layers = pl.ds(low, first + CHUNK + 1 - low)
        arrivals.append([
            pltpu.make_async_copy((base0 if first < half else base1).at[:, there], base.at[:, here], sems.at[1, p]),
            pltpu.make_async_copy((gain0 if first < half else gain1).at[:, there], gain.at[:, here], sems.at[2, p]),
            pltpu.make_async_copy(layer_in.at[layers], layer_face.at[layers], sems.at[3, p]),
            pltpu.make_async_copy(areal_in.at[:, here], areal_face.at[:, here], sems.at[4, p]),
        ])
    for group in arrivals:
        for copy in group:
            copy.start()

    def tile(k, t):
        return shares[k, 8 * t : 8 * t + 8, :]

    def side(right, right_at, left, left_at):
        right, left = turn(right, -right_at, 1), turn(left, width - 8 - left_at, 1)
        return jnp.where(lane < 8, right, jnp.where(lane >= width - 8, left, 0.0))

    planes = []
    for p in range(4):
        main = [tile(1, p)] + [tile(4 + p, 1 + t) for t in range(tiles - 1)] + [tile(p, 4), tile(0, p)]
        edge = [side(tile(7, 0), 8 * p, tile(5, 0), 8 * p)]
        for t in range(tiles):
            edge.append(side(tile(2, p), 8 * t, tile(3, p), 8 * t))
        edge.append(side(tile(4, 0), 8 * p, tile(6, 0), 8 * p))
        planes.append(
            jnp.concatenate([jnp.concatenate(main, axis=0), jnp.concatenate(edge, axis=0)], axis=1)
        )
    filled = planes[1] > 0.0
    scale = jnp.where(filled, RELAX / jnp.where(filled, planes[1], 1.0), 0.0)
    source = scale * planes[0]
    south = scale * planes[2]
    north = scale * turn(planes[2], 1, 0)
    east = scale * planes[3]
    west = scale * turn(planes[3], 1, 1)

    def around(field):
        return turn(field, -1, 0), turn(field, 1, 0), turn(field, -1, 1), turn(field, 1, 1)

    field = source
    for _ in range(SWEEPS - 1):
        s, n, e, w = around(field)
        field = ((1.0 - RELAX) * field + source) + (south * s + north * n) + (east * e + west * w)
    near = around(field)
    own = field[8 : 8 + height, 0:width]
    near = [n[8 : 8 + height, 0:width] for n in near]
    plane[...] = own
    copies = [pltpu.make_async_copy(plane, correction, sems.at[0, depth // CHUNK])]
    copies[0].start()

    for first in range(0, depth, CHUNK):
        for copy in arrivals[first // CHUNK]:
            copy.wait()

        def layer(z, carry):
            push = (layer_face[z] + layer_face[z + 1]) * own
            for d in range(4):
                push = push + areal_face[d, z] * near[d]
            for r in range(3):
                result[r, z] = base[r, z] + gain[r, z] * push
            return carry

        lax.fori_loop(first, first + CHUNK, layer, 0)
        copy = pltpu.make_async_copy(
            result.at[:, pl.ds(first, CHUNK)], new_state.at[:, pl.ds(first, CHUNK)], sems.at[0, first // CHUNK]
        )
        copy.start()
        copies.append(copy)
    for copy in copies:
        copy.wait()


def call(kernel, out_shape, in_specs, out_specs, scratch=(), flops=0, moved=0):
    return pl.pallas_call(
        kernel,
        out_shape=out_shape,
        in_specs=in_specs,
        out_specs=out_specs,
        scratch_shapes=list(scratch),
        compiler_params=PARAMS,
        cost_estimate=pl.CostEstimate(flops=flops, bytes_accessed=moved, transcendentals=0) if flops else None,
    )


def per_device(state, right_side, permeability, pore_volume, facies, storage_table, coupling_table):
    _, depth, height, width = state.shape
    columns = lax.axis_size("gz")
    row_of, rows = lax.axis_size("gx"), lax.axis_size("gy")
    block = (depth, height, width)
    bf16 = jnp.bfloat16
    storage_table, coupling_table = storage_table.transpose(1, 0, 2), coupling_table.transpose(1, 0, 2)

    state_v, right_v, perm_v, pore_v, coef, coef_lane, zlo, zhi, ylo, yhi, xpack = call(
        faces_kernel,
        [shape_of(3, *block), shape_of(*block), shape_of(*block), shape_of(*block)]
        + [shape_of(18, depth, 128), shape_of(3, 2, 8, 128)]
        + [shape_of(4, height, width)] * 2 + [shape_of(4, depth, width)] * 2 + [shape_of(4, 2, 8, 128)],
        hbm(7),
        vmem(11),
        [
            pltpu.VMEM(block, bf16),
            pltpu.VMEM(block, bf16),
            pltpu.SMEM(facies.shape, jnp.int32),
            pltpu.SMEM(storage_table.shape, F32),
            pltpu.SMEM(coupling_table.shape, F32),
            pltpu.SemaphoreType.DMA((6 + depth // CHUNK,)),
        ],
    )(*in_hbm(state, right_side, permeability, pore_volume, facies, storage_table, coupling_table))

    def from_next(first, axis):
        n = lax.axis_size(axis)
        return lax.ppermute(first, axis, [(i + 1, i) for i in range(n - 1)])

    def from_previous(last, axis):
        n = lax.axis_size(axis)
        return lax.ppermute(last, axis, [(i, i + 1) for i in range(n - 1)])

    around = []
    for axis, first, last in (("gz", zlo, zhi), ("gy", ylo, yhi), ("gx", xpack, xpack)):
        around += [from_previous(last, axis), from_next(first, axis)]
    zlo_near, zhi_near, ylo_near, yhi_near, xlo_near, xhi_near = around

    layer_face, areal_face, xnear, message = call(
        sums_kernel,
        [
            pltpu.HBM((depth + 1, height, width), F32),
            pltpu.HBM((4, *block), F32),
            shape_of(3, 2, 8, 128),
            shape_of(columns, 40, 128),
        ],
        vmem(15),
        hbm(2) + vmem(2),
        [
            pltpu.VMEM((6, height, width), F32),
            pltpu.VMEM((depth + 1, height, width), F32),
            pltpu.VMEM((4, *block), F32),
            pltpu.SemaphoreType.DMA((4,)),
        ],
    )(coef, coef_lane, state_v, right_v, perm_v, pore_v, ylo, yhi, xpack, *around)

    def cells(h, z_near, order):
        def kernel(*refs):
            cells_kernel(h, *refs)

        layers = depth // 2
        half = (layers, height, width)
        return call(
            kernel,
            [pltpu.HBM((3, *half), F32)] * 2,
            vmem(6) + hbm(5),
            hbm(2),
            [
                pltpu.VMEM((3, layers + 2, height, width), F32),
                pltpu.VMEM((3, *half), F32),
                pltpu.VMEM(half, bf16),
                pltpu.VMEM((layers + 1, height, width), F32),
                pltpu.VMEM((4, *half), F32),
                pltpu.VMEM((3, *half), F32),
                pltpu.VMEM((3, *half), F32),
                pltpu.SemaphoreType.DMA((7, layers // CHUNK)),
            ],
            flops=3 * 10**9,
            moved=3 * 10**6,
        )(coef, z_near, ylo_near, yhi_near, xnear, order, *in_hbm(state, right_side, pore_volume, layer_face, areal_face))

    parts = lax.all_to_all(message, "gz", 0, 0)
    base0, gain0 = cells(0, zlo_near, xnear)
    share, strip = call(total_kernel, [shape_of(40, 128), shape_of(32, 128)], vmem(1), vmem(2))(parts)
    pairs = []
    for x in range(row_of):
        for y in range(rows):
            for k, (dy, dx) in enumerate(DIRECTIONS):
                if 0 <= x + dx < row_of and 0 <= y + dy < rows:
                    pairs.append(
                        ((x * rows + y) * columns + k, ((x + dx) * rows + y + dy) * columns + k)
                    )
    strip = lax.ppermute(strip, ("gx", "gy", "gz"), pairs)
    base1, gain1 = cells(1, zhi_near, share)
    corner = lax.axis_index("gz") >= 4
    tile_row = lax.broadcasted_iota(jnp.int32, (40, 128), 0)
    take_strip = (tile_row < 8) | ((tile_row < 32) & jnp.logical_not(corner))
    padded = jnp.concatenate([strip, share[32:]], axis=0)
    merged = jnp.where(take_strip, padded, share)
    shares = lax.all_to_all(jnp.broadcast_to(merged[None], (columns, 40, 128)), "gz", 0, 0)

    new_state, correction = call(
        sweep_kernel,
        [pltpu.HBM((3, *block), F32), pltpu.HBM((height, width), F32)],
        vmem(1) + hbm(6),
        hbm(2),
        [
            pltpu.VMEM((3, *block), F32),
            pltpu.VMEM((3, *block), F32),
            pltpu.VMEM((depth + 1, height, width), F32),
            pltpu.VMEM((4, *block), F32),
            pltpu.VMEM((3, *block), F32),
            pltpu.VMEM((height, width), F32),
            pltpu.SemaphoreType.DMA((5, depth // CHUNK + 1)),
        ],
    )(shares, *in_hbm(base0, gain0, base1, gain1, layer_face, areal_face))
    return (new_state, correction)


def solution(mesh):
    return jax.shard_map(
        per_device,
        mesh=mesh,
        in_specs=(
            P(None, "gz", "gy", "gx"),
            P(None, "gz", "gy", "gx"),
            P("gz", "gy", "gx"),
            P("gz", "gy", "gx"),
            P("gz"),
            P(),
            P(),
        ),
        out_specs=(P(None, "gz", "gy", "gx"), P("gy", "gx")),
        check_vma=False,
    )
```

```python
import jax
import jax.numpy as jnp
from jax import lax
from jax.experimental import pallas as pl
from jax.experimental.pallas import tpu as pltpu
from jax.sharding import PartitionSpec as P

SWEEPS = 8
RELAX = 0.8
DIRECTIONS = ((-1, 0), (1, 0), (0, -1), (0, 1), (-1, -1), (1, 1), (-1, 1), (1, -1))
F32 = jnp.float32
PARAMS = pltpu.CompilerParams(vmem_limit_bytes=16 * 2**20)
CHUNK = 4


def vmem(count):
    return [pl.BlockSpec(memory_space=pltpu.VMEM)] * count


def hbm(count):
    return [pl.BlockSpec(memory_space=pltpu.HBM)] * count


def shape_of(*dims):
    return jax.ShapeDtypeStruct(dims, F32)


def in_hbm(*arrays):
    return [pltpu.with_memory_space_constraint(a, pltpu.HBM) for a in arrays]


def lane_index(shape):
    return lax.broadcasted_iota(jnp.int32, shape, len(shape) - 1)


def row_index(shape):
    return lax.broadcasted_iota(jnp.int32, shape, len(shape) - 2)


def turn(block, shift, axis):
    shift = shift % block.shape[axis]
    return pltpu.roll(block, shift, axis) if shift else block


def inverse(value):
    guess = pl.reciprocal(value, approx=True)
    return guess * (2.0 - value * guess)


def mean_weight(a, b):
    return (a + a) * b * inverse(a + b)


def faces_kernel(
    state, right, perm, pore, facies, storage_table, coupling_table,
    state_v, right_v, perm_v, pore_v, coef, coef_lane, zlo, zhi, ylo, yhi, xpack,
    perm_half, pore_half, facies_s, storage_s, coupling_s, sems,
):
    depth, height, width = perm.shape
    tiles, half = height // 8, depth // 2
    copies = [
        pltpu.make_async_copy(perm, perm_half, sems.at[0]),
        pltpu.make_async_copy(pore, pore_half, sems.at[1]),
        pltpu.make_async_copy(facies, facies_s, sems.at[2]),
        pltpu.make_async_copy(storage_table, storage_s, sems.at[3]),
        pltpu.make_async_copy(coupling_table, coupling_s, sems.at[4]),
        pltpu.make_async_copy(right.at[0], right_v, sems.at[5]),
    ]
    pieces = [
        pltpu.make_async_copy(state.at[:, pl.ds(z, CHUNK)], state_v.at[:, pl.ds(z, CHUNK)], sems.at[6 + z // CHUNK])
        for z in range(0, depth, CHUNK)
    ]
    copies[0].start()
    for piece in pieces:
        piece.start()
    for copy in copies[1:]:
        copy.start()
    lanes = lane_index((8, 128))
    pairs = lanes // 2
    packed = [[jnp.full((8, 128), 1.0 if c == 3 else 0.0, F32) for _ in range(2)] for c in range(4)]
    copies[0].wait()
    for z in range(depth):
        if z % CHUNK == 0:
            pieces[z // CHUNK].wait()
        for c in range(4):
            if c < 3:
                cells = state_v[c, z]
            else:
                cells = perm_half[z].astype(F32)
                perm_v[z] = cells
            ylo[c, z : z + 1, :] = cells[0:1]
            yhi[c, z : z + 1, :] = cells[height - 1 : height]
            if z == 0:
                zlo[c] = cells
            if z == depth - 1:
                zhi[c] = cells
            for t in range(tiles):
                i = (z % half) * tiles + t
                turned = turn(cells[8 * t : 8 * t + 8], 2 * i + 1, 1)
                packed[c][z // half] = jnp.where(pairs == i, turned, packed[c][z // half])
    for c in range(4):
        for h in range(2):
            xpack[c, h] = packed[c][h]
    for copy in copies[1:5]:
        copy.wait()
    for z in range(depth):
        pore_v[z] = pore_half[z].astype(F32)
    rows = row_index((depth, 128))
    fids = jnp.zeros((depth, 128), jnp.int32)
    fids_lane = [jnp.zeros((8, 128), jnp.int32) for _ in range(2)]
    for z in range(depth):
        fid = facies_s[z]
        fids = jnp.where(rows == z, fid, fids)
        fids_lane[z // half] = jnp.where(lanes >= 2 * tiles * (z % half), fid, fids_lane[z // half])
    kinds = storage_table.shape[1]
    for which, table in enumerate((storage_s, coupling_s)):
        for k in range(9):
            rows_of = jnp.zeros((depth, 128), F32)
            for f in range(kinds):
                rows_of = jnp.where(fids == f, table[k // 3, f, k % 3], rows_of)
            coef[9 * which + k] = rows_of
    for k in range(3):
        for h in range(2):
            lane_of = jnp.zeros((8, 128), F32)
            for f in range(kinds):
                lane_of = jnp.where(fids_lane[h] == f, coupling_s[0, f, k], lane_of)
            coef_lane[k, h] = lane_of
    copies[5].wait()


def sums_kernel(
    coef, coef_lane, state, right, perm, pore, ylo_own, yhi_own, xpack, zlo, zhi, ylo, yhi, xlo, xhi,
    layer_face, areal_face, xnear, message,
    acc,
):
    depth, height, width = perm.shape
    tiles, half = height // 8, depth // 2
    rows = row_index((height, width))
    lanes = lane_index((height, width))
    lane = lane_index((8, 128))

    def flat(own, near, k0):
        weight = mean_weight(own[3], near[3])
        jump = k0[0] * (own[0] - near[0]) + k0[1] * (own[1] - near[1]) + k0[2] * (own[2] - near[2])
        return weight, weight * jump

    def down_rows(block):
        return jnp.sum(block, axis=0, keepdims=True)

    k_rows = [coef[9 + k] for k in range(3)]
    south, south_flux = flat([yhi_own[c] for c in range(4)], [yhi[c] for c in range(4)], k_rows)
    north, north_flux = flat([ylo_own[c] for c in range(4)], [ylo[c] for c in range(4)], k_rows)
    south_sum, north_sum = down_rows(k_rows[0] * south), down_rows(k_rows[0] * north)
    south_flux, north_flux = down_rows(south_flux), down_rows(north_flux)
    side, side_sum, side_flux = [], 0.0, 0.0
    for h in range(2):
        near = [jnp.where(lane % 2 == 0, turn(xhi[c, h], -1, 1), turn(xlo[c, h], 1, 1)) for c in range(4)]
        for c in range(3):
            xnear[c, h] = near[c]
        weight, flux = flat([xpack[c, h] for c in range(4)], near, [coef_lane[k, h] for k in range(3)])
        used = lane < 2 * tiles * half
        side.append(weight)
        side_sum += jnp.where(used, coef_lane[0, h] * weight, 0.0)
        side_flux += jnp.where(used, flux, 0.0)
    gap = tiles * half
    while gap >= 2 * tiles:
        side_sum = side_sum + turn(side_sum, -gap, 1)
        side_flux = side_flux + turn(side_flux, -gap, 1)
        gap //= 2

    def row_of(k, z):
        return coef[k, pl.ds(z, 1), :]

    weight = mean_weight(zlo[3], perm[0])
    layer_face[0] = weight
    for a in range(1, 6):
        acc[a] = jnp.zeros((height, width), F32)
    acc[0] = -weight * (
        row_of(9, 0) * (state[0, 0] - zlo[0])
        + row_of(10, 0) * (state[1, 0] - zlo[1])
        + row_of(11, 0) * (state[2, 0] - zlo[2])
    )

    def layer(z, below, step, side_here, shift):
        q = perm[z]
        u = [state[c, z] for c in range(3)]
        k0 = [row_of(9 + c, z) for c in range(3)]
        down = mean_weight(q, below[3])
        layer_face[z + 1] = down
        jump = step[0] * (u[0] - below[0]) + step[1] * (u[1] - below[1]) + step[2] * (u[2] - below[2])
        v = pore[z]
        acc[0] += (
            right[z]
            - v * (row_of(0, z) * u[0] + row_of(1, z) * u[1] + row_of(2, z) * u[2])
            - down * jump
        )
        acc[1] += row_of(0, z) * v
        w = k0[0] * u[0] + k0[1] * u[1] + k0[2] * u[2]
        ty = jnp.where(rows == height - 1, 0.0, mean_weight(q, turn(q, -1, 0)))
        tx = jnp.where(lanes == width - 1, 0.0, mean_weight(q, turn(q, -1, 1)))
        acc[2] += k0[0] * ty
        acc[3] += k0[0] * tx
        acc[4] += ty * (w - turn(w, -1, 0))
        acc[5] += tx * (w - turn(w, -1, 1))
        edges = jnp.concatenate(
            [pltpu.roll(side_here, shift - 2 * t, 1) for t in range(tiles)], axis=0
        )
        areal_face[0, z] = jnp.where(rows == height - 1, areal_face[0, z, 0:1, :], ty)
        areal_face[1, z] = jnp.where(rows == 0, areal_face[1, z, 0:1, :], turn(ty, 1, 0))
        areal_face[2, z] = jnp.where(lanes == width - 1, edges, tx)
        areal_face[3, z] = jnp.where(lanes == 0, edges, turn(tx, 1, 1))

    for z in range(depth):
        areal_face[0, z, 0:1, :] = south[z : z + 1]
        areal_face[1, z, 0:1, :] = north[z : z + 1]

    for h in range(2):

        def body(z, carry, h=h):
            below = [state[c, z + 1] for c in range(3)] + [perm[z + 1]]
            step = [row_of(9 + c, z) - row_of(9 + c, z + 1) for c in range(3)]
            layer(z, below, step, side[h], 127 - 2 * tiles * (z - h * half))
            return carry

        lax.fori_loop(h * half, half if h == 0 else depth - 1, body, 0, unroll=True)
    z = depth - 1
    layer(z, [zhi[c] for c in range(4)], [row_of(9 + c, z) for c in range(3)], side[1], 127 - 2 * tiles * (half - 1))

    rhs, diag, ty, tx = acc[0], acc[1], acc[2], acc[3]
    fy, fx = acc[4], acc[5]
    edge_sum = jnp.concatenate([turn(side_sum, 127 - 2 * t, 1) for t in range(tiles)], axis=0)
    edge_flux = jnp.concatenate([turn(side_flux, 127 - 2 * t, 1) for t in range(tiles)], axis=0)
    last_row, first_row, last_lane, first_lane = rows == height - 1, rows == 0, lanes == width - 1, lanes == 0
    ty_plus, ty_minus = jnp.where(last_row, south_sum, ty), jnp.where(first_row, north_sum, turn(ty, 1, 0))
    tx_plus, tx_minus = jnp.where(last_lane, edge_sum, tx), jnp.where(first_lane, edge_sum, turn(tx, 1, 1))
    fy_plus, fy_minus = jnp.where(last_row, south_flux, fy), jnp.where(first_row, north_flux, -turn(fy, 1, 0))
    fx_plus, fx_minus = jnp.where(last_lane, edge_flux, fx), jnp.where(first_lane, edge_flux, -turn(fx, 1, 1))
    planes = [
        rhs - (fy_plus + fy_minus) - (fx_plus + fx_minus),
        diag + (ty_plus + ty_minus) + (tx_plus + tx_minus),
        ty_plus,
        tx_plus,
    ]

    last = tiles - 1

    def tile(p, t):
        return planes[p][8 * t : 8 * t + 8]

    for p in range(4):
        message[0, 8 * p : 8 * p + 8, :] = tile(p, 0)
        message[1, 8 * p : 8 * p + 8, :] = tile(p, last)
        left = jnp.zeros((8, 128), F32)
        right_side = jnp.zeros((8, 128), F32)
        for t in range(tiles):
            here = lane // 8 == t
            left = jnp.where(here, turn(tile(p, t), 8 * t, 1), left)
            right_side = jnp.where(here, turn(tile(p, t), 8 * t + 8, 1), right_side)
        message[2, 8 * p : 8 * p + 8, :] = left
        message[3, 8 * p : 8 * p + 8, :] = right_side
    for k, (t, at_end) in enumerate(((0, 0), (last, 1), (0, 1), (last, 0))):
        corner = jnp.zeros((8, 128), F32)
        for p in range(4):
            corner = jnp.where(lane // 8 == p, turn(tile(p, t), 8 * p + 8 * at_end, 1), corner)
        message[4 + k, 0:8, :] = corner
        for t in range(4):
            message[4 + k, 8 + 8 * t : 16 + 8 * t, :] = tile(k, t)
        message[k, 32:40, :] = tile(k, last)


def cells_kernel(
    h, coef, z_face, ylo, yhi, xnear, order, layer_face, areal_face, state_in, right_in, pore_in,
    base_out, gain_out,
    state, right, pore, base, gain, sems,
):
    del order
    half, height, width = pore.shape
    tiles, first, pieces = height // 8, h * half, half // CHUNK
    rows = row_index((height, width))
    lanes = lane_index((height, width))
    arrivals = []
    for p in range(pieces):
        here, there = pl.ds(p * CHUNK, CHUNK), pl.ds(first + p * CHUNK, CHUNK)
        state_low = 1 if p == 0 and h == 0 else (0 if p == 0 else p * CHUNK + 2)
        state_high = (p + 1) * CHUNK + (1 if p == pieces - 1 and h == 1 else 2)
        z_low = first - 1 + state_low
        arrivals.append([
            pltpu.make_async_copy(
                state_in.at[:, pl.ds(z_low, state_high - state_low)],
                state.at[:, pl.ds(state_low, state_high - state_low)],
                sems.at[0, p],
            ),
            pltpu.make_async_copy(right_in.at[:, there], right.at[:, here], sems.at[1, p]),
            pltpu.make_async_copy(pore_in.at[there], pore.at[here], sems.at[2, p]),
        ])
    for group in arrivals:
        for copy in group:
            copy.start()
    for c in range(3):
        state[c, 0 if h == 0 else half + 1] = z_face[c]

    def layer(i, carry):
        z = first + i
        m = [[coef[3 * r + c, pl.ds(z, 1), :] for c in range(3)] for r in range(3)]
        k = [[coef[9 + 3 * r + c, pl.ds(z, 1), :] for c in range(3)] for r in range(3)]
        weights = [layer_face[z + 1], layer_face[z]] + [areal_face[d, z] for d in range(4)]
        total = weights[0] + weights[1] + weights[2] + weights[3] + weights[4] + weights[5]
        cells, flux = [], []
        for c in range(3):
            u = state[c, i + 1]
            edges = jnp.concatenate(
                [pltpu.roll(xnear[c, h], 127 - 2 * tiles * i - 2 * t, 1) for t in range(tiles)], axis=0
            )
            near = (
                state[c, i + 2],
                state[c, i],
                jnp.where(rows == height - 1, yhi[c, pl.ds(z, 1), :], turn(u, -1, 0)),
                jnp.where(rows == 0, ylo[c, pl.ds(z, 1), :], turn(u, 1, 0)),
                jnp.where(lanes == width - 1, edges, turn(u, -1, 1)),
                jnp.where(lanes == 0, edges, turn(u, 1, 1)),
            )
            moved = weights[0] * (u - near[0])
            for w, n in zip(weights[1:], near[1:]):
                moved = moved + w * (u - n)
            cells.append(u)
            flux.append(moved)
        v = pore[i].astype(F32)
        residual = [
            right[r, i]
            - v * (m[r][0] * cells[0] + m[r][1] * cells[1] + m[r][2] * cells[2])
            - (k[r][0] * flux[0] + k[r][1] * flux[1] + k[r][2] * flux[2])
            for r in range(3)
        ]
        entries = [[v * m[r][c] + total * k[r][c] for c in range(3)] for r in range(3)]

        def cofactor(r, c):
            r1, r2, c1, c2 = (r + 1) % 3, (r + 2) % 3, (c + 1) % 3, (c + 2) % 3
            return entries[r1][c1] * entries[r2][c2] - entries[r1][c2] * entries[r2][c1]

        factors = [[cofactor(r, c) for c in range(3)] for r in range(3)]
        determinant = (
            entries[0][0] * factors[0][0] + entries[0][1] * factors[0][1] + entries[0][2] * factors[0][2]
        )
        scale = inverse(determinant)
        for r in range(3):
            base[r, i] = cells[r] + scale * (
                factors[0][r] * residual[0] + factors[1][r] * residual[1] + factors[2][r] * residual[2]
            )
            gain[r, i] = scale * (factors[0][r] * k[0][0] + factors[1][r] * k[1][0] + factors[2][r] * k[2][0])
        return carry

    departures = []
    for p in range(pieces):
        for copy in arrivals[p]:
            copy.wait()
        lax.fori_loop(p * CHUNK, (p + 1) * CHUNK, layer, 0, unroll=True)
        here = pl.ds(p * CHUNK, CHUNK)
        for n, (source, target) in enumerate(((base, base_out), (gain, gain_out))):
            copy = pltpu.make_async_copy(source.at[:, here], target.at[:, here], sems.at[3 + n, p])
            copy.start()
            departures.append(copy)
    for copy in departures:
        copy.wait()


def total_kernel(parts, total, strip):
    result = parts[0]
    for i in range(1, parts.shape[0]):
        result = result + parts[i]
    total[...] = result
    strip[...] = result[: strip.shape[0]]


def merge_kernel(corner, strip, share, copies):
    at_corner = corner[...] > 0
    for t in range(5):
        cells = slice(8 * t, 8 * t + 8)
        if t == 0:
            merged = strip[cells]
        elif t == 4:
            merged = share[cells]
        else:
            merged = jnp.where(at_corner, share[cells], strip[cells])
        for k in range(copies.shape[0]):
            copies[k, cells, :] = merged


def sweep_kernel(
    shares, layer_face, areal_face, base0, gain0, base1, gain1, new_state, correction,
    base, gain, result, plane, sems,
):
    _, depth, height, width = areal_face.shape
    tiles, half = height // 8, depth // 2
    lane = lane_index((8, 128))
    arrivals = []
    for p in range(depth // CHUNK):
        first = p * CHUNK
        here, there = pl.ds(first, CHUNK), pl.ds(first % half, CHUNK)
        arrivals.append([
            pltpu.make_async_copy((base0 if first < half else base1).at[:, there], base.at[:, here], sems.at[1, p]),
            pltpu.make_async_copy((gain0 if first < half else gain1).at[:, there], gain.at[:, here], sems.at[2, p]),
        ])
    for group in arrivals:
        for copy in group:
            copy.start()

    def tile(k, t):
        return shares[k, 8 * t : 8 * t + 8, :]

    def side(right, right_at, left, left_at):
        right, left = turn(right, -right_at, 1), turn(left, width - 8 - left_at, 1)
        return jnp.where(lane < 8, right, jnp.where(lane >= width - 8, left, 0.0))

    planes = []
    for p in range(4):
        main = [tile(1, p)] + [tile(4 + p, 1 + t) for t in range(tiles - 1)] + [tile(p, 4), tile(0, p)]
        edge = [side(tile(7, 0), 8 * p, tile(5, 0), 8 * p)]
        for t in range(tiles):
            edge.append(side(tile(2, p), 8 * t, tile(3, p), 8 * t))
        edge.append(side(tile(4, 0), 8 * p, tile(6, 0), 8 * p))
        planes.append(
            jnp.concatenate([jnp.concatenate(main, axis=0), jnp.concatenate(edge, axis=0)], axis=1)
        )
    filled = planes[1] > 0.0
    scale = jnp.where(filled, RELAX / jnp.where(filled, planes[1], 1.0), 0.0)
    source = scale * planes[0]
    south = scale * planes[2]
    north = scale * turn(planes[2], 1, 0)
    east = scale * planes[3]
    west = scale * turn(planes[3], 1, 1)

    def around(field):
        return turn(field, -1, 0), turn(field, 1, 0), turn(field, -1, 1), turn(field, 1, 1)

    field = source
    for _ in range(SWEEPS - 1):
        s, n, e, w = around(field)
        field = ((1.0 - RELAX) * field + source) + (south * s + north * n) + (east * e + west * w)
    near = around(field)
    own = field[8 : 8 + height, 0:width]
    near = [n[8 : 8 + height, 0:width] for n in near]
    plane[...] = own
    copies = [pltpu.make_async_copy(plane, correction, sems.at[0, depth // CHUNK])]
    copies[0].start()

    for first in range(0, depth, CHUNK):
        for copy in arrivals[first // CHUNK]:
            copy.wait()

        def layer(z, carry):
            push = (layer_face[z] + layer_face[z + 1]) * own
            for d in range(4):
                push = push + areal_face[d, z] * near[d]
            for r in range(3):
                result[r, z] = base[r, z] + gain[r, z] * push
            return carry

        lax.fori_loop(first, first + CHUNK, layer, 0, unroll=True)
        copy = pltpu.make_async_copy(
            result.at[:, pl.ds(first, CHUNK)], new_state.at[:, pl.ds(first, CHUNK)], sems.at[0, first // CHUNK]
        )
        copy.start()
        copies.append(copy)
    for copy in copies:
        copy.wait()


def call(kernel, out_shape, in_specs, out_specs, scratch=(), flops=0, moved=0):
    return pl.pallas_call(
        kernel,
        out_shape=out_shape,
        in_specs=in_specs,
        out_specs=out_specs,
        scratch_shapes=list(scratch),
        compiler_params=PARAMS,
        cost_estimate=pl.CostEstimate(flops=flops, bytes_accessed=moved, transcendentals=0) if flops else None,
    )


def per_device(state, right_side, permeability, pore_volume, facies, storage_table, coupling_table):
    _, depth, height, width = state.shape
    columns = lax.axis_size("gz")
    row_of, rows = lax.axis_size("gx"), lax.axis_size("gy")
    block = (depth, height, width)
    bf16 = jnp.bfloat16
    storage_table, coupling_table = storage_table.transpose(1, 0, 2), coupling_table.transpose(1, 0, 2)

    state_v, right_v, perm_v, pore_v, coef, coef_lane, zlo, zhi, ylo, yhi, xpack = call(
        faces_kernel,
        [shape_of(3, *block), shape_of(*block), shape_of(*block), shape_of(*block)]
        + [shape_of(18, depth, 128), shape_of(3, 2, 8, 128)]
        + [shape_of(4, height, width)] * 2 + [shape_of(4, depth, width)] * 2 + [shape_of(4, 2, 8, 128)],
        hbm(7),
        vmem(11),
        [
            pltpu.VMEM(block, bf16),
            pltpu.VMEM(block, bf16),
            pltpu.SMEM(facies.shape, jnp.int32),
            pltpu.SMEM(storage_table.shape, F32),
            pltpu.SMEM(coupling_table.shape, F32),
            pltpu.SemaphoreType.DMA((6 + depth // CHUNK,)),
        ],
    )(*in_hbm(state, right_side, permeability, pore_volume, facies, storage_table, coupling_table))

    def from_next(first, axis):
        n = lax.axis_size(axis)
        return lax.ppermute(first, axis, [(i + 1, i) for i in range(n - 1)])

    def from_previous(last, axis):
        n = lax.axis_size(axis)
        return lax.ppermute(last, axis, [(i, i + 1) for i in range(n - 1)])

    around = []
    for axis, first, last in (("gz", zlo, zhi), ("gy", ylo, yhi), ("gx", xpack, xpack)):
        around += [from_previous(last, axis), from_next(first, axis)]
    zlo_near, zhi_near, ylo_near, yhi_near, xlo_near, xhi_near = around

    layer_face, areal_face, xnear, message = call(
        sums_kernel,
        [
            shape_of(depth + 1, height, width),
            shape_of(4, *block),
            shape_of(3, 2, 8, 128),
            shape_of(columns, 40, 128),
        ],
        vmem(15),
        vmem(4),
        [pltpu.VMEM((6, height, width), F32)],
    )(coef, coef_lane, state_v, right_v, perm_v, pore_v, ylo, yhi, xpack, *around)

    def cells(h, z_near, order):
        def kernel(*refs):
            cells_kernel(h, *refs)

        layers = depth // 2
        half = (layers, height, width)
        return call(
            kernel,
            [pltpu.HBM((3, *half), F32)] * 2,
            vmem(8) + hbm(3),
            hbm(2),
            [
                pltpu.VMEM((3, layers + 2, height, width), F32),
                pltpu.VMEM((3, *half), F32),
                pltpu.VMEM(half, bf16),
                pltpu.VMEM((3, *half), F32),
                pltpu.VMEM((3, *half), F32),
                pltpu.SemaphoreType.DMA((5, layers // CHUNK)),
            ],
            flops=3 * 10**9,
            moved=3 * 10**6,
        )(
            coef, z_near, ylo_near, yhi_near, xnear, order, layer_face, areal_face,
            *in_hbm(state, right_side, pore_volume),
        )

    parts = lax.all_to_all(message, "gz", 0, 0)
    base0, gain0 = cells(0, zlo_near, xnear)
    share, strip = call(total_kernel, [shape_of(40, 128), shape_of(32, 128)], vmem(1), vmem(2))(parts)
    pairs = []
    for x in range(row_of):
        for y in range(rows):
            for k, (dy, dx) in enumerate(DIRECTIONS):
                if 0 <= x + dx < row_of and 0 <= y + dy < rows:
                    pairs.append(
                        ((x * rows + y) * columns + k, ((x + dx) * rows + y + dy) * columns + k)
                    )
    strip = lax.ppermute(strip, ("gx", "gy", "gz"), pairs)
    base1, gain1 = cells(1, zhi_near, share)
    corner = jnp.broadcast_to((lax.axis_index("gz") >= 4).astype(jnp.int32), (8, 128))
    copies = call(merge_kernel, shape_of(columns, 40, 128), vmem(3), vmem(1)[0])(corner, strip, share)
    shares = lax.all_to_all(copies, "gz", 0, 0)

    new_state, correction = call(
        sweep_kernel,
        [pltpu.HBM((3, *block), F32), pltpu.HBM((height, width), F32)],
        vmem(3) + hbm(4),
        hbm(2),
        [
            pltpu.VMEM((3, *block), F32),
            pltpu.VMEM((3, *block), F32),
            pltpu.VMEM((3, *block), F32),
            pltpu.VMEM((height, width), F32),
            pltpu.SemaphoreType.DMA((3, depth // CHUNK + 1)),
        ],
    )(shares, layer_face, areal_face, *in_hbm(base0, gain0, base1, gain1))
    return (new_state, correction)


def solution(mesh):
    return jax.shard_map(
        per_device,
        mesh=mesh,
        in_specs=(
            P(None, "gz", "gy", "gx"),
            P(None, "gz", "gy", "gx"),
            P("gz", "gy", "gx"),
            P("gz", "gy", "gx"),
            P("gz"),
            P(),
            P(),
        ),
        out_specs=(P(None, "gz", "gy", "gx"), P("gy", "gx")),
        check_vma=False,
    )
```

```python
import jax
import jax.numpy as jnp
from jax import lax
from jax.experimental import pallas as pl
from jax.experimental.pallas import tpu as pltpu
from jax.sharding import PartitionSpec as P

SWEEPS = 8
RELAX = 0.8
DIRECTIONS = ((-1, 0), (1, 0), (0, -1), (0, 1), (-1, -1), (1, 1), (-1, 1), (1, -1))
F32 = jnp.float32
PARAMS = pltpu.CompilerParams(vmem_limit_bytes=16 * 2**20)
CHUNK = 4


def vmem(count):
    return [pl.BlockSpec(memory_space=pltpu.VMEM)] * count


def hbm(count):
    return [pl.BlockSpec(memory_space=pltpu.HBM)] * count


def shape_of(*dims):
    return jax.ShapeDtypeStruct(dims, F32)


def in_hbm(*arrays):
    return [pltpu.with_memory_space_constraint(a, pltpu.HBM) for a in arrays]


def lane_index(shape):
    return lax.broadcasted_iota(jnp.int32, shape, len(shape) - 1)


def row_index(shape):
    return lax.broadcasted_iota(jnp.int32, shape, len(shape) - 2)


def turn(block, shift, axis):
    shift = shift % block.shape[axis]
    return pltpu.roll(block, shift, axis) if shift else block


def inverse(value):
    guess = pl.reciprocal(value, approx=True)
    return guess * (2.0 - value * guess)


def mean_weight(a, b):
    return (a + a) * b * inverse(a + b)


def parity(axis):
    return lax.rem(lax.axis_index(axis), 2)


def faces_kernel(state, perm, state_v, perm_v, zface0, zface1, yface0, yface1, xpack, perm_half, sems):
    depth, height, width = perm.shape
    tiles, half = height // 8, depth // 2
    fetch = pltpu.make_async_copy(perm, perm_half, sems.at[0])
    pieces = [
        pltpu.make_async_copy(state.at[:, pl.ds(z, CHUNK)], state_v.at[:, pl.ds(z, CHUNK)], sems.at[1 + z // CHUNK])
        for z in range(0, depth, CHUNK)
    ]
    fetch.start()
    for piece in pieces:
        piece.start()
    z_high, y_high = parity("gz"), parity("gy")
    lanes = lane_index((8, 128))
    pairs = lanes // 2
    packed = [[jnp.full((8, 128), 1.0 if c == 3 else 0.0, F32) for _ in range(2)] for c in range(4)]

    def pack(c, z, cells):
        low, high = cells[0:1], cells[height - 1 : height]
        yface0[c, z : z + 1, :] = jnp.where(y_high == 0, high, low)
        yface1[c, z : z + 1, :] = jnp.where(y_high == 0, low, high)
        for t in range(tiles):
            i = (z % half) * tiles + t
            turned = turn(cells[8 * t : 8 * t + 8], 2 * i + 1, 1)
            packed[c][z // half] = jnp.where(pairs == i, turned, packed[c][z // half])

    fetch.wait()
    for z in range(depth):
        perm_v[z] = perm_half[z].astype(F32)
        pack(3, z, perm_half[z].astype(F32))
    for z in range(depth):
        if z % CHUNK == 0:
            pieces[z // CHUNK].wait()
        for c in range(3):
            pack(c, z, state_v[c, z])
    for c in range(4):
        for h in range(2):
            xpack[c, h] = packed[c][h]
        low, high = (state_v[c, z] if c < 3 else perm_v[z] for z in (0, depth - 1))
        zface0[c] = jnp.where(z_high == 0, high, low)
        zface1[c] = jnp.where(z_high == 0, low, high)


def inner_kernel(
    state, perm, right, pore, facies, storage_table, coupling_table,
    coef, coef_lane, layer_face, areal_face, acc,
    right_v, pore_v, facies_s, storage_s, coupling_s, sems,
):
    depth, height, width = perm.shape
    tiles, half = height // 8, depth // 2
    copies = [
        pltpu.make_async_copy(source, target, sems.at[n])
        for n, (source, target) in enumerate(
            (
                (facies, facies_s),
                (storage_table, storage_s),
                (coupling_table, coupling_s),
                (pore, pore_v),
                (right.at[0], right_v),
            )
        )
    ]
    for copy in copies:
        copy.start()
    rows = row_index((height, width))
    lanes = lane_index((height, width))
    for z in range(depth):
        q = perm[z]
        if z < depth - 1:
            layer_face[z + 1] = mean_weight(q, perm[z + 1])
        ty = jnp.where(rows == height - 1, 0.0, mean_weight(q, turn(q, -1, 0)))
        tx = jnp.where(lanes == width - 1, 0.0, mean_weight(q, turn(q, -1, 1)))
        areal_face[0, z] = ty
        areal_face[1, z] = turn(ty, 1, 0)
        areal_face[2, z] = tx
        areal_face[3, z] = turn(tx, 1, 1)

    for copy in copies[:3]:
        copy.wait()
    lane, row = lane_index((8, 128)), row_index((depth, 128))
    fids = jnp.zeros((depth, 128), jnp.int32)
    fids_lane = [jnp.zeros((8, 128), jnp.int32) for _ in range(2)]
    for z in range(depth):
        fid = facies_s[z]
        fids = jnp.where(row == z, fid, fids)
        fids_lane[z // half] = jnp.where(lane >= 2 * tiles * (z % half), fid, fids_lane[z // half])
    kinds = storage_table.shape[1]
    for which, table in enumerate((storage_s, coupling_s)):
        for k in range(9):
            rows_of = jnp.zeros((depth, 128), F32)
            for f in range(kinds):
                rows_of = jnp.where(fids == f, table[k // 3, f, k % 3], rows_of)
            coef[9 * which + k] = rows_of
    for k in range(3):
        for h in range(2):
            lane_of = jnp.zeros((8, 128), F32)
            for f in range(kinds):
                lane_of = jnp.where(fids_lane[h] == f, coupling_s[0, f, k], lane_of)
            coef_lane[k, h] = lane_of
    for copy in copies[3:]:
        copy.wait()

    for a in range(6):
        acc[a] = jnp.zeros((height, width), F32)
    for z in range(depth):
        u = [state[c, z] for c in range(3)]
        m0 = [coef[c, z : z + 1, :] for c in range(3)]
        k0 = [coef[9 + c, z : z + 1, :] for c in range(3)]
        v = pore_v[z].astype(F32)
        part = right_v[z] - v * (m0[0] * u[0] + m0[1] * u[1] + m0[2] * u[2])
        if z < depth - 1:
            step = [k0[c] - coef[9 + c, z + 1 : z + 2, :] for c in range(3)]
            jump = [u[c] - state[c, z + 1] for c in range(3)]
            part = part - layer_face[z + 1] * (step[0] * jump[0] + step[1] * jump[1] + step[2] * jump[2])
        acc[0] += part
        acc[1] += m0[0] * v
        w = k0[0] * u[0] + k0[1] * u[1] + k0[2] * u[2]
        ty, tx = areal_face[0, z], areal_face[2, z]
        acc[2] += k0[0] * ty
        acc[3] += k0[0] * tx
        acc[4] += ty * (w - turn(w, -1, 0))
        acc[5] += tx * (w - turn(w, -1, 1))


def outer_kernel(
    coef, coef_lane, acc, zface0, zface1, yface0, yface1, xpack, z0, z1, y0, y1, x0, x1, layer_in,
    layer_face, znear, ynear, xnear, yweight, xweight, message,
):
    del layer_in
    _, height, width = zface0.shape
    depth = yface0.shape[1]
    tiles, half = height // 8, depth // 2
    rows = row_index((height, width))
    lanes = lane_index((height, width))
    lane = lane_index((8, 128))
    z_high, y_high, x_high = parity("gz"), parity("gy"), parity("gx")

    def received(high, first, second, c):
        a, b = first[c], second[c]
        return jnp.where(high == 0, b, a), jnp.where(high == 0, a, b)

    def flat(own, near, k0):
        weight = mean_weight(own[3], near[3])
        jump = k0[0] * (own[0] - near[0]) + k0[1] * (own[1] - near[1]) + k0[2] * (own[2] - near[2])
        return weight, weight * jump

    zown = [received(z_high, zface0, zface1, c) for c in range(4)]
    yown = [received(y_high, yface0, yface1, c) for c in range(4)]
    znears = [received(z_high, z0, z1, c) for c in range(4)]
    ynears = [received(y_high, y0, y1, c) for c in range(4)]
    for c in range(3):
        for e in range(2):
            znear[e, c] = znears[c][e]
            ynear[e, c] = ynears[c][e]
    rhs = acc[0]
    for e, z in ((0, 0), (1, depth - 1)):
        weight, flux = flat(
            [zown[c][e] for c in range(4)],
            [znears[c][e] for c in range(4)],
            [coef[9 + c, z : z + 1, :] for c in range(3)],
        )
        layer_face[z + e] = weight
        rhs = rhs - flux
    k_rows = [coef[9 + k] for k in range(3)]
    y_sum, y_flux = [], []
    for e in range(2):
        weight, flux = flat([yown[c][e] for c in range(4)], [ynears[c][e] for c in range(4)], k_rows)
        yweight[e] = weight
        y_sum.append(jnp.sum(k_rows[0] * weight, axis=0, keepdims=True))
        y_flux.append(jnp.sum(flux, axis=0, keepdims=True))
    side_sum, side_flux = 0.0, 0.0
    for h in range(2):
        near = []
        for c in range(4):
            west, east = jnp.where(x_high == 0, x1[c, h], x0[c, h]), jnp.where(x_high == 0, x0[c, h], x1[c, h])
            near.append(jnp.where(lane % 2 == 0, turn(east, -1, 1), turn(west, 1, 1)))
        for c in range(3):
            xnear[c, h] = near[c]
        weight, flux = flat([xpack[c, h] for c in range(4)], near, [coef_lane[k, h] for k in range(3)])
        used = lane < 2 * tiles * half
        xweight[h] = weight
        side_sum += jnp.where(used, coef_lane[0, h] * weight, 0.0)
        side_flux += jnp.where(used, flux, 0.0)
    gap = tiles * half
    while gap >= 2 * tiles:
        side_sum = side_sum + turn(side_sum, -gap, 1)
        side_flux = side_flux + turn(side_flux, -gap, 1)
        gap //= 2

    diag, ty, tx, fy, fx = acc[1], acc[2], acc[3], acc[4], acc[5]
    edge_sum = jnp.concatenate([turn(side_sum, 127 - 2 * t, 1) for t in range(tiles)], axis=0)
    edge_flux = jnp.concatenate([turn(side_flux, 127 - 2 * t, 1) for t in range(tiles)], axis=0)
    last_row, first_row, last_lane, first_lane = rows == height - 1, rows == 0, lanes == width - 1, lanes == 0
    ty_plus, ty_minus = jnp.where(last_row, y_sum[1], ty), jnp.where(first_row, y_sum[0], turn(ty, 1, 0))
    tx_plus, tx_minus = jnp.where(last_lane, edge_sum, tx), jnp.where(first_lane, edge_sum, turn(tx, 1, 1))
    fy_plus, fy_minus = jnp.where(last_row, y_flux[1], fy), jnp.where(first_row, y_flux[0], -turn(fy, 1, 0))
    fx_plus, fx_minus = jnp.where(last_lane, edge_flux, fx), jnp.where(first_lane, edge_flux, -turn(fx, 1, 1))
    planes = [
        rhs - (fy_plus + fy_minus) - (fx_plus + fx_minus),
        diag + (ty_plus + ty_minus) + (tx_plus + tx_minus),
        ty_plus,
        tx_plus,
    ]

    last = tiles - 1

    def tile(p, t):
        return planes[p][8 * t : 8 * t + 8]

    for p in range(4):
        message[0, 8 * p : 8 * p + 8, :] = tile(p, 0)
        message[1, 8 * p : 8 * p + 8, :] = tile(p, last)
        left = jnp.zeros((8, 128), F32)
        right_side = jnp.zeros((8, 128), F32)
        for t in range(tiles):
            here = lane // 8 == t
            left = jnp.where(here, turn(tile(p, t), 8 * t, 1), left)
            right_side = jnp.where(here, turn(tile(p, t), 8 * t + 8, 1), right_side)
        message[2, 8 * p : 8 * p + 8, :] = left
        message[3, 8 * p : 8 * p + 8, :] = right_side
    for k, (t, at_end) in enumerate(((0, 0), (last, 1), (0, 1), (last, 0))):
        corner = jnp.zeros((8, 128), F32)
        for p in range(4):
            corner = jnp.where(lane // 8 == p, turn(tile(p, t), 8 * p + 8 * at_end, 1), corner)
        message[4 + k, 0:8, :] = corner
        for t in range(4):
            message[4 + k, 8 + 8 * t : 16 + 8 * t, :] = tile(k, t)
        message[k, 32:40, :] = tile(k, last)


def cells_kernel(
    h, coef, znear, ynear, xnear, yweight, xweight, order, layer_face, areal_in, state_in, right_in, pore_in,
    base_out, gain_out, areal_face,
    state, right, pore, base, gain, sems,
):
    del order
    if h == 1:
        base, gain = base_out, gain_out
    half, height, width = pore.shape
    tiles, first, pieces = height // 8, h * half, half // CHUNK
    rows = row_index((height, width))
    lanes = lane_index((height, width))
    arrivals = []
    for p in range(pieces):
        here, there = pl.ds(p * CHUNK, CHUNK), pl.ds(first + p * CHUNK, CHUNK)
        state_low = 1 if p == 0 and h == 0 else (0 if p == 0 else p * CHUNK + 2)
        state_high = (p + 1) * CHUNK + (1 if p == pieces - 1 and h == 1 else 2)
        z_low = first - 1 + state_low
        arrivals.append([
            pltpu.make_async_copy(
                state_in.at[:, pl.ds(z_low, state_high - state_low)],
                state.at[:, pl.ds(state_low, state_high - state_low)],
                sems.at[0, p],
            ),
            pltpu.make_async_copy(right_in.at[:, there], right.at[:, here], sems.at[1, p]),
            pltpu.make_async_copy(pore_in.at[there], pore.at[here], sems.at[2, p]),
        ])
    for group in arrivals:
        for copy in group:
            copy.start()
    for c in range(3):
        state[c, 0 if h == 0 else half + 1] = znear[h, c]

    def layer(i):
        z = first + i
        m = [[coef[3 * r + c, z : z + 1, :] for c in range(3)] for r in range(3)]
        k = [[coef[9 + 3 * r + c, z : z + 1, :] for c in range(3)] for r in range(3)]

        def edges_of(packed):
            return jnp.concatenate(
                [turn(packed, 127 - 2 * tiles * i - 2 * t, 1) for t in range(tiles)], axis=0
            )

        edges = edges_of(xweight[h])
        areal = [
            jnp.where(rows == height - 1, yweight[1, z : z + 1, :], areal_in[0, z]),
            jnp.where(rows == 0, yweight[0, z : z + 1, :], areal_in[1, z]),
            jnp.where(lanes == width - 1, edges, areal_in[2, z]),
            jnp.where(lanes == 0, edges, areal_in[3, z]),
        ]
        for d in range(4):
            areal_face[d, z] = areal[d]
        weights = [layer_face[z + 1], layer_face[z]] + areal
        total = weights[0] + weights[1] + weights[2] + weights[3] + weights[4] + weights[5]
        cells, flux = [], []
        for c in range(3):
            u = state[c, i + 1]
            edges = edges_of(xnear[c, h])
            near = (
                state[c, i + 2],
                state[c, i],
                jnp.where(rows == height - 1, ynear[1, c, z : z + 1, :], turn(u, -1, 0)),
                jnp.where(rows == 0, ynear[0, c, z : z + 1, :], turn(u, 1, 0)),
                jnp.where(lanes == width - 1, edges, turn(u, -1, 1)),
                jnp.where(lanes == 0, edges, turn(u, 1, 1)),
            )
            moved = weights[0] * (u - near[0])
            for w, n in zip(weights[1:], near[1:]):
                moved = moved + w * (u - n)
            cells.append(u)
            flux.append(moved)
        v = pore[i].astype(F32)
        residual = [
            right[r, i]
            - v * (m[r][0] * cells[0] + m[r][1] * cells[1] + m[r][2] * cells[2])
            - (k[r][0] * flux[0] + k[r][1] * flux[1] + k[r][2] * flux[2])
            for r in range(3)
        ]
        entries = [[v * m[r][c] + total * k[r][c] for c in range(3)] for r in range(3)]

        def cofactor(r, c):
            r1, r2, c1, c2 = (r + 1) % 3, (r + 2) % 3, (c + 1) % 3, (c + 2) % 3
            return entries[r1][c1] * entries[r2][c2] - entries[r1][c2] * entries[r2][c1]

        factors = [[cofactor(r, c) for c in range(3)] for r in range(3)]
        determinant = (
            entries[0][0] * factors[0][0] + entries[0][1] * factors[0][1] + entries[0][2] * factors[0][2]
        )
        scale = inverse(determinant)
        for r in range(3):
            base[r, i] = cells[r] + scale * (
                factors[0][r] * residual[0] + factors[1][r] * residual[1] + factors[2][r] * residual[2]
            )
            gain[r, i] = scale * (factors[0][r] * k[0][0] + factors[1][r] * k[1][0] + factors[2][r] * k[2][0])

    departures = []
    for p in range(pieces):
        for copy in arrivals[p]:
            copy.wait()
        for i in range(p * CHUNK, (p + 1) * CHUNK):
            layer(i)
        if h == 1:
            continue
        here = pl.ds(p * CHUNK, CHUNK)
        for n, (source, target) in enumerate(((base, base_out), (gain, gain_out))):
            copy = pltpu.make_async_copy(source.at[:, here], target.at[:, here], sems.at[3 + n, p])
            copy.start()
            departures.append(copy)
    for copy in departures:
        copy.wait()


def total_kernel(parts, total, strip):
    result = parts[0]
    for i in range(1, parts.shape[0]):
        result = result + parts[i]
    total[...] = result
    strip[...] = result[: strip.shape[0]]


def merge_kernel(strip, share, copies):
    at_corner = lax.axis_index("gz") >= 4
    for t in range(5):
        cells = slice(8 * t, 8 * t + 8)
        if t == 0:
            merged = strip[cells]
        elif t == 4:
            merged = share[cells]
        else:
            merged = jnp.where(at_corner, share[cells], strip[cells])
        for k in range(copies.shape[0]):
            copies[k, cells, :] = merged


def sweep_kernel(
    shares, layer_face, areal_face, base0, gain0, base1, gain1, new_state, correction,
    base, gain, result, plane, sems,
):
    _, depth, height, width = areal_face.shape
    tiles, half = height // 8, depth // 2
    lane = lane_index((8, 128))
    arrivals = []
    for p in range(half // CHUNK):
        here = pl.ds(p * CHUNK, CHUNK)
        arrivals.append([
            pltpu.make_async_copy(base0.at[:, here], base.at[:, here], sems.at[1, p]),
            pltpu.make_async_copy(gain0.at[:, here], gain.at[:, here], sems.at[2, p]),
        ])
    for group in arrivals:
        for copy in group:
            copy.start()

    def tile(k, t):
        return shares[k, 8 * t : 8 * t + 8, :]

    def side(right, right_at, left, left_at):
        right, left = turn(right, -right_at, 1), turn(left, width - 8 - left_at, 1)
        return jnp.where(lane < 8, right, jnp.where(lane >= width - 8, left, 0.0))

    planes = []
    for p in range(4):
        main = [tile(1, p)] + [tile(4 + p, 1 + t) for t in range(tiles - 1)] + [tile(p, 4), tile(0, p)]
        edge = [side(tile(7, 0), 8 * p, tile(5, 0), 8 * p)]
        for t in range(tiles):
            edge.append(side(tile(2, p), 8 * t, tile(3, p), 8 * t))
        edge.append(side(tile(4, 0), 8 * p, tile(6, 0), 8 * p))
        planes.append(
            jnp.concatenate([jnp.concatenate(main, axis=0), jnp.concatenate(edge, axis=0)], axis=1)
        )
    filled = planes[1] > 0.0
    scale = jnp.where(filled, RELAX / jnp.where(filled, planes[1], 1.0), 0.0)
    source = scale * planes[0]
    south = scale * planes[2]
    north = scale * turn(planes[2], 1, 0)
    east = scale * planes[3]
    west = scale * turn(planes[3], 1, 1)

    def around(field):
        return turn(field, -1, 0), turn(field, 1, 0), turn(field, -1, 1), turn(field, 1, 1)

    field = source
    for _ in range(SWEEPS - 1):
        s, n, e, w = around(field)
        field = ((1.0 - RELAX) * field + source) + (south * s + north * n) + (east * e + west * w)
    near = around(field)
    own = field[8 : 8 + height, 0:width]
    near = [n[8 : 8 + height, 0:width] for n in near]
    plane[...] = own
    copies = [pltpu.make_async_copy(plane, correction, sems.at[0, depth // CHUNK])]
    copies[0].start()

    for first in [*range(half, depth, CHUNK), *range(0, half, CHUNK)]:
        for copy in arrivals[first // CHUNK] if first < half else ():
            copy.wait()

        for z in range(first, first + CHUNK):
            push = (layer_face[z] + layer_face[z + 1]) * own
            for d in range(4):
                push = push + areal_face[d, z] * near[d]
            for r in range(3):
                if first < half:
                    result[r, z] = base[r, z] + gain[r, z] * push
                else:
                    result[r, z] = base1[r, z - half] + gain1[r, z - half] * push
        copy = pltpu.make_async_copy(
            result.at[:, pl.ds(first, CHUNK)], new_state.at[:, pl.ds(first, CHUNK)], sems.at[0, first // CHUNK]
        )
        copy.start()
        copies.append(copy)
    for copy in copies:
        copy.wait()


def call(kernel, out_shape, in_specs, out_specs, scratch=(), flops=0, moved=0, aliases=None):
    return pl.pallas_call(
        kernel,
        out_shape=out_shape,
        in_specs=in_specs,
        out_specs=out_specs,
        scratch_shapes=list(scratch),
        compiler_params=PARAMS,
        input_output_aliases=aliases or {},
        cost_estimate=pl.CostEstimate(flops=flops, bytes_accessed=moved, transcendentals=0) if flops else None,
    )


def per_device(state, right_side, permeability, pore_volume, facies, storage_table, coupling_table):
    _, depth, height, width = state.shape
    columns = lax.axis_size("gz")
    row_of, rows = lax.axis_size("gx"), lax.axis_size("gy")
    block = (depth, height, width)
    bf16 = jnp.bfloat16
    storage_table, coupling_table = storage_table.transpose(1, 0, 2), coupling_table.transpose(1, 0, 2)

    state_v, perm_v, zface0, zface1, yface0, yface1, xpack = call(
        faces_kernel,
        [shape_of(3, *block), shape_of(*block)]
        + [shape_of(4, height, width)] * 2 + [shape_of(4, depth, width)] * 2 + [shape_of(4, 2, 8, 128)],
        hbm(2),
        vmem(7),
        [pltpu.VMEM(block, bf16), pltpu.SemaphoreType.DMA((1 + depth // CHUNK,))],
    )(*in_hbm(state, permeability))

    def exchange(face, axis, odd):
        pairs = []
        for i in range(odd, lax.axis_size(axis) - 1, 2):
            pairs += [(i, i + 1), (i + 1, i)]
        return lax.ppermute(face, axis, pairs)

    received = []
    for axis, first, second in (("gz", zface0, zface1), ("gy", yface0, yface1), ("gx", xpack, xpack)):
        received += [exchange(first, axis, 0), exchange(second, axis, 1)]

    coef, coef_lane, layer_face, areal_face, acc = call(
        inner_kernel,
        [
            shape_of(18, depth, 128),
            shape_of(3, 2, 8, 128),
            shape_of(depth + 1, height, width),
            shape_of(4, *block),
            shape_of(6, height, width),
        ],
        vmem(2) + hbm(5),
        vmem(5),
        [
            pltpu.VMEM(block, F32),
            pltpu.VMEM(block, bf16),
            pltpu.SMEM(facies.shape, jnp.int32),
            pltpu.SMEM(storage_table.shape, F32),
            pltpu.SMEM(coupling_table.shape, F32),
            pltpu.SemaphoreType.DMA((5,)),
        ],
        flops=2 * 10**9,
        moved=2 * 10**6,
    )(state_v, perm_v, *in_hbm(right_side, pore_volume, facies, storage_table, coupling_table))

    layer_face, znear, ynear, xnear, yweight, xweight, message = call(
        outer_kernel,
        [
            shape_of(depth + 1, height, width),
            shape_of(2, 3, height, width),
            shape_of(2, 3, depth, width),
            shape_of(3, 2, 8, 128),
            shape_of(2, depth, width),
            shape_of(2, 8, 128),
            shape_of(columns, 40, 128),
        ],
        vmem(15),
        vmem(7),
        aliases={14: 0},
    )(coef, coef_lane, acc, zface0, zface1, yface0, yface1, xpack, *received, layer_face)

    def cells(h, order, areal_face):
        def kernel(*refs):
            cells_kernel(h, *refs)

        layers = depth // 2
        half = (layers, height, width)
        kept = [shape_of(3, *half)] * 2 if h == 1 else [pltpu.HBM((3, *half), F32)] * 2
        return call(
            kernel,
            kept + [shape_of(4, *block)],
            vmem(9) + hbm(3),
            (vmem(2) if h == 1 else hbm(2)) + vmem(1),
            [
                pltpu.VMEM((3, layers + 2, height, width), F32),
                pltpu.VMEM((3, *half), F32),
                pltpu.VMEM(half, bf16),
                pltpu.VMEM((3, *half), F32),
                pltpu.VMEM((3, *half), F32),
                pltpu.SemaphoreType.DMA((5, layers // CHUNK)),
            ],
            flops=3 * 10**9,
            moved=3 * 10**6,
            aliases={8: 2},
        )(
            coef, znear, ynear, xnear, yweight, xweight, order, layer_face, areal_face,
            *in_hbm(state, right_side, pore_volume),
        )

    parts = lax.all_to_all(message, "gz", 0, 0)
    share, strip = call(total_kernel, [shape_of(40, 128), shape_of(32, 128)], vmem(1), vmem(2))(parts)
    pairs = []
    for x in range(row_of):
        for y in range(rows):
            for k, (dy, dx) in enumerate(DIRECTIONS):
                if 0 <= x + dx < row_of and 0 <= y + dy < rows:
                    pairs.append(
                        ((x * rows + y) * columns + k, ((x + dx) * rows + y + dy) * columns + k)
                    )
    strip = lax.ppermute(strip, ("gx", "gy", "gz"), pairs)
    base0, gain0, areal_face = cells(0, share, areal_face)
    copies = call(merge_kernel, shape_of(columns, 40, 128), vmem(2), vmem(1)[0])(strip, share)
    base1, gain1, areal_face = cells(1, strip, areal_face)
    shares = lax.all_to_all(copies, "gz", 0, 0)

    new_state, correction = call(
        sweep_kernel,
        [pltpu.HBM((3, *block), F32), pltpu.HBM((height, width), F32)],
        vmem(3) + hbm(2) + vmem(2),
        hbm(2),
        [
            pltpu.VMEM((3, depth // 2, height, width), F32),
            pltpu.VMEM((3, depth // 2, height, width), F32),
            pltpu.VMEM((3, *block), F32),
            pltpu.VMEM((height, width), F32),
            pltpu.SemaphoreType.DMA((3, depth // CHUNK + 1)),
        ],
    )(shares, layer_face, areal_face, *in_hbm(base0, gain0), base1, gain1)
    return (new_state, correction)


def solution(mesh):
    return jax.shard_map(
        per_device,
        mesh=mesh,
        in_specs=(
            P(None, "gz", "gy", "gx"),
            P(None, "gz", "gy", "gx"),
            P("gz", "gy", "gx"),
            P("gz", "gy", "gx"),
            P("gz"),
            P(),
            P(),
        ),
        out_specs=(P(None, "gz", "gy", "gx"), P("gy", "gx")),
        check_vma=False,
    )
```

```python
import jax
import jax.numpy as jnp
from jax import lax
from jax.experimental import pallas as pl
from jax.experimental.pallas import tpu as pltpu
from jax.sharding import PartitionSpec as P

SWEEPS = 8
RELAX = 0.8
DIRECTIONS = ((-1, 0), (1, 0), (0, -1), (0, 1), (-1, -1), (1, 1), (-1, 1), (1, -1))
F32 = jnp.float32
PARAMS = pltpu.CompilerParams(vmem_limit_bytes=16 * 2**20)
CHUNK = 4


def vmem(count):
    return [pl.BlockSpec(memory_space=pltpu.VMEM)] * count


def hbm(count):
    return [pl.BlockSpec(memory_space=pltpu.HBM)] * count


def shape_of(*dims):
    return jax.ShapeDtypeStruct(dims, F32)


def in_hbm(*arrays):
    return [pltpu.with_memory_space_constraint(a, pltpu.HBM) for a in arrays]


def lane_index(shape):
    return lax.broadcasted_iota(jnp.int32, shape, len(shape) - 1)


def row_index(shape):
    return lax.broadcasted_iota(jnp.int32, shape, len(shape) - 2)


def turn(block, shift, axis):
    shift = shift % block.shape[axis]
    return pltpu.roll(block, shift, axis) if shift else block


def inverse(value):
    guess = pl.reciprocal(value, approx=True)
    return guess * (2.0 - value * guess)


def mean_weight(a, b):
    return (a + a) * b * inverse(a + b)


def parity(axis):
    return lax.rem(lax.axis_index(axis), 2)


def faces_kernel(state, perm, state_v, perm_v, zface0, zface1, yface0, yface1, xpack, perm_half, sems):
    depth, height, width = perm.shape
    tiles, half = height // 8, depth // 2
    fetch = pltpu.make_async_copy(perm, perm_half, sems.at[0])
    pieces = [
        pltpu.make_async_copy(state.at[:, pl.ds(z, CHUNK)], state_v.at[:, pl.ds(z, CHUNK)], sems.at[1 + z // CHUNK])
        for z in range(0, depth, CHUNK)
    ]
    fetch.start()
    for piece in pieces:
        piece.start()
    z_high, y_high = parity("gz"), parity("gy")
    lanes = lane_index((8, 128))
    pairs = lanes // 2
    packed = [[jnp.full((8, 128), 1.0 if c == 3 else 0.0, F32) for _ in range(2)] for c in range(4)]

    def pack(c, z, cells):
        low, high = cells[0:1], cells[height - 1 : height]
        yface0[c, z : z + 1, :] = jnp.where(y_high == 0, high, low)
        yface1[c, z : z + 1, :] = jnp.where(y_high == 0, low, high)
        for t in range(tiles):
            i = (z % half) * tiles + t
            turned = turn(cells[8 * t : 8 * t + 8], 2 * i + 1, 1)
            packed[c][z // half] = jnp.where(pairs == i, turned, packed[c][z // half])

    fetch.wait()
    for z in range(depth):
        perm_v[z] = perm_half[z].astype(F32)
        pack(3, z, perm_half[z].astype(F32))
    for z in range(depth):
        if z % CHUNK == 0:
            pieces[z // CHUNK].wait()
        for c in range(3):
            pack(c, z, state_v[c, z])
    for c in range(4):
        for h in range(2):
            xpack[c, h] = packed[c][h]
        low, high = (state_v[c, z] if c < 3 else perm_v[z] for z in (0, depth - 1))
        zface0[c] = jnp.where(z_high == 0, high, low)
        zface1[c] = jnp.where(z_high == 0, low, high)


def inner_kernel(
    state, perm, right, pore, facies, storage_table, coupling_table,
    coef, coef_lane, layer_face, areal_face, acc,
    right_v, pore_v, facies_s, storage_s, coupling_s, sems,
):
    depth, height, width = perm.shape
    tiles, half = height // 8, depth // 2
    copies = [
        pltpu.make_async_copy(source, target, sems.at[n])
        for n, (source, target) in enumerate(
            (
                (facies, facies_s),
                (storage_table, storage_s),
                (coupling_table, coupling_s),
                (pore, pore_v),
                (right.at[0], right_v),
            )
        )
    ]
    for copy in copies:
        copy.start()
    rows = row_index((height, width))
    lanes = lane_index((height, width))
    for z in range(depth):
        q = perm[z]
        if z < depth - 1:
            layer_face[z + 1] = mean_weight(q, perm[z + 1])
        ty = jnp.where(rows == height - 1, 0.0, mean_weight(q, turn(q, -1, 0)))
        tx = jnp.where(lanes == width - 1, 0.0, mean_weight(q, turn(q, -1, 1)))
        areal_face[0, z] = ty
        areal_face[1, z] = tx

    for copy in copies[:3]:
        copy.wait()
    lane, row = lane_index((8, 128)), row_index((depth, 128))
    fids = jnp.zeros((depth, 128), jnp.int32)
    fids_lane = [jnp.zeros((8, 128), jnp.int32) for _ in range(2)]
    for z in range(depth):
        fid = facies_s[z]
        fids = jnp.where(row == z, fid, fids)
        fids_lane[z // half] = jnp.where(lane >= 2 * tiles * (z % half), fid, fids_lane[z // half])
    kinds = storage_table.shape[1]
    for which, table in enumerate((storage_s, coupling_s)):
        for k in range(9):
            rows_of = jnp.zeros((depth, 128), F32)
            for f in range(kinds):
                rows_of = jnp.where(fids == f, table[k // 3, f, k % 3], rows_of)
            coef[9 * which + k] = rows_of
    for k in range(3):
        for h in range(2):
            lane_of = jnp.zeros((8, 128), F32)
            for f in range(kinds):
                lane_of = jnp.where(fids_lane[h] == f, coupling_s[0, f, k], lane_of)
            coef_lane[k, h] = lane_of
    for copy in copies[3:]:
        copy.wait()

    for a in range(6):
        acc[a] = jnp.zeros((height, width), F32)
    for z in range(depth):
        u = [state[c, z] for c in range(3)]
        m0 = [coef[c, z : z + 1, :] for c in range(3)]
        k0 = [coef[9 + c, z : z + 1, :] for c in range(3)]
        v = pore_v[z].astype(F32)
        part = right_v[z] - v * (m0[0] * u[0] + m0[1] * u[1] + m0[2] * u[2])
        if z < depth - 1:
            step = [k0[c] - coef[9 + c, z + 1 : z + 2, :] for c in range(3)]
            jump = [u[c] - state[c, z + 1] for c in range(3)]
            part = part - layer_face[z + 1] * (step[0] * jump[0] + step[1] * jump[1] + step[2] * jump[2])
        acc[0] += part
        acc[1] += m0[0] * v
        w = k0[0] * u[0] + k0[1] * u[1] + k0[2] * u[2]
        ty, tx = areal_face[0, z], areal_face[1, z]
        acc[2] += k0[0] * ty
        acc[3] += k0[0] * tx
        acc[4] += ty * (w - turn(w, -1, 0))
        acc[5] += tx * (w - turn(w, -1, 1))


def outer_kernel(
    coef, coef_lane, acc, zface0, zface1, yface0, yface1, xpack, z0, z1, y0, y1, x0, x1, layer_in,
    layer_face, znear, ynear, xnear, yweight, xweight, message,
):
    del layer_in
    _, height, width = zface0.shape
    depth = yface0.shape[1]
    tiles, half = height // 8, depth // 2
    rows = row_index((height, width))
    lanes = lane_index((height, width))
    lane = lane_index((8, 128))
    z_high, y_high, x_high = parity("gz"), parity("gy"), parity("gx")

    def received(high, first, second, c):
        a, b = first[c], second[c]
        return jnp.where(high == 0, b, a), jnp.where(high == 0, a, b)

    def flat(own, near, k0):
        weight = mean_weight(own[3], near[3])
        jump = k0[0] * (own[0] - near[0]) + k0[1] * (own[1] - near[1]) + k0[2] * (own[2] - near[2])
        return weight, weight * jump

    zown = [received(z_high, zface0, zface1, c) for c in range(4)]
    yown = [received(y_high, yface0, yface1, c) for c in range(4)]
    znears = [received(z_high, z0, z1, c) for c in range(4)]
    ynears = [received(y_high, y0, y1, c) for c in range(4)]
    for c in range(3):
        for e in range(2):
            znear[e, c] = znears[c][e]
            ynear[e, c] = ynears[c][e]
    rhs = acc[0]
    for e, z in ((0, 0), (1, depth - 1)):
        weight, flux = flat(
            [zown[c][e] for c in range(4)],
            [znears[c][e] for c in range(4)],
            [coef[9 + c, z : z + 1, :] for c in range(3)],
        )
        layer_face[z + e] = weight
        rhs = rhs - flux
    k_rows = [coef[9 + k] for k in range(3)]
    y_sum, y_flux = [], []
    for e in range(2):
        weight, flux = flat([yown[c][e] for c in range(4)], [ynears[c][e] for c in range(4)], k_rows)
        yweight[e] = weight
        y_sum.append(jnp.sum(k_rows[0] * weight, axis=0, keepdims=True))
        y_flux.append(jnp.sum(flux, axis=0, keepdims=True))
    side_sum, side_flux = 0.0, 0.0
    for h in range(2):
        near = []
        for c in range(4):
            west, east = jnp.where(x_high == 0, x1[c, h], x0[c, h]), jnp.where(x_high == 0, x0[c, h], x1[c, h])
            near.append(jnp.where(lane % 2 == 0, turn(east, -1, 1), turn(west, 1, 1)))
        for c in range(3):
            xnear[c, h] = near[c]
        weight, flux = flat([xpack[c, h] for c in range(4)], near, [coef_lane[k, h] for k in range(3)])
        used = lane < 2 * tiles * half
        xweight[h] = weight
        side_sum += jnp.where(used, coef_lane[0, h] * weight, 0.0)
        side_flux += jnp.where(used, flux, 0.0)
    gap = tiles * half
    while gap >= 2 * tiles:
        side_sum = side_sum + turn(side_sum, -gap, 1)
        side_flux = side_flux + turn(side_flux, -gap, 1)
        gap //= 2

    diag, ty, tx, fy, fx = acc[1], acc[2], acc[3], acc[4], acc[5]
    edge_sum = jnp.concatenate([turn(side_sum, 127 - 2 * t, 1) for t in range(tiles)], axis=0)
    edge_flux = jnp.concatenate([turn(side_flux, 127 - 2 * t, 1) for t in range(tiles)], axis=0)
    last_row, first_row, last_lane, first_lane = rows == height - 1, rows == 0, lanes == width - 1, lanes == 0
    ty_plus, ty_minus = jnp.where(last_row, y_sum[1], ty), jnp.where(first_row, y_sum[0], turn(ty, 1, 0))
    tx_plus, tx_minus = jnp.where(last_lane, edge_sum, tx), jnp.where(first_lane, edge_sum, turn(tx, 1, 1))
    fy_plus, fy_minus = jnp.where(last_row, y_flux[1], fy), jnp.where(first_row, y_flux[0], -turn(fy, 1, 0))
    fx_plus, fx_minus = jnp.where(last_lane, edge_flux, fx), jnp.where(first_lane, edge_flux, -turn(fx, 1, 1))
    planes = [
        rhs - (fy_plus + fy_minus) - (fx_plus + fx_minus),
        diag + (ty_plus + ty_minus) + (tx_plus + tx_minus),
        ty_plus,
        tx_plus,
    ]

    last = tiles - 1

    def tile(p, t):
        return planes[p][8 * t : 8 * t + 8]

    for p in range(4):
        message[0, 8 * p : 8 * p + 8, :] = tile(p, 0)
        message[1, 8 * p : 8 * p + 8, :] = tile(p, last)
        left = jnp.zeros((8, 128), F32)
        right_side = jnp.zeros((8, 128), F32)
        for t in range(tiles):
            here = lane // 8 == t
            left = jnp.where(here, turn(tile(p, t), 8 * t, 1), left)
            right_side = jnp.where(here, turn(tile(p, t), 8 * t + 8, 1), right_side)
        message[2, 8 * p : 8 * p + 8, :] = left
        message[3, 8 * p : 8 * p + 8, :] = right_side
    for k, (t, at_end) in enumerate(((0, 0), (last, 1), (0, 1), (last, 0))):
        corner = jnp.zeros((8, 128), F32)
        for p in range(4):
            corner = jnp.where(lane // 8 == p, turn(tile(p, t), 8 * p + 8 * at_end, 1), corner)
        message[4 + k, 0:8, :] = corner
        for t in range(4):
            message[4 + k, 8 + 8 * t : 16 + 8 * t, :] = tile(k, t)
        message[k, 32:40, :] = tile(k, last)


def areal_weights(z, areal_face, yweight, xweight):
    _, depth, height, width = areal_face.shape
    tiles, half = height // 8, depth // 2
    rows = row_index((height, width))
    lanes = lane_index((height, width))
    edges = edges_of(xweight[z // half], z % half, tiles)
    ty, tx = areal_face[0, z], areal_face[1, z]
    return (
        jnp.where(rows == height - 1, yweight[1, z : z + 1, :], ty),
        jnp.where(rows == 0, yweight[0, z : z + 1, :], turn(ty, 1, 0)),
        jnp.where(lanes == width - 1, edges, tx),
        jnp.where(lanes == 0, edges, turn(tx, 1, 1)),
    )


def edges_of(packed, i, tiles):
    return jnp.concatenate([turn(packed, 127 - 2 * tiles * i - 2 * t, 1) for t in range(tiles)], axis=0)


def cells_kernel(
    coef, znear, ynear, xnear, yweight, xweight, order, layer_face, areal_face, state, right_in, pore_in,
    base, gain,
    right, pore, sems,
):
    del order
    depth, height, width = pore.shape
    tiles, half = height // 8, depth // 2
    rows = row_index((height, width))
    lanes = lane_index((height, width))
    arrivals = []
    for p in range(depth // CHUNK):
        here = pl.ds(p * CHUNK, CHUNK)
        arrivals.append([
            pltpu.make_async_copy(right_in.at[:, here], right.at[:, here], sems.at[0, p]),
            pltpu.make_async_copy(pore_in.at[here], pore.at[here], sems.at[1, p]),
        ])
    for group in arrivals:
        for copy in group:
            copy.start()

    def layer(z):
        m = [[coef[3 * r + c, z : z + 1, :] for c in range(3)] for r in range(3)]
        k = [[coef[9 + 3 * r + c, z : z + 1, :] for c in range(3)] for r in range(3)]
        weights = [layer_face[z + 1], layer_face[z], *areal_weights(z, areal_face, yweight, xweight)]
        total = weights[0] + weights[1] + weights[2] + weights[3] + weights[4] + weights[5]
        cells, flux = [], []
        for c in range(3):
            u = state[c, z]
            edges = edges_of(xnear[c, z // half], z % half, tiles)
            near = (
                znear[1, c] if z == depth - 1 else state[c, z + 1],
                znear[0, c] if z == 0 else state[c, z - 1],
                jnp.where(rows == height - 1, ynear[1, c, z : z + 1, :], turn(u, -1, 0)),
                jnp.where(rows == 0, ynear[0, c, z : z + 1, :], turn(u, 1, 0)),
                jnp.where(lanes == width - 1, edges, turn(u, -1, 1)),
                jnp.where(lanes == 0, edges, turn(u, 1, 1)),
            )
            moved = weights[0] * (u - near[0])
            for w, n in zip(weights[1:], near[1:]):
                moved = moved + w * (u - n)
            cells.append(u)
            flux.append(moved)
        v = pore[z].astype(F32)
        residual = [
            right[r, z]
            - v * (m[r][0] * cells[0] + m[r][1] * cells[1] + m[r][2] * cells[2])
            - (k[r][0] * flux[0] + k[r][1] * flux[1] + k[r][2] * flux[2])
            for r in range(3)
        ]
        entries = [[v * m[r][c] + total * k[r][c] for c in range(3)] for r in range(3)]

        def cofactor(r, c):
            r1, r2, c1, c2 = (r + 1) % 3, (r + 2) % 3, (c + 1) % 3, (c + 2) % 3
            return entries[r1][c1] * entries[r2][c2] - entries[r1][c2] * entries[r2][c1]

        factors = [[cofactor(r, c) for c in range(3)] for r in range(3)]
        determinant = (
            entries[0][0] * factors[0][0] + entries[0][1] * factors[0][1] + entries[0][2] * factors[0][2]
        )
        scale = inverse(determinant)
        for r in range(3):
            base[r, z] = cells[r] + scale * (
                factors[0][r] * residual[0] + factors[1][r] * residual[1] + factors[2][r] * residual[2]
            )
            gain[r, z] = scale * (factors[0][r] * k[0][0] + factors[1][r] * k[1][0] + factors[2][r] * k[2][0])

    for z in range(depth):
        if z % CHUNK == 0:
            for copy in arrivals[z // CHUNK]:
                copy.wait()
        layer(z)


def total_kernel(parts, total, strip):
    result = parts[0]
    for i in range(1, parts.shape[0]):
        result = result + parts[i]
    total[...] = result
    strip[...] = result[: strip.shape[0]]


def merge_kernel(strip, share, order, copies):
    del order
    at_corner = lax.axis_index("gz") >= 4
    for t in range(5):
        cells = slice(8 * t, 8 * t + 8)
        if t == 0:
            merged = strip[cells]
        elif t == 4:
            merged = share[cells]
        else:
            merged = jnp.where(at_corner, share[cells], strip[cells])
        for k in range(copies.shape[0]):
            copies[k, cells, :] = merged


def sweep_kernel(
    shares, layer_face, areal_face, yweight, xweight, base, gain, new_state, correction,
    result, plane, sems,
):
    _, depth, height, width = areal_face.shape
    tiles = height // 8
    lane = lane_index((8, 128))

    def tile(k, t):
        return shares[k, 8 * t : 8 * t + 8, :]

    def side(right, right_at, left, left_at):
        right, left = turn(right, -right_at, 1), turn(left, width - 8 - left_at, 1)
        return jnp.where(lane < 8, right, jnp.where(lane >= width - 8, left, 0.0))

    planes = []
    for p in range(4):
        main = [tile(1, p)] + [tile(4 + p, 1 + t) for t in range(tiles - 1)] + [tile(p, 4), tile(0, p)]
        edge = [side(tile(7, 0), 8 * p, tile(5, 0), 8 * p)]
        for t in range(tiles):
            edge.append(side(tile(2, p), 8 * t, tile(3, p), 8 * t))
        edge.append(side(tile(4, 0), 8 * p, tile(6, 0), 8 * p))
        planes.append(
            jnp.concatenate([jnp.concatenate(main, axis=0), jnp.concatenate(edge, axis=0)], axis=1)
        )
    filled = planes[1] > 0.0
    scale = jnp.where(filled, RELAX / jnp.where(filled, planes[1], 1.0), 0.0)
    source = scale * planes[0]
    south = scale * planes[2]
    north = scale * turn(planes[2], 1, 0)
    east = scale * planes[3]
    west = scale * turn(planes[3], 1, 1)

    def around(field):
        return turn(field, -1, 0), turn(field, 1, 0), turn(field, -1, 1), turn(field, 1, 1)

    field = source
    for _ in range(SWEEPS - 1):
        s, n, e, w = around(field)
        field = ((1.0 - RELAX) * field + source) + (south * s + north * n) + (east * e + west * w)
    near = around(field)
    own = field[8 : 8 + height, 0:width]
    near = [n[8 : 8 + height, 0:width] for n in near]
    plane[...] = own
    copies = [pltpu.make_async_copy(plane, correction, sems.at[depth // CHUNK])]
    copies[0].start()

    for first in range(0, depth, CHUNK):
        for z in range(first, first + CHUNK):
            push = (layer_face[z] + layer_face[z + 1]) * own
            for weight, field in zip(areal_weights(z, areal_face, yweight, xweight), near):
                push = push + weight * field
            for r in range(3):
                result[r, z] = base[r, z] + gain[r, z] * push
        copy = pltpu.make_async_copy(
            result.at[:, pl.ds(first, CHUNK)], new_state.at[:, pl.ds(first, CHUNK)], sems.at[first // CHUNK]
        )
        copy.start()
        copies.append(copy)
    for copy in copies:
        copy.wait()


def call(kernel, out_shape, in_specs, out_specs, scratch=(), flops=0, moved=0, aliases=None):
    return pl.pallas_call(
        kernel,
        out_shape=out_shape,
        in_specs=in_specs,
        out_specs=out_specs,
        scratch_shapes=list(scratch),
        compiler_params=PARAMS,
        input_output_aliases=aliases or {},
        cost_estimate=pl.CostEstimate(flops=flops, bytes_accessed=moved, transcendentals=0) if flops else None,
    )


def per_device(state, right_side, permeability, pore_volume, facies, storage_table, coupling_table):
    _, depth, height, width = state.shape
    columns = lax.axis_size("gz")
    row_of, rows = lax.axis_size("gx"), lax.axis_size("gy")
    block = (depth, height, width)
    bf16 = jnp.bfloat16
    storage_table, coupling_table = storage_table.transpose(1, 0, 2), coupling_table.transpose(1, 0, 2)

    state_v, perm_v, zface0, zface1, yface0, yface1, xpack = call(
        faces_kernel,
        [shape_of(3, *block), shape_of(*block)]
        + [shape_of(4, height, width)] * 2 + [shape_of(4, depth, width)] * 2 + [shape_of(4, 2, 8, 128)],
        hbm(2),
        vmem(7),
        [pltpu.VMEM(block, bf16), pltpu.SemaphoreType.DMA((1 + depth // CHUNK,))],
    )(*in_hbm(state, permeability))

    def exchange(face, axis, odd):
        pairs = []
        for i in range(odd, lax.axis_size(axis) - 1, 2):
            pairs += [(i, i + 1), (i + 1, i)]
        return lax.ppermute(face, axis, pairs)

    received = []
    for axis, first, second in (("gz", zface0, zface1), ("gy", yface0, yface1), ("gx", xpack, xpack)):
        received += [exchange(first, axis, 0), exchange(second, axis, 1)]

    coef, coef_lane, layer_face, areal_face, acc = call(
        inner_kernel,
        [
            shape_of(18, depth, 128),
            shape_of(3, 2, 8, 128),
            shape_of(depth + 1, height, width),
            shape_of(2, *block),
            shape_of(6, height, width),
        ],
        vmem(2) + hbm(5),
        vmem(5),
        [
            pltpu.VMEM(block, F32),
            pltpu.VMEM(block, bf16),
            pltpu.SMEM(facies.shape, jnp.int32),
            pltpu.SMEM(storage_table.shape, F32),
            pltpu.SMEM(coupling_table.shape, F32),
            pltpu.SemaphoreType.DMA((5,)),
        ],
        flops=2 * 10**9,
        moved=2 * 10**6,
    )(state_v, perm_v, *in_hbm(right_side, pore_volume, facies, storage_table, coupling_table))

    layer_face, znear, ynear, xnear, yweight, xweight, message = call(
        outer_kernel,
        [
            shape_of(depth + 1, height, width),
            shape_of(2, 3, height, width),
            shape_of(2, 3, depth, width),
            shape_of(3, 2, 8, 128),
            shape_of(2, depth, width),
            shape_of(2, 8, 128),
            shape_of(columns, 40, 128),
        ],
        vmem(15),
        vmem(7),
        aliases={14: 0},
    )(coef, coef_lane, acc, zface0, zface1, yface0, yface1, xpack, *received, layer_face)

    parts = lax.all_to_all(message, "gz", 0, 0)
    share, strip = call(total_kernel, [shape_of(40, 128), shape_of(32, 128)], vmem(1), vmem(2))(parts)
    pairs = []
    for x in range(row_of):
        for y in range(rows):
            for k, (dy, dx) in enumerate(DIRECTIONS):
                if 0 <= x + dx < row_of and 0 <= y + dy < rows:
                    pairs.append(
                        ((x * rows + y) * columns + k, ((x + dx) * rows + y + dy) * columns + k)
                    )
    strip = lax.ppermute(strip, ("gx", "gy", "gz"), pairs)
    base, gain = call(
        cells_kernel,
        [shape_of(3, *block)] * 2,
        vmem(10) + hbm(2),
        vmem(2),
        [
            pltpu.VMEM((3, *block), F32),
            pltpu.VMEM(block, bf16),
            pltpu.SemaphoreType.DMA((2, depth // CHUNK)),
        ],
        flops=4 * 10**9,
        moved=4 * 10**6,
    )(
        coef, znear, ynear, xnear, yweight, xweight, share, layer_face, areal_face, state_v,
        *in_hbm(right_side, pore_volume),
    )
    copies = call(merge_kernel, shape_of(columns, 40, 128), vmem(3), vmem(1)[0])(strip, share, base)
    shares = lax.all_to_all(copies, "gz", 0, 0)

    new_state, correction = call(
        sweep_kernel,
        [pltpu.HBM((3, *block), F32), pltpu.HBM((height, width), F32)],
        vmem(7),
        hbm(2),
        [
            pltpu.VMEM((3, *block), F32),
            pltpu.VMEM((height, width), F32),
            pltpu.SemaphoreType.DMA((depth // CHUNK + 1,)),
        ],
    )(shares, layer_face, areal_face, yweight, xweight, base, gain)
    return (new_state, correction)


def solution(mesh):
    return jax.shard_map(
        per_device,
        mesh=mesh,
        in_specs=(
            P(None, "gz", "gy", "gx"),
            P(None, "gz", "gy", "gx"),
            P("gz", "gy", "gx"),
            P("gz", "gy", "gx"),
            P("gz"),
            P(),
            P(),
        ),
        out_specs=(P(None, "gz", "gy", "gx"), P("gy", "gx")),
        check_vma=False,
    )
```

```python
import jax
import jax.numpy as jnp
from jax import lax
from jax.experimental import pallas as pl
from jax.experimental.pallas import tpu as pltpu
from jax.sharding import PartitionSpec as P

SWEEPS = 8
RELAX = 0.8
DIRECTIONS = ((-1, 0), (1, 0), (0, -1), (0, 1), (-1, -1), (1, 1), (-1, 1), (1, -1))
F32 = jnp.float32
PARAMS = pltpu.CompilerParams(vmem_limit_bytes=16 * 2**20)
CHUNK = 4
PIECE = 8


def vmem(count):
    return [pl.BlockSpec(memory_space=pltpu.VMEM)] * count


def hbm(count):
    return [pl.BlockSpec(memory_space=pltpu.HBM)] * count


def shape_of(*dims):
    return jax.ShapeDtypeStruct(dims, F32)


def in_hbm(*arrays):
    return [pltpu.with_memory_space_constraint(a, pltpu.HBM) for a in arrays]


def lane_index(shape):
    return lax.broadcasted_iota(jnp.int32, shape, len(shape) - 1)


def row_index(shape):
    return lax.broadcasted_iota(jnp.int32, shape, len(shape) - 2)


def turn(block, shift, axis):
    shift = shift % block.shape[axis]
    return pltpu.roll(block, shift, axis) if shift else block


def inverse(value):
    guess = pl.reciprocal(value, approx=True)
    return guess * (2.0 - value * guess)


def mean_weight(a, b):
    return (a + a) * b * inverse(a + b)


def parity(axis):
    return lax.rem(lax.axis_index(axis), 2)


def faces_kernel(state, perm, state_v, perm_v, zface0, zface1, yface0, yface1, xpack, perm_half, sems):
    depth, height, width = perm.shape
    tiles, half = height // 8, depth // 2
    fetch = pltpu.make_async_copy(perm, perm_half, sems.at[0])
    pieces = [
        pltpu.make_async_copy(state.at[:, pl.ds(z, PIECE)], state_v.at[:, pl.ds(z, PIECE)], sems.at[1 + z // PIECE])
        for z in range(0, depth, PIECE)
    ]
    fetch.start()
    for piece in pieces:
        piece.start()
    z_high, y_high = parity("gz"), parity("gy")
    lanes = lane_index((8, 128))
    pairs = lanes // 2
    packed = [[jnp.full((8, 128), 1.0 if c == 3 else 0.0, F32) for _ in range(2)] for c in range(4)]

    def pack(c, z, cells):
        low, high = cells[0:1], cells[height - 1 : height]
        yface0[c, z : z + 1, :] = jnp.where(y_high == 0, high, low)
        yface1[c, z : z + 1, :] = jnp.where(y_high == 0, low, high)
        for t in range(tiles):
            i = (z % half) * tiles + t
            turned = turn(cells[8 * t : 8 * t + 8], 2 * i + 1, 1)
            packed[c][z // half] = jnp.where(pairs == i, turned, packed[c][z // half])

    fetch.wait()
    for z in range(depth):
        perm_v[z] = perm_half[z].astype(F32)
        pack(3, z, perm_half[z].astype(F32))
    for z in range(depth):
        if z % PIECE == 0:
            pieces[z // PIECE].wait()
        for c in range(3):
            pack(c, z, state_v[c, z])
    for c in range(4):
        for h in range(2):
            xpack[c, h] = packed[c][h]
        low, high = (state_v[c, z] if c < 3 else perm_v[z] for z in (0, depth - 1))
        zface0[c] = jnp.where(z_high == 0, high, low)
        zface1[c] = jnp.where(z_high == 0, low, high)


def inner_kernel(
    state, perm, right, pore, facies, storage_table, coupling_table,
    coef, coef_lane, layer_face, areal_face, acc,
    right_v, pore_v, facies_s, storage_s, coupling_s, sems,
):
    depth, height, width = perm.shape
    tiles, half = height // 8, depth // 2
    copies = [
        pltpu.make_async_copy(source, target, sems.at[n])
        for n, (source, target) in enumerate(
            (
                (facies, facies_s),
                (storage_table, storage_s),
                (coupling_table, coupling_s),
                (pore, pore_v),
                (right.at[0], right_v),
            )
        )
    ]
    for copy in copies:
        copy.start()
    rows = row_index((height, width))
    lanes = lane_index((height, width))
    for z in range(depth):
        q = perm[z]
        if z < depth - 1:
            layer_face[z + 1] = mean_weight(q, perm[z + 1])
        ty = jnp.where(rows == height - 1, 0.0, mean_weight(q, turn(q, -1, 0)))
        tx = jnp.where(lanes == width - 1, 0.0, mean_weight(q, turn(q, -1, 1)))
        areal_face[0, z] = ty
        areal_face[1, z] = tx

    for copy in copies[:3]:
        copy.wait()
    lane, row = lane_index((8, 128)), row_index((depth, 128))
    fids = jnp.zeros((depth, 128), jnp.int32)
    fids_lane = [jnp.zeros((8, 128), jnp.int32) for _ in range(2)]
    for z in range(depth):
        fid = facies_s[z]
        fids = jnp.where(row == z, fid, fids)
        fids_lane[z // half] = jnp.where(lane >= 2 * tiles * (z % half), fid, fids_lane[z // half])
    kinds = storage_table.shape[1]
    for which, table in enumerate((storage_s, coupling_s)):
        for k in range(9):
            rows_of = jnp.zeros((depth, 128), F32)
            for f in range(kinds):
                rows_of = jnp.where(fids == f, table[k // 3, f, k % 3], rows_of)
            coef[9 * which + k] = rows_of
    for k in range(3):
        for h in range(2):
            lane_of = jnp.zeros((8, 128), F32)
            for f in range(kinds):
                lane_of = jnp.where(fids_lane[h] == f, coupling_s[0, f, k], lane_of)
            coef_lane[k, h] = lane_of
    for copy in copies[3:]:
        copy.wait()

    for a in range(6):
        acc[a] = jnp.zeros((height, width), F32)
    for z in range(depth):
        u = [state[c, z] for c in range(3)]
        m0 = [coef[c, z : z + 1, :] for c in range(3)]
        k0 = [coef[9 + c, z : z + 1, :] for c in range(3)]
        v = pore_v[z].astype(F32)
        part = right_v[z] - v * (m0[0] * u[0] + m0[1] * u[1] + m0[2] * u[2])
        if z < depth - 1:
            step = [k0[c] - coef[9 + c, z + 1 : z + 2, :] for c in range(3)]
            jump = [u[c] - state[c, z + 1] for c in range(3)]
            part = part - layer_face[z + 1] * (step[0] * jump[0] + step[1] * jump[1] + step[2] * jump[2])
        acc[0] += part
        acc[1] += m0[0] * v
        w = k0[0] * u[0] + k0[1] * u[1] + k0[2] * u[2]
        ty, tx = areal_face[0, z], areal_face[1, z]
        acc[2] += k0[0] * ty
        acc[3] += k0[0] * tx
        acc[4] += ty * (w - turn(w, -1, 0))
        acc[5] += tx * (w - turn(w, -1, 1))


def outer_kernel(
    coef, coef_lane, acc, zface0, zface1, yface0, yface1, xpack, z0, z1, y0, y1, x0, x1, layer_in,
    layer_face, znear, ynear, xnear, yweight, xweight, message,
):
    del layer_in
    _, height, width = zface0.shape
    depth = yface0.shape[1]
    tiles, half = height // 8, depth // 2
    rows = row_index((height, width))
    lanes = lane_index((height, width))
    lane = lane_index((8, 128))
    z_high, y_high, x_high = parity("gz"), parity("gy"), parity("gx")

    def received(high, first, second, c):
        a, b = first[c], second[c]
        return jnp.where(high == 0, b, a), jnp.where(high == 0, a, b)

    def flat(own, near, k0):
        weight = mean_weight(own[3], near[3])
        jump = k0[0] * (own[0] - near[0]) + k0[1] * (own[1] - near[1]) + k0[2] * (own[2] - near[2])
        return weight, weight * jump

    zown = [received(z_high, zface0, zface1, c) for c in range(4)]
    yown = [received(y_high, yface0, yface1, c) for c in range(4)]
    znears = [received(z_high, z0, z1, c) for c in range(4)]
    ynears = [received(y_high, y0, y1, c) for c in range(4)]
    for c in range(3):
        for e in range(2):
            znear[e, c] = znears[c][e]
            ynear[e, c] = ynears[c][e]
    rhs = acc[0]
    for e, z in ((0, 0), (1, depth - 1)):
        weight, flux = flat(
            [zown[c][e] for c in range(4)],
            [znears[c][e] for c in range(4)],
            [coef[9 + c, z : z + 1, :] for c in range(3)],
        )
        layer_face[z + e] = weight
        rhs = rhs - flux
    k_rows = [coef[9 + k] for k in range(3)]
    y_sum, y_flux = [], []
    for e in range(2):
        weight, flux = flat([yown[c][e] for c in range(4)], [ynears[c][e] for c in range(4)], k_rows)
        yweight[e] = weight
        y_sum.append(jnp.sum(k_rows[0] * weight, axis=0, keepdims=True))
        y_flux.append(jnp.sum(flux, axis=0, keepdims=True))
    side_sum, side_flux = 0.0, 0.0
    for h in range(2):
        near = []
        for c in range(4):
            west, east = jnp.where(x_high == 0, x1[c, h], x0[c, h]), jnp.where(x_high == 0, x0[c, h], x1[c, h])
            near.append(jnp.where(lane % 2 == 0, turn(east, -1, 1), turn(west, 1, 1)))
        for c in range(3):
            xnear[c, h] = near[c]
        weight, flux = flat([xpack[c, h] for c in range(4)], near, [coef_lane[k, h] for k in range(3)])
        used = lane < 2 * tiles * half
        xweight[h] = weight
        side_sum += jnp.where(used, coef_lane[0, h] * weight, 0.0)
        side_flux += jnp.where(used, flux, 0.0)
    gap = tiles * half
    while gap >= 2 * tiles:
        side_sum = side_sum + turn(side_sum, -gap, 1)
        side_flux = side_flux + turn(side_flux, -gap, 1)
        gap //= 2

    diag, ty, tx, fy, fx = acc[1], acc[2], acc[3], acc[4], acc[5]
    edge_sum = jnp.concatenate([turn(side_sum, 127 - 2 * t, 1) for t in range(tiles)], axis=0)
    edge_flux = jnp.concatenate([turn(side_flux, 127 - 2 * t, 1) for t in range(tiles)], axis=0)
    last_row, first_row, last_lane, first_lane = rows == height - 1, rows == 0, lanes == width - 1, lanes == 0
    ty_plus, ty_minus = jnp.where(last_row, y_sum[1], ty), jnp.where(first_row, y_sum[0], turn(ty, 1, 0))
    tx_plus, tx_minus = jnp.where(last_lane, edge_sum, tx), jnp.where(first_lane, edge_sum, turn(tx, 1, 1))
    fy_plus, fy_minus = jnp.where(last_row, y_flux[1], fy), jnp.where(first_row, y_flux[0], -turn(fy, 1, 0))
    fx_plus, fx_minus = jnp.where(last_lane, edge_flux, fx), jnp.where(first_lane, edge_flux, -turn(fx, 1, 1))
    planes = [
        rhs - (fy_plus + fy_minus) - (fx_plus + fx_minus),
        diag + (ty_plus + ty_minus) + (tx_plus + tx_minus),
        ty_plus,
        tx_plus,
    ]

    last = tiles - 1

    def tile(p, t):
        return planes[p][8 * t : 8 * t + 8]

    for p in range(4):
        message[0, 8 * p : 8 * p + 8, :] = tile(p, 0)
        message[1, 8 * p : 8 * p + 8, :] = tile(p, last)
        left = jnp.zeros((8, 128), F32)
        right_side = jnp.zeros((8, 128), F32)
        for t in range(tiles):
            here = lane // 8 == t
            left = jnp.where(here, turn(tile(p, t), 8 * t, 1), left)
            right_side = jnp.where(here, turn(tile(p, t), 8 * t + 8, 1), right_side)
        message[2, 8 * p : 8 * p + 8, :] = left
        message[3, 8 * p : 8 * p + 8, :] = right_side
    for k, (t, at_end) in enumerate(((0, 0), (last, 1), (0, 1), (last, 0))):
        corner = jnp.zeros((8, 128), F32)
        for p in range(4):
            corner = jnp.where(lane // 8 == p, turn(tile(p, t), 8 * p + 8 * at_end, 1), corner)
        message[4 + k, 0:8, :] = corner
        for t in range(4):
            message[4 + k, 8 + 8 * t : 16 + 8 * t, :] = tile(k, t)
        message[k, 32:40, :] = tile(k, last)


def areal_weights(z, areal_face, yweight, xweight):
    _, depth, height, width = areal_face.shape
    tiles, half = height // 8, depth // 2
    rows = row_index((height, width))
    lanes = lane_index((height, width))
    edges = edges_of(xweight[z // half], z % half, tiles)
    ty, tx = areal_face[0, z], areal_face[1, z]
    return (
        jnp.where(rows == height - 1, yweight[1, z : z + 1, :], ty),
        jnp.where(rows == 0, yweight[0, z : z + 1, :], turn(ty, 1, 0)),
        jnp.where(lanes == width - 1, edges, tx),
        jnp.where(lanes == 0, edges, turn(tx, 1, 1)),
    )


def edges_of(packed, i, tiles):
    return jnp.concatenate([turn(packed, 127 - 2 * tiles * i - 2 * t, 1) for t in range(tiles)], axis=0)


def cells_kernel(
    coef, znear, ynear, xnear, yweight, xweight, order, layer_face, areal_face, state, right_in, pore_in,
    base, gain,
    right, pore, sems,
):
    del order
    depth, height, width = pore.shape
    tiles, half = height // 8, depth // 2
    rows = row_index((height, width))
    lanes = lane_index((height, width))
    arrivals = []
    for p in range(depth // CHUNK):
        here = pl.ds(p * CHUNK, CHUNK)
        arrivals.append([
            pltpu.make_async_copy(right_in.at[:, here], right.at[:, here], sems.at[0, p]),
            pltpu.make_async_copy(pore_in.at[here], pore.at[here], sems.at[1, p]),
        ])
    for group in arrivals:
        for copy in group:
            copy.start()

    def layer(z):
        m = [[coef[3 * r + c, z : z + 1, :] for c in range(3)] for r in range(3)]
        k = [[coef[9 + 3 * r + c, z : z + 1, :] for c in range(3)] for r in range(3)]
        weights = [layer_face[z + 1], layer_face[z], *areal_weights(z, areal_face, yweight, xweight)]
        total = weights[0] + weights[1] + weights[2] + weights[3] + weights[4] + weights[5]
        nearby = []
        for c in range(3):
            u = state[c, z]
            edges = edges_of(xnear[c, z // half], z % half, tiles)
            near = (
                znear[1, c] if z == depth - 1 else state[c, z + 1],
                znear[0, c] if z == 0 else state[c, z - 1],
                jnp.where(rows == height - 1, ynear[1, c, z : z + 1, :], turn(u, -1, 0)),
                jnp.where(rows == 0, ynear[0, c, z : z + 1, :], turn(u, 1, 0)),
                jnp.where(lanes == width - 1, edges, turn(u, -1, 1)),
                jnp.where(lanes == 0, edges, turn(u, 1, 1)),
            )
            moved = weights[0] * near[0]
            for w, n in zip(weights[1:], near[1:]):
                moved = moved + w * n
            nearby.append(moved)
        v = pore[z].astype(F32)
        source = [
            right[r, z] + (k[r][0] * nearby[0] + k[r][1] * nearby[1] + k[r][2] * nearby[2]) for r in range(3)
        ]
        entries = [[v * m[r][c] + total * k[r][c] for c in range(3)] for r in range(3)]

        def cofactor(r, c):
            r1, r2, c1, c2 = (r + 1) % 3, (r + 2) % 3, (c + 1) % 3, (c + 2) % 3
            return entries[r1][c1] * entries[r2][c2] - entries[r1][c2] * entries[r2][c1]

        factors = [[cofactor(r, c) for c in range(3)] for r in range(3)]
        determinant = (
            entries[0][0] * factors[0][0] + entries[0][1] * factors[0][1] + entries[0][2] * factors[0][2]
        )
        scale = inverse(determinant)
        for r in range(3):
            base[r, z] = scale * (
                factors[0][r] * source[0] + factors[1][r] * source[1] + factors[2][r] * source[2]
            )
            gain[r, z] = scale * (factors[0][r] * k[0][0] + factors[1][r] * k[1][0] + factors[2][r] * k[2][0])

    for z in range(depth):
        if z % CHUNK == 0:
            for copy in arrivals[z // CHUNK]:
                copy.wait()
        layer(z)


def total_kernel(parts, total, strip):
    result = parts[0]
    for i in range(1, parts.shape[0]):
        result = result + parts[i]
    total[...] = result
    strip[...] = result[: strip.shape[0]]


def merge_kernel(strip, share, order, copies):
    del order
    at_corner = lax.axis_index("gz") >= 4
    for t in range(5):
        cells = slice(8 * t, 8 * t + 8)
        if t == 0:
            merged = strip[cells]
        elif t == 4:
            merged = share[cells]
        else:
            merged = jnp.where(at_corner, share[cells], strip[cells])
        for k in range(copies.shape[0]):
            copies[k, cells, :] = merged


def sweep_kernel(
    shares, layer_face, areal_face, yweight, xweight, base, gain, new_state, correction,
    result, plane, sems,
):
    _, depth, height, width = areal_face.shape
    tiles = height // 8
    lane = lane_index((8, 128))

    def tile(k, t):
        return shares[k, 8 * t : 8 * t + 8, :]

    def side(right, right_at, left, left_at):
        right, left = turn(right, -right_at, 1), turn(left, width - 8 - left_at, 1)
        return jnp.where(lane < 8, right, jnp.where(lane >= width - 8, left, 0.0))

    planes = []
    for p in range(4):
        main = [tile(1, p)] + [tile(4 + p, 1 + t) for t in range(tiles - 1)] + [tile(p, 4), tile(0, p)]
        edge = [side(tile(7, 0), 8 * p, tile(5, 0), 8 * p)]
        for t in range(tiles):
            edge.append(side(tile(2, p), 8 * t, tile(3, p), 8 * t))
        edge.append(side(tile(4, 0), 8 * p, tile(6, 0), 8 * p))
        planes.append(
            jnp.concatenate([jnp.concatenate(main, axis=0), jnp.concatenate(edge, axis=0)], axis=1)
        )
    filled = planes[1] > 0.0
    scale = jnp.where(filled, RELAX / jnp.where(filled, planes[1], 1.0), 0.0)
    source = scale * planes[0]
    south = scale * planes[2]
    north = scale * turn(planes[2], 1, 0)
    east = scale * planes[3]
    west = scale * turn(planes[3], 1, 1)

    def around(field):
        return turn(field, -1, 0), turn(field, 1, 0), turn(field, -1, 1), turn(field, 1, 1)

    field = source
    for _ in range(SWEEPS - 1):
        s, n, e, w = around(field)
        field = ((1.0 - RELAX) * field + source) + (south * s + north * n) + (east * e + west * w)
    near = around(field)
    own = field[8 : 8 + height, 0:width]
    near = [n[8 : 8 + height, 0:width] for n in near]
    plane[...] = own
    copies = [pltpu.make_async_copy(plane, correction, sems.at[depth // CHUNK])]
    copies[0].start()

    for first in range(0, depth, CHUNK):
        for z in range(first, first + CHUNK):
            push = (layer_face[z] + layer_face[z + 1]) * own
            for weight, field in zip(areal_weights(z, areal_face, yweight, xweight), near):
                push = push + weight * field
            for r in range(3):
                result[r, z] = base[r, z] + gain[r, z] * push
        copy = pltpu.make_async_copy(
            result.at[:, pl.ds(first, CHUNK)], new_state.at[:, pl.ds(first, CHUNK)], sems.at[first // CHUNK]
        )
        copy.start()
        copies.append(copy)
    for copy in copies:
        copy.wait()


def call(kernel, out_shape, in_specs, out_specs, scratch=(), flops=0, moved=0, aliases=None):
    return pl.pallas_call(
        kernel,
        out_shape=out_shape,
        in_specs=in_specs,
        out_specs=out_specs,
        scratch_shapes=list(scratch),
        compiler_params=PARAMS,
        input_output_aliases=aliases or {},
        cost_estimate=pl.CostEstimate(flops=flops, bytes_accessed=moved, transcendentals=0) if flops else None,
    )


def per_device(state, right_side, permeability, pore_volume, facies, storage_table, coupling_table):
    _, depth, height, width = state.shape
    columns = lax.axis_size("gz")
    row_of, rows = lax.axis_size("gx"), lax.axis_size("gy")
    block = (depth, height, width)
    bf16 = jnp.bfloat16
    storage_table, coupling_table = storage_table.transpose(1, 0, 2), coupling_table.transpose(1, 0, 2)

    state_v, perm_v, zface0, zface1, yface0, yface1, xpack = call(
        faces_kernel,
        [shape_of(3, *block), shape_of(*block)]
        + [shape_of(4, height, width)] * 2 + [shape_of(4, depth, width)] * 2 + [shape_of(4, 2, 8, 128)],
        hbm(2),
        vmem(7),
        [pltpu.VMEM(block, bf16), pltpu.SemaphoreType.DMA((1 + depth // PIECE,))],
    )(*in_hbm(state, permeability))

    def exchange(face, axis, odd):
        pairs = []
        for i in range(odd, lax.axis_size(axis) - 1, 2):
            pairs += [(i, i + 1), (i + 1, i)]
        return lax.ppermute(face, axis, pairs)

    received = []
    for axis, first, second in (("gz", zface0, zface1), ("gy", yface0, yface1), ("gx", xpack, xpack)):
        received += [exchange(first, axis, 0), exchange(second, axis, 1)]

    coef, coef_lane, layer_face, areal_face, acc = call(
        inner_kernel,
        [
            shape_of(18, depth, 128),
            shape_of(3, 2, 8, 128),
            shape_of(depth + 1, height, width),
            shape_of(2, *block),
            shape_of(6, height, width),
        ],
        vmem(2) + hbm(5),
        vmem(5),
        [
            pltpu.VMEM(block, F32),
            pltpu.VMEM(block, bf16),
            pltpu.SMEM(facies.shape, jnp.int32),
            pltpu.SMEM(storage_table.shape, F32),
            pltpu.SMEM(coupling_table.shape, F32),
            pltpu.SemaphoreType.DMA((5,)),
        ],
        flops=10**8,
        moved=2 * 10**6,
    )(state_v, perm_v, *in_hbm(right_side, pore_volume, facies, storage_table, coupling_table))

    layer_face, znear, ynear, xnear, yweight, xweight, message = call(
        outer_kernel,
        [
            shape_of(depth + 1, height, width),
            shape_of(2, 3, height, width),
            shape_of(2, 3, depth, width),
            shape_of(3, 2, 8, 128),
            shape_of(2, depth, width),
            shape_of(2, 8, 128),
            shape_of(columns, 40, 128),
        ],
        vmem(15),
        vmem(7),
        aliases={14: 0},
    )(coef, coef_lane, acc, zface0, zface1, yface0, yface1, xpack, *received, layer_face)

    parts = lax.all_to_all(message, "gz", 0, 0)
    share, strip = call(total_kernel, [shape_of(40, 128), shape_of(32, 128)], vmem(1), vmem(2))(parts)
    pairs = []
    for x in range(row_of):
        for y in range(rows):
            for k, (dy, dx) in enumerate(DIRECTIONS):
                if 0 <= x + dx < row_of and 0 <= y + dy < rows:
                    pairs.append(
                        ((x * rows + y) * columns + k, ((x + dx) * rows + y + dy) * columns + k)
                    )
    strip = lax.ppermute(strip, ("gx", "gy", "gz"), pairs)
    base, gain = call(
        cells_kernel,
        [shape_of(3, *block)] * 2,
        vmem(10) + hbm(2),
        vmem(2),
        [
            pltpu.VMEM((3, *block), F32),
            pltpu.VMEM(block, bf16),
            pltpu.SemaphoreType.DMA((2, depth // CHUNK)),
        ],
        flops=4 * 10**9,
        moved=4 * 10**6,
    )(
        coef, znear, ynear, xnear, yweight, xweight, share, layer_face, areal_face, state_v,
        *in_hbm(right_side, pore_volume),
    )
    copies = call(merge_kernel, shape_of(columns, 40, 128), vmem(3), vmem(1)[0])(strip, share, base)
    shares = lax.all_to_all(copies, "gz", 0, 0)

    new_state, correction = call(
        sweep_kernel,
        [pltpu.HBM((3, *block), F32), pltpu.HBM((height, width), F32)],
        vmem(7),
        hbm(2),
        [
            pltpu.VMEM((3, *block), F32),
            pltpu.VMEM((height, width), F32),
            pltpu.SemaphoreType.DMA((depth // CHUNK + 1,)),
        ],
    )(shares, layer_face, areal_face, yweight, xweight, base, gain)
    return (new_state, correction)


def solution(mesh):
    return jax.shard_map(
        per_device,
        mesh=mesh,
        in_specs=(
            P(None, "gz", "gy", "gx"),
            P(None, "gz", "gy", "gx"),
            P("gz", "gy", "gx"),
            P("gz", "gy", "gx"),
            P("gz"),
            P(),
            P(),
        ),
        out_specs=(P(None, "gz", "gy", "gx"), P("gy", "gx")),
        check_vma=False,
    )
```

```python
import jax
import jax.numpy as jnp
from jax import lax
from jax.experimental import pallas as pl
from jax.experimental.pallas import tpu as pltpu
from jax.sharding import PartitionSpec as P

SWEEPS = 8
RELAX = 0.8
DIRECTIONS = ((-1, 0), (1, 0), (0, -1), (0, 1), (-1, -1), (1, 1), (-1, 1), (1, -1))
F32 = jnp.float32
PARAMS = pltpu.CompilerParams(vmem_limit_bytes=16 * 2**20)
CHUNK = 4
PIECE = 8


def vmem(count):
    return [pl.BlockSpec(memory_space=pltpu.VMEM)] * count


def hbm(count):
    return [pl.BlockSpec(memory_space=pltpu.HBM)] * count


def shape_of(*dims):
    return jax.ShapeDtypeStruct(dims, F32)


def in_hbm(*arrays):
    return [pltpu.with_memory_space_constraint(a, pltpu.HBM) for a in arrays]


def lane_index(shape):
    return lax.broadcasted_iota(jnp.int32, shape, len(shape) - 1)


def row_index(shape):
    return lax.broadcasted_iota(jnp.int32, shape, len(shape) - 2)


def turn(block, shift, axis):
    shift = shift % block.shape[axis]
    return pltpu.roll(block, shift, axis) if shift else block


def inverse(value):
    guess = pl.reciprocal(value, approx=True)
    return guess * (2.0 - value * guess)


def mean_weight(a, b):
    return (a + a) * b * inverse(a + b)


def parity(axis):
    return lax.rem(lax.axis_index(axis), 2)


def faces_kernel(state, perm, state_v, perm_v, zface0, zface1, yface0, yface1, xpack, perm_half, sems):
    depth, height, width = perm.shape
    tiles, half = height // 8, depth // 2
    fetch = pltpu.make_async_copy(perm, perm_half, sems.at[0])
    pieces = [
        pltpu.make_async_copy(state.at[:, pl.ds(z, PIECE)], state_v.at[:, pl.ds(z, PIECE)], sems.at[1 + z // PIECE])
        for z in range(0, depth, PIECE)
    ]
    fetch.start()
    for piece in pieces:
        piece.start()
    z_high, y_high = parity("gz"), parity("gy")
    lanes = lane_index((8, 128))
    pairs = lanes // 2
    packed = [[jnp.full((8, 128), 1.0 if c == 3 else 0.0, F32) for _ in range(2)] for c in range(4)]

    def pack(c, z, cells):
        low, high = cells[0:1], cells[height - 1 : height]
        yface0[c, z : z + 1, :] = jnp.where(y_high == 0, high, low)
        yface1[c, z : z + 1, :] = jnp.where(y_high == 0, low, high)
        for t in range(tiles):
            i = (z % half) * tiles + t
            turned = turn(cells[8 * t : 8 * t + 8], 2 * i + 1, 1)
            packed[c][z // half] = jnp.where(pairs == i, turned, packed[c][z // half])

    fetch.wait()
    for z in range(depth):
        perm_v[z] = perm_half[z].astype(F32)
        pack(3, z, perm_half[z].astype(F32))
    for z in range(depth):
        if z % PIECE == 0:
            pieces[z // PIECE].wait()
        for c in range(3):
            pack(c, z, state_v[c, z])
    for c in range(4):
        for h in range(2):
            xpack[c, h] = packed[c][h]
        low, high = (state_v[c, z] if c < 3 else perm_v[z] for z in (0, depth - 1))
        zface0[c] = jnp.where(z_high == 0, high, low)
        zface1[c] = jnp.where(z_high == 0, low, high)


def inner_kernel(
    state, perm, right, pore, facies, storage_table, coupling_table,
    coef, coef_lane, layer_face, areal_face, acc,
    right_v, pore_v, facies_s, storage_s, coupling_s, sems,
):
    depth, height, width = perm.shape
    tiles, half = height // 8, depth // 2
    copies = [
        pltpu.make_async_copy(source, target, sems.at[n])
        for n, (source, target) in enumerate(
            (
                (facies, facies_s),
                (storage_table, storage_s),
                (coupling_table, coupling_s),
                (pore, pore_v),
                (right.at[0], right_v),
            )
        )
    ]
    for copy in copies:
        copy.start()
    rows = row_index((height, width))
    lanes = lane_index((height, width))
    for z in range(depth):
        q = perm[z]
        if z < depth - 1:
            layer_face[z + 1] = mean_weight(q, perm[z + 1])
        ty = jnp.where(rows == height - 1, 0.0, mean_weight(q, turn(q, -1, 0)))
        tx = jnp.where(lanes == width - 1, 0.0, mean_weight(q, turn(q, -1, 1)))
        areal_face[0, z] = ty
        areal_face[1, z] = tx

    for copy in copies[:3]:
        copy.wait()
    lane, row = lane_index((8, 128)), row_index((depth, 128))
    fids = jnp.zeros((depth, 128), jnp.int32)
    fids_lane = [jnp.zeros((8, 128), jnp.int32) for _ in range(2)]
    for z in range(depth):
        fid = facies_s[z]
        fids = jnp.where(row == z, fid, fids)
        fids_lane[z // half] = jnp.where(lane >= 2 * tiles * (z % half), fid, fids_lane[z // half])
    kinds = storage_table.shape[1]
    for which, table in enumerate((storage_s, coupling_s)):
        for k in range(9):
            rows_of = jnp.zeros((depth, 128), F32)
            for f in range(kinds):
                rows_of = jnp.where(fids == f, table[k // 3, f, k % 3], rows_of)
            coef[9 * which + k] = rows_of
    for k in range(3):
        for h in range(2):
            lane_of = jnp.zeros((8, 128), F32)
            for f in range(kinds):
                lane_of = jnp.where(fids_lane[h] == f, coupling_s[0, f, k], lane_of)
            coef_lane[k, h] = lane_of
    for copy in copies[3:]:
        copy.wait()

    for a in range(6):
        acc[a] = jnp.zeros((height, width), F32)
    for z in range(depth):
        u = [state[c, z] for c in range(3)]
        m0 = [coef[c, z : z + 1, :] for c in range(3)]
        k0 = [coef[9 + c, z : z + 1, :] for c in range(3)]
        v = pore_v[z].astype(F32)
        part = right_v[z] - v * (m0[0] * u[0] + m0[1] * u[1] + m0[2] * u[2])
        if z < depth - 1:
            step = [k0[c] - coef[9 + c, z + 1 : z + 2, :] for c in range(3)]
            jump = [u[c] - state[c, z + 1] for c in range(3)]
            part = part - layer_face[z + 1] * (step[0] * jump[0] + step[1] * jump[1] + step[2] * jump[2])
        acc[0] += part
        acc[1] += m0[0] * v
        w = k0[0] * u[0] + k0[1] * u[1] + k0[2] * u[2]
        ty, tx = areal_face[0, z], areal_face[1, z]
        acc[2] += k0[0] * ty
        acc[3] += k0[0] * tx
        acc[4] += ty * (w - turn(w, -1, 0))
        acc[5] += tx * (w - turn(w, -1, 1))


def outer_kernel(
    coef, coef_lane, acc, zface0, zface1, yface0, yface1, xpack, z0, z1, y0, y1, x0, x1, layer_in,
    layer_face, znear, ynear, xnear, yweight, xweight, message,
):
    del layer_in
    _, height, width = zface0.shape
    depth = yface0.shape[1]
    tiles, half = height // 8, depth // 2
    rows = row_index((height, width))
    lanes = lane_index((height, width))
    lane = lane_index((8, 128))
    z_high, y_high, x_high = parity("gz"), parity("gy"), parity("gx")

    def received(high, first, second, c):
        a, b = first[c], second[c]
        return jnp.where(high == 0, b, a), jnp.where(high == 0, a, b)

    def flat(own, near, k0):
        weight = mean_weight(own[3], near[3])
        jump = k0[0] * (own[0] - near[0]) + k0[1] * (own[1] - near[1]) + k0[2] * (own[2] - near[2])
        return weight, weight * jump

    zown = [received(z_high, zface0, zface1, c) for c in range(4)]
    yown = [received(y_high, yface0, yface1, c) for c in range(4)]
    znears = [received(z_high, z0, z1, c) for c in range(4)]
    ynears = [received(y_high, y0, y1, c) for c in range(4)]
    for c in range(3):
        for e in range(2):
            znear[e, c] = znears[c][e]
            ynear[e, c] = ynears[c][e]
    rhs = acc[0]
    for e, z in ((0, 0), (1, depth - 1)):
        weight, flux = flat(
            [zown[c][e] for c in range(4)],
            [znears[c][e] for c in range(4)],
            [coef[9 + c, z : z + 1, :] for c in range(3)],
        )
        layer_face[z + e] = weight
        rhs = rhs - flux
    k_rows = [coef[9 + k] for k in range(3)]
    y_sum, y_flux = [], []
    for e in range(2):
        weight, flux = flat([yown[c][e] for c in range(4)], [ynears[c][e] for c in range(4)], k_rows)
        yweight[e] = weight
        y_sum.append(jnp.sum(k_rows[0] * weight, axis=0, keepdims=True))
        y_flux.append(jnp.sum(flux, axis=0, keepdims=True))
    side_sum, side_flux = 0.0, 0.0
    for h in range(2):
        near = []
        for c in range(4):
            west, east = jnp.where(x_high == 0, x1[c, h], x0[c, h]), jnp.where(x_high == 0, x0[c, h], x1[c, h])
            near.append(jnp.where(lane % 2 == 0, turn(east, -1, 1), turn(west, 1, 1)))
        for c in range(3):
            xnear[c, h] = near[c]
        weight, flux = flat([xpack[c, h] for c in range(4)], near, [coef_lane[k, h] for k in range(3)])
        used = lane < 2 * tiles * half
        xweight[h] = weight
        side_sum += jnp.where(used, coef_lane[0, h] * weight, 0.0)
        side_flux += jnp.where(used, flux, 0.0)
    gap = tiles * half
    while gap >= 2 * tiles:
        side_sum = side_sum + turn(side_sum, -gap, 1)
        side_flux = side_flux + turn(side_flux, -gap, 1)
        gap //= 2

    diag, ty, tx, fy, fx = acc[1], acc[2], acc[3], acc[4], acc[5]
    edge_sum = jnp.concatenate([turn(side_sum, 127 - 2 * t, 1) for t in range(tiles)], axis=0)
    edge_flux = jnp.concatenate([turn(side_flux, 127 - 2 * t, 1) for t in range(tiles)], axis=0)
    last_row, first_row, last_lane, first_lane = rows == height - 1, rows == 0, lanes == width - 1, lanes == 0
    ty_plus, ty_minus = jnp.where(last_row, y_sum[1], ty), jnp.where(first_row, y_sum[0], turn(ty, 1, 0))
    tx_plus, tx_minus = jnp.where(last_lane, edge_sum, tx), jnp.where(first_lane, edge_sum, turn(tx, 1, 1))
    fy_plus, fy_minus = jnp.where(last_row, y_flux[1], fy), jnp.where(first_row, y_flux[0], -turn(fy, 1, 0))
    fx_plus, fx_minus = jnp.where(last_lane, edge_flux, fx), jnp.where(first_lane, edge_flux, -turn(fx, 1, 1))
    planes = [
        rhs - (fy_plus + fy_minus) - (fx_plus + fx_minus),
        diag + (ty_plus + ty_minus) + (tx_plus + tx_minus),
        ty_plus,
        tx_plus,
    ]

    last = tiles - 1

    def tile(p, t):
        return planes[p][8 * t : 8 * t + 8]

    for p in range(4):
        message[0, 8 * p : 8 * p + 8, :] = tile(p, 0)
        message[1, 8 * p : 8 * p + 8, :] = tile(p, last)
        left = jnp.zeros((8, 128), F32)
        right_side = jnp.zeros((8, 128), F32)
        for t in range(tiles):
            here = lane // 8 == t
            left = jnp.where(here, turn(tile(p, t), 8 * t, 1), left)
            right_side = jnp.where(here, turn(tile(p, t), 8 * t + 8, 1), right_side)
        message[2, 8 * p : 8 * p + 8, :] = left
        message[3, 8 * p : 8 * p + 8, :] = right_side
    for k, (t, at_end) in enumerate(((0, 0), (last, 1), (0, 1), (last, 0))):
        corner = jnp.zeros((8, 128), F32)
        for p in range(4):
            corner = jnp.where(lane // 8 == p, turn(tile(p, t), 8 * p + 8 * at_end, 1), corner)
        message[4 + k, 0:8, :] = corner
        for t in range(4):
            message[4 + k, 8 + 8 * t : 16 + 8 * t, :] = tile(k, t)
        message[k, 32:40, :] = tile(k, last)


def areal_weights(z, areal_face, yweight, xweight):
    _, depth, height, width = areal_face.shape
    tiles, half = height // 8, depth // 2
    rows = row_index((height, width))
    lanes = lane_index((height, width))
    edges = edges_of(xweight[z // half], z % half, tiles)
    ty, tx = areal_face[0, z], areal_face[1, z]
    return (
        jnp.where(rows == height - 1, yweight[1, z : z + 1, :], ty),
        jnp.where(rows == 0, yweight[0, z : z + 1, :], turn(ty, 1, 0)),
        jnp.where(lanes == width - 1, edges, tx),
        jnp.where(lanes == 0, edges, turn(tx, 1, 1)),
    )


def edges_of(packed, i, tiles):
    return jnp.concatenate([turn(packed, 127 - 2 * tiles * i - 2 * t, 1) for t in range(tiles)], axis=0)


def cells_kernel(
    coef, znear, ynear, xnear, yweight, xweight, order, layer_face, areal_face, state, right_in, pore_in,
    base, gain,
    right, pore, sems,
):
    del order
    depth, height, width = pore.shape
    tiles, half = height // 8, depth // 2
    rows = row_index((height, width))
    lanes = lane_index((height, width))
    arrivals = []
    for p in range(depth // CHUNK):
        here = pl.ds(p * CHUNK, CHUNK)
        arrivals.append([
            pltpu.make_async_copy(right_in.at[:, here], right.at[:, here], sems.at[0, p]),
            pltpu.make_async_copy(pore_in.at[here], pore.at[here], sems.at[1, p]),
        ])
    for group in arrivals:
        for copy in group:
            copy.start()

    def layer(z):
        m = [[coef[3 * r + c, z : z + 1, :] for c in range(3)] for r in range(3)]
        k = [[coef[9 + 3 * r + c, z : z + 1, :] for c in range(3)] for r in range(3)]
        weights = [layer_face[z + 1], layer_face[z], *areal_weights(z, areal_face, yweight, xweight)]
        total = weights[0] + weights[1] + weights[2] + weights[3] + weights[4] + weights[5]
        nearby = []
        for c in range(3):
            u = state[c, z]
            edges = edges_of(xnear[c, z // half], z % half, tiles)
            near = (
                znear[1, c] if z == depth - 1 else state[c, z + 1],
                znear[0, c] if z == 0 else state[c, z - 1],
                jnp.where(rows == height - 1, ynear[1, c, z : z + 1, :], turn(u, -1, 0)),
                jnp.where(rows == 0, ynear[0, c, z : z + 1, :], turn(u, 1, 0)),
                jnp.where(lanes == width - 1, edges, turn(u, -1, 1)),
                jnp.where(lanes == 0, edges, turn(u, 1, 1)),
            )
            moved = weights[0] * near[0]
            for w, n in zip(weights[1:], near[1:]):
                moved = moved + w * n
            nearby.append(moved)
        v = pore[z].astype(F32)
        source = [
            right[r, z] + (k[r][0] * nearby[0] + k[r][1] * nearby[1] + k[r][2] * nearby[2]) for r in range(3)
        ]
        entries = [[v * m[r][c] + total * k[r][c] for c in range(3)] for r in range(3)]

        def cofactor(r, c):
            r1, r2, c1, c2 = (r + 1) % 3, (r + 2) % 3, (c + 1) % 3, (c + 2) % 3
            return entries[r1][c1] * entries[r2][c2] - entries[r1][c2] * entries[r2][c1]

        factors = [[cofactor(r, c) for c in range(3)] for r in range(3)]
        determinant = (
            entries[0][0] * factors[0][0] + entries[0][1] * factors[0][1] + entries[0][2] * factors[0][2]
        )
        scale = inverse(determinant)
        for r in range(3):
            base[r, z] = scale * (
                factors[0][r] * source[0] + factors[1][r] * source[1] + factors[2][r] * source[2]
            )
            gain[r, z] = scale * (factors[0][r] * k[0][0] + factors[1][r] * k[1][0] + factors[2][r] * k[2][0])

    for z in range(depth):
        if z % CHUNK == 0:
            for copy in arrivals[z // CHUNK]:
                copy.wait()
        layer(z)


def total_kernel(parts, total, strip):
    result = parts[0]
    for i in range(1, parts.shape[0]):
        result = result + parts[i]
    total[...] = result
    strip[...] = result[: strip.shape[0]]


def merge_kernel(strip, share, order, copies):
    del order
    at_corner = lax.axis_index("gz") >= 4
    for t in range(5):
        cells = slice(8 * t, 8 * t + 8)
        if t == 0:
            merged = strip[cells]
        elif t == 4:
            merged = share[cells]
        else:
            merged = jnp.where(at_corner, share[cells], strip[cells])
        for k in range(copies.shape[0]):
            copies[k, cells, :] = merged


def sweep_kernel(
    shares, layer_face, areal_face, yweight, xweight, base, gain, new_state, correction,
    result, plane, sems,
):
    _, depth, height, width = areal_face.shape
    tiles = height // 8
    lane = lane_index((8, 128))

    def tile(k, t):
        return shares[k, 8 * t : 8 * t + 8, :]

    def side(right, right_at, left, left_at):
        right, left = turn(right, -right_at, 1), turn(left, width - 8 - left_at, 1)
        return jnp.where(lane < 8, right, jnp.where(lane >= width - 8, left, 0.0))

    planes = []
    for p in range(4):
        main = [tile(1, p)] + [tile(4 + p, 1 + t) for t in range(tiles - 1)] + [tile(p, 4), tile(0, p)]
        edge = [side(tile(7, 0), 8 * p, tile(5, 0), 8 * p)]
        for t in range(tiles):
            edge.append(side(tile(2, p), 8 * t, tile(3, p), 8 * t))
        edge.append(side(tile(4, 0), 8 * p, tile(6, 0), 8 * p))
        planes.append(
            jnp.concatenate([jnp.concatenate(main, axis=0), jnp.concatenate(edge, axis=0)], axis=1)
        )
    filled = planes[1] > 0.0
    scale = jnp.where(filled, RELAX / jnp.where(filled, planes[1], 1.0), 0.0)
    source = scale * planes[0]
    south = scale * planes[2]
    north = scale * turn(planes[2], 1, 0)
    east = scale * planes[3]
    west = scale * turn(planes[3], 1, 1)

    def around(field):
        return turn(field, -1, 0), turn(field, 1, 0), turn(field, -1, 1), turn(field, 1, 1)

    field = source
    for _ in range(SWEEPS - 1):
        s, n, e, w = around(field)
        field = ((1.0 - RELAX) * field + source) + (south * s + north * n) + (east * e + west * w)
    near = around(field)
    own = field[8 : 8 + height, 0:width]
    near = [n[8 : 8 + height, 0:width] for n in near]
    plane[...] = own
    copies = [pltpu.make_async_copy(plane, correction, sems.at[depth // CHUNK])]
    copies[0].start()

    for first in range(0, depth, CHUNK):
        for z in range(first, first + CHUNK):
            push = (layer_face[z] + layer_face[z + 1]) * own
            for weight, field in zip(areal_weights(z, areal_face, yweight, xweight), near):
                push = push + weight * field
            for r in range(3):
                result[r, z] = base[r, z] + gain[r, z] * push
        copy = pltpu.make_async_copy(
            result.at[:, pl.ds(first, CHUNK)], new_state.at[:, pl.ds(first, CHUNK)], sems.at[first // CHUNK]
        )
        copy.start()
        copies.append(copy)
    for copy in copies:
        copy.wait()


def call(kernel, out_shape, in_specs, out_specs, scratch=(), flops=0, moved=0, aliases=None):
    return pl.pallas_call(
        kernel,
        out_shape=out_shape,
        in_specs=in_specs,
        out_specs=out_specs,
        scratch_shapes=list(scratch),
        compiler_params=PARAMS,
        input_output_aliases=aliases or {},
        cost_estimate=pl.CostEstimate(flops=flops, bytes_accessed=moved, transcendentals=0) if flops else None,
    )


def per_device(state, right_side, permeability, pore_volume, facies, storage_table, coupling_table):
    _, depth, height, width = state.shape
    columns = lax.axis_size("gz")
    row_of, rows = lax.axis_size("gx"), lax.axis_size("gy")
    block = (depth, height, width)
    bf16 = jnp.bfloat16
    storage_table, coupling_table = storage_table.transpose(1, 0, 2), coupling_table.transpose(1, 0, 2)

    state_v, perm_v, zface0, zface1, yface0, yface1, xpack = call(
        faces_kernel,
        [shape_of(3, *block), shape_of(*block)]
        + [shape_of(4, height, width)] * 2 + [shape_of(4, depth, width)] * 2 + [shape_of(4, 2, 8, 128)],
        hbm(2),
        vmem(7),
        [pltpu.VMEM(block, bf16), pltpu.SemaphoreType.DMA((1 + depth // PIECE,))],
    )(*in_hbm(state, permeability))

    def exchange(face, axis, odd):
        pairs = []
        for i in range(odd, lax.axis_size(axis) - 1, 2):
            pairs += [(i, i + 1), (i + 1, i)]
        return lax.ppermute(face, axis, pairs)

    received = []
    for axis, first, second in (("gz", zface0, zface1), ("gy", yface0, yface1), ("gx", xpack, xpack)):
        received += [exchange(first, axis, 0), exchange(second, axis, 1)]

    coef, coef_lane, layer_face, areal_face, acc = call(
        inner_kernel,
        [
            shape_of(18, depth, 128),
            shape_of(3, 2, 8, 128),
            shape_of(depth + 1, height, width),
            shape_of(2, *block),
            shape_of(6, height, width),
        ],
        vmem(2) + hbm(5),
        vmem(5),
        [
            pltpu.VMEM(block, F32),
            pltpu.VMEM(block, bf16),
            pltpu.SMEM(facies.shape, jnp.int32),
            pltpu.SMEM(storage_table.shape, F32),
            pltpu.SMEM(coupling_table.shape, F32),
            pltpu.SemaphoreType.DMA((5,)),
        ],
        flops=6 * 10**8,
        moved=2 * 10**6,
    )(state_v, perm_v, *in_hbm(right_side, pore_volume, facies, storage_table, coupling_table))

    layer_face, znear, ynear, xnear, yweight, xweight, message = call(
        outer_kernel,
        [
            shape_of(depth + 1, height, width),
            shape_of(2, 3, height, width),
            shape_of(2, 3, depth, width),
            shape_of(3, 2, 8, 128),
            shape_of(2, depth, width),
            shape_of(2, 8, 128),
            shape_of(columns, 40, 128),
        ],
        vmem(15),
        vmem(7),
        aliases={14: 0},
    )(coef, coef_lane, acc, zface0, zface1, yface0, yface1, xpack, *received, layer_face)

    parts = lax.all_to_all(message, "gz", 0, 0)
    share, strip = call(total_kernel, [shape_of(40, 128), shape_of(32, 128)], vmem(1), vmem(2))(parts)
    pairs = []
    for x in range(row_of):
        for y in range(rows):
            for k, (dy, dx) in enumerate(DIRECTIONS):
                if 0 <= x + dx < row_of and 0 <= y + dy < rows:
                    pairs.append(
                        ((x * rows + y) * columns + k, ((x + dx) * rows + y + dy) * columns + k)
                    )
    strip = lax.ppermute(strip, ("gx", "gy", "gz"), pairs)
    base, gain = call(
        cells_kernel,
        [shape_of(3, *block)] * 2,
        vmem(10) + hbm(2),
        vmem(2),
        [
            pltpu.VMEM((3, *block), F32),
            pltpu.VMEM(block, bf16),
            pltpu.SemaphoreType.DMA((2, depth // CHUNK)),
        ],
        flops=4 * 10**9,
        moved=4 * 10**6,
    )(
        coef, znear, ynear, xnear, yweight, xweight, share, layer_face, areal_face, state_v,
        *in_hbm(right_side, pore_volume),
    )
    copies = call(merge_kernel, shape_of(columns, 40, 128), vmem(3), vmem(1)[0])(strip, share, base)
    shares = lax.all_to_all(copies, "gz", 0, 0)

    new_state, correction = call(
        sweep_kernel,
        [pltpu.HBM((3, *block), F32), pltpu.HBM((height, width), F32)],
        vmem(7),
        hbm(2),
        [
            pltpu.VMEM((3, *block), F32),
            pltpu.VMEM((height, width), F32),
            pltpu.SemaphoreType.DMA((depth // CHUNK + 1,)),
        ],
    )(shares, layer_face, areal_face, yweight, xweight, base, gain)
    return (new_state, correction)


def solution(mesh):
    return jax.shard_map(
        per_device,
        mesh=mesh,
        in_specs=(
            P(None, "gz", "gy", "gx"),
            P(None, "gz", "gy", "gx"),
            P("gz", "gy", "gx"),
            P("gz", "gy", "gx"),
            P("gz"),
            P(),
            P(),
        ),
        out_specs=(P(None, "gz", "gy", "gx"), P("gy", "gx")),
        check_vma=False,
    )
```

```python
import jax
import jax.numpy as jnp
from jax import lax
from jax.experimental import pallas as pl
from jax.experimental.pallas import tpu as pltpu
from jax.sharding import PartitionSpec as P

SWEEPS = 8
RELAX = 0.8
DIRECTIONS = ((-1, 0), (1, 0), (0, -1), (0, 1), (-1, -1), (1, 1), (-1, 1), (1, -1))
F32 = jnp.float32
PARAMS = pltpu.CompilerParams(vmem_limit_bytes=16 * 2**20)
CHUNK = 4
PIECE = 8


def vmem(count):
    return [pl.BlockSpec(memory_space=pltpu.VMEM)] * count


def hbm(count):
    return [pl.BlockSpec(memory_space=pltpu.HBM)] * count


def shape_of(*dims):
    return jax.ShapeDtypeStruct(dims, F32)


def in_hbm(*arrays):
    return [pltpu.with_memory_space_constraint(a, pltpu.HBM) for a in arrays]


def lane_index(shape):
    return lax.broadcasted_iota(jnp.int32, shape, len(shape) - 1)


def row_index(shape):
    return lax.broadcasted_iota(jnp.int32, shape, len(shape) - 2)


def turn(block, shift, axis):
    shift = shift % block.shape[axis]
    return pltpu.roll(block, shift, axis) if shift else block


def inverse(value):
    guess = pl.reciprocal(value, approx=True)
    return guess * (2.0 - value * guess)


def mean_weight(a, b):
    return (a + a) * b * inverse(a + b)


def parity(axis):
    return lax.rem(lax.axis_index(axis), 2)


def faces_kernel(state, perm, state_v, perm_v, zface0, zface1, yface0, yface1, xpack, perm_half, sems):
    depth, height, width = perm.shape
    tiles, half = height // 8, depth // 2
    fetch = pltpu.make_async_copy(perm, perm_half, sems.at[0])
    pieces = [
        pltpu.make_async_copy(state.at[:, pl.ds(z, PIECE)], state_v.at[:, pl.ds(z, PIECE)], sems.at[1 + z // PIECE])
        for z in range(0, depth, PIECE)
    ]
    fetch.start()
    for piece in pieces:
        piece.start()
    z_high, y_high = parity("gz"), parity("gy")
    lanes = lane_index((8, 128))
    pairs = lanes // 2
    packed = [[jnp.full((8, 128), 1.0 if c == 3 else 0.0, F32) for _ in range(2)] for c in range(4)]

    def pack(c, z, cells):
        low, high = cells[0:1], cells[height - 1 : height]
        yface0[c, z : z + 1, :] = jnp.where(y_high == 0, high, low)
        yface1[c, z : z + 1, :] = jnp.where(y_high == 0, low, high)
        for t in range(tiles):
            i = (z % half) * tiles + t
            turned = turn(cells[8 * t : 8 * t + 8], 2 * i + 1, 1)
            packed[c][z // half] = jnp.where(pairs == i, turned, packed[c][z // half])

    fetch.wait()
    for z in range(depth):
        perm_v[z] = perm_half[z].astype(F32)
        pack(3, z, perm_half[z].astype(F32))
    for z in range(depth):
        if z % PIECE == 0:
            pieces[z // PIECE].wait()
        for c in range(3):
            pack(c, z, state_v[c, z])
    for c in range(4):
        for h in range(2):
            xpack[c, h] = packed[c][h]
        low, high = (state_v[c, z] if c < 3 else perm_v[z] for z in (0, depth - 1))
        zface0[c] = jnp.where(z_high == 0, high, low)
        zface1[c] = jnp.where(z_high == 0, low, high)


def inner_kernel(
    state, perm, right, pore, facies, storage_table, coupling_table,
    coef, coef_lane, layer_face, areal_face, acc, right_head, pore_v,
    right_v, facies_s, storage_s, coupling_s, sems,
):
    depth, height, width = perm.shape
    tiles, half = height // 8, depth // 2
    copies = [
        pltpu.make_async_copy(source, target, sems.at[n])
        for n, (source, target) in enumerate(
            (
                (facies, facies_s),
                (storage_table, storage_s),
                (coupling_table, coupling_s),
                (pore, pore_v),
                (right.at[0], right_v),
                (right.at[:, pl.ds(0, CHUNK)], right_head),
            )
        )
    ]
    for copy in copies:
        copy.start()
    rows = row_index((height, width))
    lanes = lane_index((height, width))
    for z in range(depth):
        q = perm[z]
        if z < depth - 1:
            layer_face[z + 1] = mean_weight(q, perm[z + 1])
        ty = jnp.where(rows == height - 1, 0.0, mean_weight(q, turn(q, -1, 0)))
        tx = jnp.where(lanes == width - 1, 0.0, mean_weight(q, turn(q, -1, 1)))
        areal_face[0, z] = ty
        areal_face[1, z] = tx

    for copy in copies[:3]:
        copy.wait()
    lane, row = lane_index((8, 128)), row_index((depth, 128))
    fids = jnp.zeros((depth, 128), jnp.int32)
    fids_lane = [jnp.zeros((8, 128), jnp.int32) for _ in range(2)]
    for z in range(depth):
        fid = facies_s[z]
        fids = jnp.where(row == z, fid, fids)
        fids_lane[z // half] = jnp.where(lane >= 2 * tiles * (z % half), fid, fids_lane[z // half])
    kinds = storage_table.shape[1]
    for which, table in enumerate((storage_s, coupling_s)):
        for k in range(9):
            rows_of = jnp.zeros((depth, 128), F32)
            for f in range(kinds):
                rows_of = jnp.where(fids == f, table[k // 3, f, k % 3], rows_of)
            coef[9 * which + k] = rows_of
    for k in range(3):
        for h in range(2):
            lane_of = jnp.zeros((8, 128), F32)
            for f in range(kinds):
                lane_of = jnp.where(fids_lane[h] == f, coupling_s[0, f, k], lane_of)
            coef_lane[k, h] = lane_of
    for copy in copies[3:5]:
        copy.wait()

    for a in range(6):
        acc[a] = jnp.zeros((height, width), F32)
    for z in range(depth):
        u = [state[c, z] for c in range(3)]
        m0 = [coef[c, z : z + 1, :] for c in range(3)]
        k0 = [coef[9 + c, z : z + 1, :] for c in range(3)]
        v = pore_v[z].astype(F32)
        part = right_v[z] - v * (m0[0] * u[0] + m0[1] * u[1] + m0[2] * u[2])
        if z < depth - 1:
            step = [k0[c] - coef[9 + c, z + 1 : z + 2, :] for c in range(3)]
            jump = [u[c] - state[c, z + 1] for c in range(3)]
            part = part - layer_face[z + 1] * (step[0] * jump[0] + step[1] * jump[1] + step[2] * jump[2])
        acc[0] += part
        acc[1] += m0[0] * v
        w = k0[0] * u[0] + k0[1] * u[1] + k0[2] * u[2]
        ty, tx = areal_face[0, z], areal_face[1, z]
        acc[2] += k0[0] * ty
        acc[3] += k0[0] * tx
        acc[4] += ty * (w - turn(w, -1, 0))
        acc[5] += tx * (w - turn(w, -1, 1))
    copies[5].wait()


def outer_kernel(
    coef, coef_lane, acc, zface0, zface1, yface0, yface1, xpack, z0, z1, y0, y1, x0, x1, layer_in,
    layer_face, znear, ynear, xnear, yweight, xweight, message,
):
    del layer_in
    _, height, width = zface0.shape
    depth = yface0.shape[1]
    tiles, half = height // 8, depth // 2
    rows = row_index((height, width))
    lanes = lane_index((height, width))
    lane = lane_index((8, 128))
    z_high, y_high, x_high = parity("gz"), parity("gy"), parity("gx")

    def received(high, first, second, c):
        a, b = first[c], second[c]
        return jnp.where(high == 0, b, a), jnp.where(high == 0, a, b)

    def flat(own, near, k0):
        weight = mean_weight(own[3], near[3])
        jump = k0[0] * (own[0] - near[0]) + k0[1] * (own[1] - near[1]) + k0[2] * (own[2] - near[2])
        return weight, weight * jump

    zown = [received(z_high, zface0, zface1, c) for c in range(4)]
    yown = [received(y_high, yface0, yface1, c) for c in range(4)]
    znears = [received(z_high, z0, z1, c) for c in range(4)]
    ynears = [received(y_high, y0, y1, c) for c in range(4)]
    for c in range(3):
        for e in range(2):
            znear[e, c] = znears[c][e]
            ynear[e, c] = ynears[c][e]
    rhs = acc[0]
    for e, z in ((0, 0), (1, depth - 1)):
        weight, flux = flat(
            [zown[c][e] for c in range(4)],
            [znears[c][e] for c in range(4)],
            [coef[9 + c, z : z + 1, :] for c in range(3)],
        )
        layer_face[z + e] = weight
        rhs = rhs - flux
    k_rows = [coef[9 + k] for k in range(3)]
    y_sum, y_flux = [], []
    for e in range(2):
        weight, flux = flat([yown[c][e] for c in range(4)], [ynears[c][e] for c in range(4)], k_rows)
        yweight[e] = weight
        y_sum.append(jnp.sum(k_rows[0] * weight, axis=0, keepdims=True))
        y_flux.append(jnp.sum(flux, axis=0, keepdims=True))
    side_sum, side_flux = 0.0, 0.0
    for h in range(2):
        near = []
        for c in range(4):
            west, east = jnp.where(x_high == 0, x1[c, h], x0[c, h]), jnp.where(x_high == 0, x0[c, h], x1[c, h])
            near.append(jnp.where(lane % 2 == 0, turn(east, -1, 1), turn(west, 1, 1)))
        for c in range(3):
            xnear[c, h] = near[c]
        weight, flux = flat([xpack[c, h] for c in range(4)], near, [coef_lane[k, h] for k in range(3)])
        used = lane < 2 * tiles * half
        xweight[h] = weight
        side_sum += jnp.where(used, coef_lane[0, h] * weight, 0.0)
        side_flux += jnp.where(used, flux, 0.0)
    gap = tiles * half
    while gap >= 2 * tiles:
        side_sum = side_sum + turn(side_sum, -gap, 1)
        side_flux = side_flux + turn(side_flux, -gap, 1)
        gap //= 2

    diag, ty, tx, fy, fx = acc[1], acc[2], acc[3], acc[4], acc[5]
    edge_sum = jnp.concatenate([turn(side_sum, 127 - 2 * t, 1) for t in range(tiles)], axis=0)
    edge_flux = jnp.concatenate([turn(side_flux, 127 - 2 * t, 1) for t in range(tiles)], axis=0)
    last_row, first_row, last_lane, first_lane = rows == height - 1, rows == 0, lanes == width - 1, lanes == 0
    ty_plus, ty_minus = jnp.where(last_row, y_sum[1], ty), jnp.where(first_row, y_sum[0], turn(ty, 1, 0))
    tx_plus, tx_minus = jnp.where(last_lane, edge_sum, tx), jnp.where(first_lane, edge_sum, turn(tx, 1, 1))
    fy_plus, fy_minus = jnp.where(last_row, y_flux[1], fy), jnp.where(first_row, y_flux[0], -turn(fy, 1, 0))
    fx_plus, fx_minus = jnp.where(last_lane, edge_flux, fx), jnp.where(first_lane, edge_flux, -turn(fx, 1, 1))
    planes = [
        rhs - (fy_plus + fy_minus) - (fx_plus + fx_minus),
        diag + (ty_plus + ty_minus) + (tx_plus + tx_minus),
        ty_plus,
        tx_plus,
    ]

    last = tiles - 1

    def tile(p, t):
        return planes[p][8 * t : 8 * t + 8]

    for p in range(4):
        message[0, 8 * p : 8 * p + 8, :] = tile(p, 0)
        message[1, 8 * p : 8 * p + 8, :] = tile(p, last)
        left = jnp.zeros((8, 128), F32)
        right_side = jnp.zeros((8, 128), F32)
        for t in range(tiles):
            here = lane // 8 == t
            left = jnp.where(here, turn(tile(p, t), 8 * t, 1), left)
            right_side = jnp.where(here, turn(tile(p, t), 8 * t + 8, 1), right_side)
        message[2, 8 * p : 8 * p + 8, :] = left
        message[3, 8 * p : 8 * p + 8, :] = right_side
    for k, (t, at_end) in enumerate(((0, 0), (last, 1), (0, 1), (last, 0))):
        corner = jnp.zeros((8, 128), F32)
        for p in range(4):
            corner = jnp.where(lane // 8 == p, turn(tile(p, t), 8 * p + 8 * at_end, 1), corner)
        message[4 + k, 0:8, :] = corner
        for t in range(4):
            message[4 + k, 8 + 8 * t : 16 + 8 * t, :] = tile(k, t)
        message[k, 32:40, :] = tile(k, last)


def areal_weights(z, areal_face, yweight, xweight):
    _, depth, height, width = areal_face.shape
    tiles, half = height // 8, depth // 2
    rows = row_index((height, width))
    lanes = lane_index((height, width))
    edges = edges_of(xweight[z // half], z % half, tiles)
    ty, tx = areal_face[0, z], areal_face[1, z]
    return (
        jnp.where(rows == height - 1, yweight[1, z : z + 1, :], ty),
        jnp.where(rows == 0, yweight[0, z : z + 1, :], turn(ty, 1, 0)),
        jnp.where(lanes == width - 1, edges, tx),
        jnp.where(lanes == 0, edges, turn(tx, 1, 1)),
    )


def edges_of(packed, i, tiles):
    return jnp.concatenate([turn(packed, 127 - 2 * tiles * i - 2 * t, 1) for t in range(tiles)], axis=0)


def cells_kernel(
    coef, znear, ynear, xnear, yweight, xweight, order, layer_face, areal_face, state, right_head, pore, right_in,
    base, gain,
    right, sems,
):
    del order
    depth, height, width = pore.shape
    tiles, half = height // 8, depth // 2
    rows = row_index((height, width))
    lanes = lane_index((height, width))
    arrivals = {}
    for p in range(1, depth // CHUNK):
        here = pl.ds(p * CHUNK, CHUNK)
        arrivals[p] = pltpu.make_async_copy(right_in.at[:, here], right.at[:, here], sems.at[p])
        arrivals[p].start()

    def layer(z):
        m = [[coef[3 * r + c, z : z + 1, :] for c in range(3)] for r in range(3)]
        k = [[coef[9 + 3 * r + c, z : z + 1, :] for c in range(3)] for r in range(3)]
        weights = [layer_face[z + 1], layer_face[z], *areal_weights(z, areal_face, yweight, xweight)]
        total = weights[0] + weights[1] + weights[2] + weights[3] + weights[4] + weights[5]
        nearby = []
        for c in range(3):
            u = state[c, z]
            edges = edges_of(xnear[c, z // half], z % half, tiles)
            near = (
                znear[1, c] if z == depth - 1 else state[c, z + 1],
                znear[0, c] if z == 0 else state[c, z - 1],
                jnp.where(rows == height - 1, ynear[1, c, z : z + 1, :], turn(u, -1, 0)),
                jnp.where(rows == 0, ynear[0, c, z : z + 1, :], turn(u, 1, 0)),
                jnp.where(lanes == width - 1, edges, turn(u, -1, 1)),
                jnp.where(lanes == 0, edges, turn(u, 1, 1)),
            )
            moved = weights[0] * near[0]
            for w, n in zip(weights[1:], near[1:]):
                moved = moved + w * n
            nearby.append(moved)
        v = pore[z].astype(F32)
        source = [
            (right_head if z < CHUNK else right)[r, z] + (k[r][0] * nearby[0] + k[r][1] * nearby[1] + k[r][2] * nearby[2]) for r in range(3)
        ]
        entries = [[v * m[r][c] + total * k[r][c] for c in range(3)] for r in range(3)]

        def cofactor(r, c):
            r1, r2, c1, c2 = (r + 1) % 3, (r + 2) % 3, (c + 1) % 3, (c + 2) % 3
            return entries[r1][c1] * entries[r2][c2] - entries[r1][c2] * entries[r2][c1]

        factors = [[cofactor(r, c) for c in range(3)] for r in range(3)]
        determinant = (
            entries[0][0] * factors[0][0] + entries[0][1] * factors[0][1] + entries[0][2] * factors[0][2]
        )
        scale = inverse(determinant)
        for r in range(3):
            base[r, z] = scale * (
                factors[0][r] * source[0] + factors[1][r] * source[1] + factors[2][r] * source[2]
            )
            gain[r, z] = scale * (factors[0][r] * k[0][0] + factors[1][r] * k[1][0] + factors[2][r] * k[2][0])

    for z in range(depth):
        if z and z % CHUNK == 0:
            arrivals[z // CHUNK].wait()
        layer(z)


def total_kernel(parts, total, strip):
    result = parts[0]
    for i in range(1, parts.shape[0]):
        result = result + parts[i]
    total[...] = result
    strip[...] = result[: strip.shape[0]]


def merge_kernel(strip, share, order, copies):
    del order
    at_corner = lax.axis_index("gz") >= 4
    for t in range(5):
        cells = slice(8 * t, 8 * t + 8)
        if t == 0:
            merged = strip[cells]
        elif t == 4:
            merged = share[cells]
        else:
            merged = jnp.where(at_corner, share[cells], strip[cells])
        for k in range(copies.shape[0]):
            copies[k, cells, :] = merged


def sweep_kernel(
    shares, layer_face, areal_face, yweight, xweight, base, gain, new_state, correction,
    result, plane, sems,
):
    _, depth, height, width = areal_face.shape
    tiles = height // 8
    lane = lane_index((8, 128))

    def tile(k, t):
        return shares[k, 8 * t : 8 * t + 8, :]

    def side(right, right_at, left, left_at):
        right, left = turn(right, -right_at, 1), turn(left, width - 8 - left_at, 1)
        return jnp.where(lane < 8, right, jnp.where(lane >= width - 8, left, 0.0))

    planes = []
    for p in range(4):
        main = [tile(1, p)] + [tile(4 + p, 1 + t) for t in range(tiles - 1)] + [tile(p, 4), tile(0, p)]
        edge = [side(tile(7, 0), 8 * p, tile(5, 0), 8 * p)]
        for t in range(tiles):
            edge.append(side(tile(2, p), 8 * t, tile(3, p), 8 * t))
        edge.append(side(tile(4, 0), 8 * p, tile(6, 0), 8 * p))
        planes.append(
            jnp.concatenate([jnp.concatenate(main, axis=0), jnp.concatenate(edge, axis=0)], axis=1)
        )
    filled = planes[1] > 0.0
    scale = jnp.where(filled, RELAX / jnp.where(filled, planes[1], 1.0), 0.0)
    source = scale * planes[0]
    south = scale * planes[2]
    north = scale * turn(planes[2], 1, 0)
    east = scale * planes[3]
    west = scale * turn(planes[3], 1, 1)

    def around(field):
        return turn(field, -1, 0), turn(field, 1, 0), turn(field, -1, 1), turn(field, 1, 1)

    field = source
    for _ in range(SWEEPS - 1):
        s, n, e, w = around(field)
        field = ((1.0 - RELAX) * field + source) + (south * s + north * n) + (east * e + west * w)
    near = around(field)
    own = field[8 : 8 + height, 0:width]
    near = [n[8 : 8 + height, 0:width] for n in near]
    plane[...] = own
    copies = [pltpu.make_async_copy(plane, correction, sems.at[depth // CHUNK])]
    copies[0].start()

    for first in range(0, depth, CHUNK):
        for z in range(first, first + CHUNK):
            push = (layer_face[z] + layer_face[z + 1]) * own
            for weight, field in zip(areal_weights(z, areal_face, yweight, xweight), near):
                push = push + weight * field
            for r in range(3):
                result[r, z] = base[r, z] + gain[r, z] * push
        copy = pltpu.make_async_copy(
            result.at[:, pl.ds(first, CHUNK)], new_state.at[:, pl.ds(first, CHUNK)], sems.at[first // CHUNK]
        )
        copy.start()
        copies.append(copy)
    for copy in copies:
        copy.wait()


def call(kernel, out_shape, in_specs, out_specs, scratch=(), flops=0, moved=0, aliases=None):
    return pl.pallas_call(
        kernel,
        out_shape=out_shape,
        in_specs=in_specs,
        out_specs=out_specs,
        scratch_shapes=list(scratch),
        compiler_params=PARAMS,
        input_output_aliases=aliases or {},
        cost_estimate=pl.CostEstimate(flops=flops, bytes_accessed=moved, transcendentals=0) if flops else None,
    )


def per_device(state, right_side, permeability, pore_volume, facies, storage_table, coupling_table):
    _, depth, height, width = state.shape
    columns = lax.axis_size("gz")
    row_of, rows = lax.axis_size("gx"), lax.axis_size("gy")
    block = (depth, height, width)
    bf16 = jnp.bfloat16
    storage_table, coupling_table = storage_table.transpose(1, 0, 2), coupling_table.transpose(1, 0, 2)

    state_v, perm_v, zface0, zface1, yface0, yface1, xpack = call(
        faces_kernel,
        [shape_of(3, *block), shape_of(*block)]
        + [shape_of(4, height, width)] * 2 + [shape_of(4, depth, width)] * 2 + [shape_of(4, 2, 8, 128)],
        hbm(2),
        vmem(7),
        [pltpu.VMEM(block, bf16), pltpu.SemaphoreType.DMA((1 + depth // PIECE,))],
    )(*in_hbm(state, permeability))

    def exchange(face, axis, odd):
        pairs = []
        for i in range(odd, lax.axis_size(axis) - 1, 2):
            pairs += [(i, i + 1), (i + 1, i)]
        return lax.ppermute(face, axis, pairs)

    received = []
    for axis, first, second in (("gz", zface0, zface1), ("gy", yface0, yface1), ("gx", xpack, xpack)):
        received += [exchange(first, axis, 0), exchange(second, axis, 1)]

    coef, coef_lane, layer_face, areal_face, acc, right_head, pore_v = call(
        inner_kernel,
        [
            shape_of(18, depth, 128),
            shape_of(3, 2, 8, 128),
            shape_of(depth + 1, height, width),
            shape_of(2, *block),
            shape_of(6, height, width),
            shape_of(3, CHUNK, height, width),
            jax.ShapeDtypeStruct(block, bf16),
        ],
        vmem(2) + hbm(5),
        vmem(7),
        [
            pltpu.VMEM(block, F32),
            pltpu.SMEM(facies.shape, jnp.int32),
            pltpu.SMEM(storage_table.shape, F32),
            pltpu.SMEM(coupling_table.shape, F32),
            pltpu.SemaphoreType.DMA((6,)),
        ],
        flops=6 * 10**8,
        moved=2 * 10**6,
    )(state_v, perm_v, *in_hbm(right_side, pore_volume, facies, storage_table, coupling_table))

    layer_face, znear, ynear, xnear, yweight, xweight, message = call(
        outer_kernel,
        [
            shape_of(depth + 1, height, width),
            shape_of(2, 3, height, width),
            shape_of(2, 3, depth, width),
            shape_of(3, 2, 8, 128),
            shape_of(2, depth, width),
            shape_of(2, 8, 128),
            shape_of(columns, 40, 128),
        ],
        vmem(15),
        vmem(7),
        aliases={14: 0},
    )(coef, coef_lane, acc, zface0, zface1, yface0, yface1, xpack, *received, layer_face)

    parts = lax.all_to_all(message, "gz", 0, 0)
    share, strip = call(total_kernel, [shape_of(40, 128), shape_of(32, 128)], vmem(1), vmem(2))(parts)
    pairs = []
    for x in range(row_of):
        for y in range(rows):
            for k, (dy, dx) in enumerate(DIRECTIONS):
                if 0 <= x + dx < row_of and 0 <= y + dy < rows:
                    pairs.append(
                        ((x * rows + y) * columns + k, ((x + dx) * rows + y + dy) * columns + k)
                    )
    strip = lax.ppermute(strip, ("gx", "gy", "gz"), pairs)
    base, gain = call(
        cells_kernel,
        [shape_of(3, *block)] * 2,
        vmem(12) + hbm(1),
        vmem(2),
        [pltpu.VMEM((3, *block), F32), pltpu.SemaphoreType.DMA((depth // CHUNK,))],
        flops=4 * 10**9,
        moved=4 * 10**6,
    )(
        coef, znear, ynear, xnear, yweight, xweight, share, layer_face, areal_face, state_v,
        right_head, pore_v, *in_hbm(right_side),
    )
    copies = call(merge_kernel, shape_of(columns, 40, 128), vmem(3), vmem(1)[0])(strip, share, base)
    shares = lax.all_to_all(copies, "gz", 0, 0)

    new_state, correction = call(
        sweep_kernel,
        [pltpu.HBM((3, *block), F32), pltpu.HBM((height, width), F32)],
        vmem(7),
        hbm(2),
        [
            pltpu.VMEM((3, *block), F32),
            pltpu.VMEM((height, width), F32),
            pltpu.SemaphoreType.DMA((depth // CHUNK + 1,)),
        ],
    )(shares, layer_face, areal_face, yweight, xweight, base, gain)
    return (new_state, correction)


def solution(mesh):
    return jax.shard_map(
        per_device,
        mesh=mesh,
        in_specs=(
            P(None, "gz", "gy", "gx"),
            P(None, "gz", "gy", "gx"),
            P("gz", "gy", "gx"),
            P("gz", "gy", "gx"),
            P("gz"),
            P(),
            P(),
        ),
        out_specs=(P(None, "gz", "gy", "gx"), P("gy", "gx")),
        check_vma=False,
    )
```

```python
import jax
import jax.numpy as jnp
from jax import lax
from jax.experimental import pallas as pl
from jax.experimental.pallas import tpu as pltpu
from jax.sharding import PartitionSpec as P

SWEEPS = 8
RELAX = 0.8
DIRECTIONS = ((-1, 0), (1, 0), (0, -1), (0, 1), (-1, -1), (1, 1), (-1, 1), (1, -1))
F32 = jnp.float32
PARAMS = pltpu.CompilerParams(vmem_limit_bytes=16 * 2**20)
CHUNK = 4
PIECE = 8


def vmem(count):
    return [pl.BlockSpec(memory_space=pltpu.VMEM)] * count


def hbm(count):
    return [pl.BlockSpec(memory_space=pltpu.HBM)] * count


def shape_of(*dims):
    return jax.ShapeDtypeStruct(dims, F32)


def in_hbm(*arrays):
    return [pltpu.with_memory_space_constraint(a, pltpu.HBM) for a in arrays]


def lane_index(shape):
    return lax.broadcasted_iota(jnp.int32, shape, len(shape) - 1)


def row_index(shape):
    return lax.broadcasted_iota(jnp.int32, shape, len(shape) - 2)


def turn(block, shift, axis):
    shift = shift % block.shape[axis]
    return pltpu.roll(block, shift, axis) if shift else block


def inverse(value):
    guess = pl.reciprocal(value, approx=True)
    return guess * (2.0 - value * guess)


def mean_weight(a, b):
    return (a + a) * b * inverse(a + b)


def parity(axis):
    return lax.rem(lax.axis_index(axis), 2)


def faces_kernel(
    state, perm, facies, storage_table, coupling_table,
    state_v, perm_v, coef, coef_lane, zface0, zface1, yface0, yface1, xpack,
    perm_half, facies_s, storage_s, coupling_s, sems,
):
    depth, height, width = perm.shape
    tiles, half = height // 8, depth // 2
    fetch = pltpu.make_async_copy(perm, perm_half, sems.at[0])
    pieces = [
        pltpu.make_async_copy(state.at[:, pl.ds(z, PIECE)], state_v.at[:, pl.ds(z, PIECE)], sems.at[1 + z // PIECE])
        for z in range(0, depth, PIECE)
    ]
    tables = [
        pltpu.make_async_copy(source, target, sems.at[1 + depth // PIECE + n])
        for n, (source, target) in enumerate(
            ((facies, facies_s), (storage_table, storage_s), (coupling_table, coupling_s))
        )
    ]
    fetch.start()
    for copy in tables:
        copy.start()
    for piece in pieces:
        piece.start()
    z_high, y_high = parity("gz"), parity("gy")
    lanes = lane_index((8, 128))
    pairs = lanes // 2
    packed = [[jnp.full((8, 128), 1.0 if c == 3 else 0.0, F32) for _ in range(2)] for c in range(4)]

    def pack(c, z, cells):
        low, high = cells[0:1], cells[height - 1 : height]
        yface0[c, z : z + 1, :] = jnp.where(y_high == 0, high, low)
        yface1[c, z : z + 1, :] = jnp.where(y_high == 0, low, high)
        for t in range(tiles):
            i = (z % half) * tiles + t
            turned = turn(cells[8 * t : 8 * t + 8], 2 * i + 1, 1)
            packed[c][z // half] = jnp.where(pairs == i, turned, packed[c][z // half])

    fetch.wait()
    for z in range(depth):
        perm_v[z] = perm_half[z].astype(F32)
        pack(3, z, perm_half[z].astype(F32))
    for copy in tables:
        copy.wait()
    row = row_index((depth, 128))
    fids = jnp.zeros((depth, 128), jnp.int32)
    fids_lane = [jnp.zeros((8, 128), jnp.int32) for _ in range(2)]
    for z in range(depth):
        fid = facies_s[z]
        fids = jnp.where(row == z, fid, fids)
        fids_lane[z // half] = jnp.where(lanes >= 2 * tiles * (z % half), fid, fids_lane[z // half])
    kinds = storage_table.shape[1]
    for which, table in enumerate((storage_s, coupling_s)):
        for k in range(9):
            rows_of = jnp.zeros((depth, 128), F32)
            for f in range(kinds):
                rows_of = jnp.where(fids == f, table[k // 3, f, k % 3], rows_of)
            coef[9 * which + k] = rows_of
    for k in range(3):
        for h in range(2):
            lane_of = jnp.zeros((8, 128), F32)
            for f in range(kinds):
                lane_of = jnp.where(fids_lane[h] == f, coupling_s[0, f, k], lane_of)
            coef_lane[k, h] = lane_of
    for z in range(depth):
        if z % PIECE == 0:
            pieces[z // PIECE].wait()
        for c in range(3):
            pack(c, z, state_v[c, z])
    for c in range(4):
        for h in range(2):
            xpack[c, h] = packed[c][h]
        low, high = (state_v[c, z] if c < 3 else perm_v[z] for z in (0, depth - 1))
        zface0[c] = jnp.where(z_high == 0, high, low)
        zface1[c] = jnp.where(z_high == 0, low, high)


def inner_kernel(
    state, perm, coef, right, pore,
    layer_face, areal_face, acc, right_v, right_head, pore_v,
    sems,
):
    depth, height, width = perm.shape
    tiles, half = height // 8, depth // 2
    copies = [
        pltpu.make_async_copy(source, target, sems.at[n])
        for n, (source, target) in enumerate(
            (
                (pore, pore_v),
                (right.at[0], right_v),
                (right.at[pl.ds(1, 2), pl.ds(0, CHUNK)], right_head),
            )
        )
    ]
    for copy in copies:
        copy.start()
    rows = row_index((height, width))
    lanes = lane_index((height, width))
    for z in range(depth):
        q = perm[z]
        if z < depth - 1:
            layer_face[z + 1] = mean_weight(q, perm[z + 1])
        ty = jnp.where(rows == height - 1, 0.0, mean_weight(q, turn(q, -1, 0)))
        tx = jnp.where(lanes == width - 1, 0.0, mean_weight(q, turn(q, -1, 1)))
        areal_face[0, z] = ty
        areal_face[1, z] = tx

    for copy in copies[:2]:
        copy.wait()

    for a in range(6):
        acc[a] = jnp.zeros((height, width), F32)
    for z in range(depth):
        u = [state[c, z] for c in range(3)]
        m0 = [coef[c, z : z + 1, :] for c in range(3)]
        k0 = [coef[9 + c, z : z + 1, :] for c in range(3)]
        v = pore_v[z].astype(F32)
        part = right_v[z] - v * (m0[0] * u[0] + m0[1] * u[1] + m0[2] * u[2])
        if z < depth - 1:
            step = [k0[c] - coef[9 + c, z + 1 : z + 2, :] for c in range(3)]
            jump = [u[c] - state[c, z + 1] for c in range(3)]
            part = part - layer_face[z + 1] * (step[0] * jump[0] + step[1] * jump[1] + step[2] * jump[2])
        acc[0] += part
        acc[1] += m0[0] * v
        w = k0[0] * u[0] + k0[1] * u[1] + k0[2] * u[2]
        ty, tx = areal_face[0, z], areal_face[1, z]
        acc[2] += k0[0] * ty
        acc[3] += k0[0] * tx
        acc[4] += ty * (w - turn(w, -1, 0))
        acc[5] += tx * (w - turn(w, -1, 1))
    copies[2].wait()


def outer_kernel(
    coef, coef_lane, acc, zface0, zface1, yface0, yface1, xpack, z0, z1, y0, y1, x0, x1, layer_in,
    layer_face, znear, ynear, xnear, yweight, xweight, message,
):
    del layer_in
    _, height, width = zface0.shape
    depth = yface0.shape[1]
    tiles, half = height // 8, depth // 2
    rows = row_index((height, width))
    lanes = lane_index((height, width))
    lane = lane_index((8, 128))
    z_high, y_high, x_high = parity("gz"), parity("gy"), parity("gx")

    def received(high, first, second, c):
        a, b = first[c], second[c]
        return jnp.where(high == 0, b, a), jnp.where(high == 0, a, b)

    def flat(own, near, k0):
        weight = mean_weight(own[3], near[3])
        jump = k0[0] * (own[0] - near[0]) + k0[1] * (own[1] - near[1]) + k0[2] * (own[2] - near[2])
        return weight, weight * jump

    zown = [received(z_high, zface0, zface1, c) for c in range(4)]
    yown = [received(y_high, yface0, yface1, c) for c in range(4)]
    znears = [received(z_high, z0, z1, c) for c in range(4)]
    ynears = [received(y_high, y0, y1, c) for c in range(4)]
    for c in range(3):
        for e in range(2):
            znear[e, c] = znears[c][e]
            ynear[e, c] = ynears[c][e]
    rhs = acc[0]
    for e, z in ((0, 0), (1, depth - 1)):
        weight, flux = flat(
            [zown[c][e] for c in range(4)],
            [znears[c][e] for c in range(4)],
            [coef[9 + c, z : z + 1, :] for c in range(3)],
        )
        layer_face[z + e] = weight
        rhs = rhs - flux
    k_rows = [coef[9 + k] for k in range(3)]
    y_sum, y_flux = [], []
    for e in range(2):
        weight, flux = flat([yown[c][e] for c in range(4)], [ynears[c][e] for c in range(4)], k_rows)
        yweight[e] = weight
        y_sum.append(jnp.sum(k_rows[0] * weight, axis=0, keepdims=True))
        y_flux.append(jnp.sum(flux, axis=0, keepdims=True))
    side_sum, side_flux = 0.0, 0.0
    for h in range(2):
        near = []
        for c in range(4):
            west, east = jnp.where(x_high == 0, x1[c, h], x0[c, h]), jnp.where(x_high == 0, x0[c, h], x1[c, h])
            near.append(jnp.where(lane % 2 == 0, turn(east, -1, 1), turn(west, 1, 1)))
        for c in range(3):
            xnear[c, h] = near[c]
        weight, flux = flat([xpack[c, h] for c in range(4)], near, [coef_lane[k, h] for k in range(3)])
        used = lane < 2 * tiles * half
        xweight[h] = weight
        side_sum += jnp.where(used, coef_lane[0, h] * weight, 0.0)
        side_flux += jnp.where(used, flux, 0.0)
    gap = tiles * half
    while gap >= 2 * tiles:
        side_sum = side_sum + turn(side_sum, -gap, 1)
        side_flux = side_flux + turn(side_flux, -gap, 1)
        gap //= 2

    diag, ty, tx, fy, fx = acc[1], acc[2], acc[3], acc[4], acc[5]
    edge_sum = jnp.concatenate([turn(side_sum, 127 - 2 * t, 1) for t in range(tiles)], axis=0)
    edge_flux = jnp.concatenate([turn(side_flux, 127 - 2 * t, 1) for t in range(tiles)], axis=0)
    last_row, first_row, last_lane, first_lane = rows == height - 1, rows == 0, lanes == width - 1, lanes == 0
    ty_plus, ty_minus = jnp.where(last_row, y_sum[1], ty), jnp.where(first_row, y_sum[0], turn(ty, 1, 0))
    tx_plus, tx_minus = jnp.where(last_lane, edge_sum, tx), jnp.where(first_lane, edge_sum, turn(tx, 1, 1))
    fy_plus, fy_minus = jnp.where(last_row, y_flux[1], fy), jnp.where(first_row, y_flux[0], -turn(fy, 1, 0))
    fx_plus, fx_minus = jnp.where(last_lane, edge_flux, fx), jnp.where(first_lane, edge_flux, -turn(fx, 1, 1))
    planes = [
        rhs - (fy_plus + fy_minus) - (fx_plus + fx_minus),
        diag + (ty_plus + ty_minus) + (tx_plus + tx_minus),
        ty_plus,
        tx_plus,
    ]

    last = tiles - 1

    def tile(p, t):
        return planes[p][8 * t : 8 * t + 8]

    for p in range(4):
        message[0, 8 * p : 8 * p + 8, :] = tile(p, 0)
        message[1, 8 * p : 8 * p + 8, :] = tile(p, last)
        left = jnp.zeros((8, 128), F32)
        right_side = jnp.zeros((8, 128), F32)
        for t in range(tiles):
            here = lane // 8 == t
            left = jnp.where(here, turn(tile(p, t), 8 * t, 1), left)
            right_side = jnp.where(here, turn(tile(p, t), 8 * t + 8, 1), right_side)
        message[2, 8 * p : 8 * p + 8, :] = left
        message[3, 8 * p : 8 * p + 8, :] = right_side
    for k, (t, at_end) in enumerate(((0, 0), (last, 1), (0, 1), (last, 0))):
        corner = jnp.zeros((8, 128), F32)
        for p in range(4):
            corner = jnp.where(lane // 8 == p, turn(tile(p, t), 8 * p + 8 * at_end, 1), corner)
        message[4 + k, 0:8, :] = corner
        for t in range(4):
            message[4 + k, 8 + 8 * t : 16 + 8 * t, :] = tile(k, t)
        message[k, 32:40, :] = tile(k, last)


def areal_weights(z, areal_face, yweight, xweight):
    _, depth, height, width = areal_face.shape
    tiles, half = height // 8, depth // 2
    rows = row_index((height, width))
    lanes = lane_index((height, width))
    edges = edges_of(xweight[z // half], z % half, tiles)
    ty, tx = areal_face[0, z], areal_face[1, z]
    return (
        jnp.where(rows == height - 1, yweight[1, z : z + 1, :], ty),
        jnp.where(rows == 0, yweight[0, z : z + 1, :], turn(ty, 1, 0)),
        jnp.where(lanes == width - 1, edges, tx),
        jnp.where(lanes == 0, edges, turn(tx, 1, 1)),
    )


def edges_of(packed, i, tiles):
    return jnp.concatenate([turn(packed, 127 - 2 * tiles * i - 2 * t, 1) for t in range(tiles)], axis=0)


def cells_kernel(
    coef, znear, ynear, xnear, yweight, xweight, order, layer_face, areal_face, state, right_first, right_head, pore, right_in,
    base, gain,
    right, sems,
):
    del order
    depth, height, width = pore.shape
    tiles, half = height // 8, depth // 2
    rows = row_index((height, width))
    lanes = lane_index((height, width))
    arrivals = {}
    for p in range(1, depth // CHUNK):
        here = pl.ds(p * CHUNK, CHUNK)
        arrivals[p] = pltpu.make_async_copy(right_in.at[pl.ds(1, 2), here], right.at[:, here], sems.at[p])
        arrivals[p].start()

    def layer(z):
        m = [[coef[3 * r + c, z : z + 1, :] for c in range(3)] for r in range(3)]
        k = [[coef[9 + 3 * r + c, z : z + 1, :] for c in range(3)] for r in range(3)]
        weights = [layer_face[z + 1], layer_face[z], *areal_weights(z, areal_face, yweight, xweight)]
        total = weights[0] + weights[1] + weights[2] + weights[3] + weights[4] + weights[5]
        nearby = []
        for c in range(3):
            u = state[c, z]
            edges = edges_of(xnear[c, z // half], z % half, tiles)
            near = (
                znear[1, c] if z == depth - 1 else state[c, z + 1],
                znear[0, c] if z == 0 else state[c, z - 1],
                jnp.where(rows == height - 1, ynear[1, c, z : z + 1, :], turn(u, -1, 0)),
                jnp.where(rows == 0, ynear[0, c, z : z + 1, :], turn(u, 1, 0)),
                jnp.where(lanes == width - 1, edges, turn(u, -1, 1)),
                jnp.where(lanes == 0, edges, turn(u, 1, 1)),
            )
            moved = weights[0] * near[0]
            for w, n in zip(weights[1:], near[1:]):
                moved = moved + w * n
            nearby.append(moved)
        v = pore[z].astype(F32)
        source = [
            (right_first[z] if r == 0 else (right_head if z < CHUNK else right)[r - 1, z])
            + (k[r][0] * nearby[0] + k[r][1] * nearby[1] + k[r][2] * nearby[2]) for r in range(3)
        ]
        entries = [[v * m[r][c] + total * k[r][c] for c in range(3)] for r in range(3)]

        def cofactor(r, c):
            r1, r2, c1, c2 = (r + 1) % 3, (r + 2) % 3, (c + 1) % 3, (c + 2) % 3
            return entries[r1][c1] * entries[r2][c2] - entries[r1][c2] * entries[r2][c1]

        factors = [[cofactor(r, c) for c in range(3)] for r in range(3)]
        determinant = (
            entries[0][0] * factors[0][0] + entries[0][1] * factors[0][1] + entries[0][2] * factors[0][2]
        )
        scale = inverse(determinant)
        for r in range(3):
            base[r, z] = scale * (
                factors[0][r] * source[0] + factors[1][r] * source[1] + factors[2][r] * source[2]
            )
            gain[r, z] = scale * (factors[0][r] * k[0][0] + factors[1][r] * k[1][0] + factors[2][r] * k[2][0])

    for z in range(depth):
        if z and z % CHUNK == 0:
            arrivals[z // CHUNK].wait()
        layer(z)


def total_kernel(parts, total, strip):
    result = parts[0]
    for i in range(1, parts.shape[0]):
        result = result + parts[i]
    total[...] = result
    strip[...] = result[: strip.shape[0]]


def merge_kernel(strip, share, order, copies):
    del order
    at_corner = lax.axis_index("gz") >= 4
    for t in range(5):
        cells = slice(8 * t, 8 * t + 8)
        if t == 0:
            merged = strip[cells]
        elif t == 4:
            merged = share[cells]
        else:
            merged = jnp.where(at_corner, share[cells], strip[cells])
        for k in range(copies.shape[0]):
            copies[k, cells, :] = merged


def sweep_kernel(
    shares, layer_face, areal_face, yweight, xweight, base, gain, new_state, correction,
    result, plane, sems,
):
    _, depth, height, width = areal_face.shape
    tiles = height // 8
    lane = lane_index((8, 128))

    def tile(k, t):
        return shares[k, 8 * t : 8 * t + 8, :]

    def side(right, right_at, left, left_at):
        right, left = turn(right, -right_at, 1), turn(left, width - 8 - left_at, 1)
        return jnp.where(lane < 8, right, jnp.where(lane >= width - 8, left, 0.0))

    planes = []
    for p in range(4):
        main = [tile(1, p)] + [tile(4 + p, 1 + t) for t in range(tiles - 1)] + [tile(p, 4), tile(0, p)]
        edge = [side(tile(7, 0), 8 * p, tile(5, 0), 8 * p)]
        for t in range(tiles):
            edge.append(side(tile(2, p), 8 * t, tile(3, p), 8 * t))
        edge.append(side(tile(4, 0), 8 * p, tile(6, 0), 8 * p))
        planes.append(
            jnp.concatenate([jnp.concatenate(main, axis=0), jnp.concatenate(edge, axis=0)], axis=1)
        )
    filled = planes[1] > 0.0
    scale = jnp.where(filled, RELAX / jnp.where(filled, planes[1], 1.0), 0.0)
    source = scale * planes[0]
    south = scale * planes[2]
    north = scale * turn(planes[2], 1, 0)
    east = scale * planes[3]
    west = scale * turn(planes[3], 1, 1)

    def around(field):
        return turn(field, -1, 0), turn(field, 1, 0), turn(field, -1, 1), turn(field, 1, 1)

    field = source
    for _ in range(SWEEPS - 1):
        s, n, e, w = around(field)
        field = ((1.0 - RELAX) * field + source) + (south * s + north * n) + (east * e + west * w)
    near = around(field)
    own = field[8 : 8 + height, 0:width]
    near = [n[8 : 8 + height, 0:width] for n in near]
    plane[...] = own
    copies = [pltpu.make_async_copy(plane, correction, sems.at[depth // CHUNK])]
    copies[0].start()

    for first in range(0, depth, CHUNK):
        for z in range(first, first + CHUNK):
            push = (layer_face[z] + layer_face[z + 1]) * own
            for weight, field in zip(areal_weights(z, areal_face, yweight, xweight), near):
                push = push + weight * field
            for r in range(3):
                result[r, z] = base[r, z] + gain[r, z] * push
        copy = pltpu.make_async_copy(
            result.at[:, pl.ds(first, CHUNK)], new_state.at[:, pl.ds(first, CHUNK)], sems.at[first // CHUNK]
        )
        copy.start()
        copies.append(copy)
    for copy in copies:
        copy.wait()


def call(kernel, out_shape, in_specs, out_specs, scratch=(), flops=0, moved=0, aliases=None):
    return pl.pallas_call(
        kernel,
        out_shape=out_shape,
        in_specs=in_specs,
        out_specs=out_specs,
        scratch_shapes=list(scratch),
        compiler_params=PARAMS,
        input_output_aliases=aliases or {},
        cost_estimate=pl.CostEstimate(flops=flops, bytes_accessed=moved, transcendentals=0) if flops else None,
    )


def per_device(state, right_side, permeability, pore_volume, facies, storage_table, coupling_table):
    _, depth, height, width = state.shape
    columns = lax.axis_size("gz")
    row_of, rows = lax.axis_size("gx"), lax.axis_size("gy")
    block = (depth, height, width)
    bf16 = jnp.bfloat16
    storage_table, coupling_table = storage_table.transpose(1, 0, 2), coupling_table.transpose(1, 0, 2)

    state_v, perm_v, coef, coef_lane, zface0, zface1, yface0, yface1, xpack = call(
        faces_kernel,
        [shape_of(3, *block), shape_of(*block), shape_of(18, depth, 128), shape_of(3, 2, 8, 128)]
        + [shape_of(4, height, width)] * 2 + [shape_of(4, depth, width)] * 2 + [shape_of(4, 2, 8, 128)],
        hbm(5),
        vmem(9),
        [
            pltpu.VMEM(block, bf16),
            pltpu.SMEM(facies.shape, jnp.int32),
            pltpu.SMEM(storage_table.shape, F32),
            pltpu.SMEM(coupling_table.shape, F32),
            pltpu.SemaphoreType.DMA((4 + depth // PIECE,)),
        ],
    )(*in_hbm(state, permeability, facies, storage_table, coupling_table))

    def exchange(face, axis, odd):
        pairs = []
        for i in range(odd, lax.axis_size(axis) - 1, 2):
            pairs += [(i, i + 1), (i + 1, i)]
        return lax.ppermute(face, axis, pairs)

    received = []
    for axis, first, second in (("gz", zface0, zface1), ("gy", yface0, yface1), ("gx", xpack, xpack)):
        received += [exchange(first, axis, 0), exchange(second, axis, 1)]

    layer_face, areal_face, acc, right_first, right_head, pore_v = call(
        inner_kernel,
        [
            shape_of(depth + 1, height, width),
            shape_of(2, *block),
            shape_of(6, height, width),
            shape_of(*block),
            shape_of(2, CHUNK, height, width),
            jax.ShapeDtypeStruct(block, bf16),
        ],
        vmem(3) + hbm(2),
        vmem(6),
        [pltpu.SemaphoreType.DMA((3,))],
        flops=6 * 10**8,
        moved=2 * 10**6,
    )(state_v, perm_v, coef, *in_hbm(right_side, pore_volume))

    layer_face, znear, ynear, xnear, yweight, xweight, message = call(
        outer_kernel,
        [
            shape_of(depth + 1, height, width),
            shape_of(2, 3, height, width),
            shape_of(2, 3, depth, width),
            shape_of(3, 2, 8, 128),
            shape_of(2, depth, width),
            shape_of(2, 8, 128),
            shape_of(columns, 40, 128),
        ],
        vmem(15),
        vmem(7),
        aliases={14: 0},
    )(coef, coef_lane, acc, zface0, zface1, yface0, yface1, xpack, *received, layer_face)

    parts = lax.all_to_all(message, "gz", 0, 0)
    share, strip = call(total_kernel, [shape_of(40, 128), shape_of(32, 128)], vmem(1), vmem(2))(parts)
    pairs = []
    for x in range(row_of):
        for y in range(rows):
            for k, (dy, dx) in enumerate(DIRECTIONS):
                if 0 <= x + dx < row_of and 0 <= y + dy < rows:
                    pairs.append(
                        ((x * rows + y) * columns + k, ((x + dx) * rows + y + dy) * columns + k)
                    )
    strip = lax.ppermute(strip, ("gx", "gy", "gz"), pairs)
    base, gain = call(
        cells_kernel,
        [shape_of(3, *block)] * 2,
        vmem(13) + hbm(1),
        vmem(2),
        [pltpu.VMEM((2, *block), F32), pltpu.SemaphoreType.DMA((depth // CHUNK,))],
        flops=4 * 10**9,
        moved=4 * 10**6,
    )(
        coef, znear, ynear, xnear, yweight, xweight, share, layer_face, areal_face, state_v,
        right_first, right_head, pore_v, *in_hbm(right_side),
    )
    copies = call(merge_kernel, shape_of(columns, 40, 128), vmem(3), vmem(1)[0])(strip, share, base)
    shares = lax.all_to_all(copies, "gz", 0, 0)

    new_state, correction = call(
        sweep_kernel,
        [pltpu.HBM((3, *block), F32), pltpu.HBM((height, width), F32)],
        vmem(7),
        hbm(2),
        [
            pltpu.VMEM((3, *block), F32),
            pltpu.VMEM((height, width), F32),
            pltpu.SemaphoreType.DMA((depth // CHUNK + 1,)),
        ],
    )(shares, layer_face, areal_face, yweight, xweight, base, gain)
    return (new_state, correction)


def solution(mesh):
    return jax.shard_map(
        per_device,
        mesh=mesh,
        in_specs=(
            P(None, "gz", "gy", "gx"),
            P(None, "gz", "gy", "gx"),
            P("gz", "gy", "gx"),
            P("gz", "gy", "gx"),
            P("gz"),
            P(),
            P(),
        ),
        out_specs=(P(None, "gz", "gy", "gx"), P("gy", "gx")),
        check_vma=False,
    )
```
